32 devices in a mesh: grp: 2 (over x), dp: 4 (over z), tp: 4 (over y, core).
Axes of the slice: x: 2, y: 2, z: 4, core: 2. Of those that a mesh axis runs over, the one named last changes fastest.
Arguments:
- tokens: bfloat16 [16384, 768], P(('grp', 'dp', 'tp')), may hold values from -6 to 6
- patch_side: int32 [8], P(('grp', 'dp')), may hold values from 8 to 48, as said below
- gain_attn: float32 [768], replicated, may hold values from 0.25 to 1.75
- w_qkv: bfloat16 [768, 2304], P(None, 'tp'), may hold values from -0.21875 to 0.21875
- w_out: bfloat16 [768, 768], P('tp'), may hold values from -0.875 to 0.875
- gain_mlp: float32 [768], replicated, may hold values from 0.25 to 1.75
- w_up: bfloat16 [768, 3072], P(None, 'tp'), may hold values from -0.21875 to 0.21875
- w_down: bfloat16 [3072, 768], P('tp'), may hold values from -0.109375 to 0.109375
- cotangent: bfloat16 [16384, 768], P(('grp', 'dp', 'tp')), may hold values from -6 to 6
Outputs:
- mixed_rows: bfloat16 [16384, 768], P(('grp', 'dp', 'tp'))
- input_grad: float32 [16384, 768], P(('grp', 'dp', 'tp'))
- grad_gain_attn: float32 [768], replicated
- grad_qkv: float32 [768, 2304], P('dp', 'tp')
- grad_out: float32 [768, 768], P('tp', 'dp')
- grad_gain_mlp: float32 [768], replicated
- grad_up: float32 [768, 3072], P('dp', 'tp')
- grad_down: float32 [3072, 768], P('tp', 'dp')
The draws below stay inside these ranges and needn't reach their ends.
Inputs may be any that keep to these rules, and one draw needn't show every extreme that they name: `patch_side`: every entry is one of 8, 10, 12, 16, 20, 24, 30, 40, 48; some group has 8 and some 48.
All inputs are finite; a program needn't handle non-finite values.
Results may differ from the reference program's by a relative error of at most 0.012.
The reference program's roundings to bfloat16 on the way count: a program that leaves them out, or rounds other values in their place, can miss the bound.
Values may be sent and summed in bfloat16 or wider, within the bound.
No kernel may reach another device: no remote copies, remote signals or barrier semaphores. Data moves between devices by JAX's collectives and lax.ppermute only.
A program may use at most 128 MiB of HBM per device.

```python
import jax
import jax.numpy as jnp
from jax import lax

D = 768
HEADS = 12
HD = 64
FF = 3072
IMAGE = 240
TOK_GRP = 2048
GROUPS = 8
TOKENS = 16384


def draw_patch_side(key, part):
    key = jax.random.fold_in(key, 7)
    first_key, second_key = jax.random.split(key)
    choices_table = jnp.array([8, 10, 12, 16, 20, 24, 30, 40, 48], jnp.int32)
    picks = jax.random.randint(first_key, (GROUPS,), 0, 9)
    placing = jax.random.permutation(second_key, GROUPS)
    picks = jnp.where(placing == 0, 0, jnp.where(placing == 1, 8, picks))
    return choices_table[picks]


def spiked(values, own_key, source, target, blocks, factor):
    def block_of(position):
        return (jnp.arange(values.shape[position]) // (values.shape[position] // blocks)).reshape((-1,) + (1,) * (values.ndim - 1 - position))

    first = jax.random.permutation(own_key, blocks)[block_of(target)]
    far = (block_of(target) + blocks // 2) % blocks
    return jnp.where((block_of(source) == first) | (block_of(source) == far), factor * values, values)


def block_scale(own_key, dims, pieces, low, high):
    gain = 1.0
    for position, blocks in pieces:
        heights = jax.random.uniform(jax.random.fold_in(jax.random.fold_in(own_key, 6), position), (blocks,), jnp.float32, low / len(pieces), high / len(pieces))
        gain = gain * jnp.repeat(jnp.exp(heights), dims[position] // blocks).reshape((-1,) + (1,) * (len(dims) - 1 - position))
    return gain


def noise(own_key, extent, width, reach, shards=(), kind=jnp.bfloat16):
    values = jax.random.normal(own_key, extent, jnp.float32) * width
    if len(shards) > 0:
        values = block_scale(own_key, extent, shards, -0.22, 0.18) * values
    return jnp.clip(values, min=-reach, max=reach).astype(kind)


def heavy_noise(rng, shape, scale, most, pieces, heavy, held_as=jnp.bfloat16):
    result = scale * jax.random.normal(rng, shape, jnp.float32)
    if pieces:
        result = result * block_scale(rng, shape, pieces, -0.22, 0.18)
    return jnp.clip(spiked(result, jax.random.fold_in(rng, 3), *heavy), -most, most).astype(held_as)


def setup_inputs(seed: int = 0) -> dict:
    key_list = jax.random.split(jax.random.key(seed), 10)
    tokens = noise(key_list[0], (TOKENS, D), 1.0, 6.0, ((0, 32),))
    patch_side = draw_patch_side(jax.random.fold_in(key_list[9], 71), 0)
    gain_attn = jnp.clip(1.0 + 0.15 * jax.random.normal(key_list[2], (D,), jnp.float32), 0.25, 1.75)
    w_qkv = noise(key_list[3], (D, 3 * D), D ** -0.5, 0.21875, ((1, 4),))
    w_out = noise(key_list[4], (D, D), (D // 16) ** -0.5, 0.875, ((0, 4),))
    gain_mlp = jnp.clip(1.0 + 0.15 * jax.random.normal(key_list[5], (D,), jnp.float32), 0.25, 1.75)
    w_up = noise(key_list[6], (D, FF), D ** -0.5, 0.21875, ((1, 4),))
    w_down = noise(key_list[7], (FF, D), FF ** -0.5, 0.109375, ((0, 4),))
    cotangent = heavy_noise(key_list[8], (TOKENS, D), 1.0, 6.0, ((0, 32),), (0, 1, 32, 2.75))
    return dict(tokens=tokens, patch_side=patch_side, gain_attn=gain_attn, w_qkv=w_qkv, w_out=w_out, gain_mlp=gain_mlp, w_up=w_up, w_down=w_down, cotangent=cotangent)


@jax.custom_vjp
def low(v):
    return lax.optimization_barrier(v.astype(jnp.bfloat16)).astype(jnp.float32)

@jax.custom_vjp
def low_back(v):
    return v

def low_keep(v):
    return (low(v), None)

def low_pass(kept, grad):
    return (grad,)

def back_keep(v):
    return (v, None)

def back_low(kept, grad):
    return (low(grad),)
low.defvjp(low_keep, low_pass)
low_back.defvjp(back_keep, back_low)
epsilon = 1e-06
highest = lax.Precision.HIGHEST

def segments(patch_size, length):
    cell_count = (IMAGE // patch_size) ** 2
    positions = jnp.arange(length, dtype=jnp.int32)
    return jnp.minimum(positions // cell_count, length // cell_count).astype(jnp.int32)

def normalize(values, scaling):
    centred = values - lax.optimization_barrier(jnp.mean(values, axis=1, keepdims=True))
    spread = lax.optimization_barrier(jnp.mean(centred * centred, axis=1, keepdims=True))
    return centred * lax.rsqrt(spread + epsilon) * scaling

def matmul(left, right):
    return jnp.dot(left, right, precision=highest)

def attention(queries, key_rows, values, image_id):
    length = queries.shape[0]
    block_rows = min(512, length)

    def block_out(number):
        first_row = number * block_rows
        q_rows = lax.dynamic_slice_in_dim(queries, first_row, block_rows, 0)
        query_ids = lax.dynamic_slice_in_dim(image_id, first_row, block_rows, 0)
        scores = jnp.einsum('qhd,khd->hqk', q_rows, key_rows, precision=highest) * 0.125
        scores = low_back(scores)
        scores = jnp.where(query_ids[None, :, None] == image_id[None, None, :], scores, -1e+30)
        attn_probs = low(jax.nn.softmax(scores, axis=2))
        return jnp.einsum('hqk,khd->qhd', attn_probs, values, precision=highest)
    blocks = lax.map(jax.checkpoint(block_out), jnp.arange(length // block_rows, dtype=jnp.int32))
    return blocks.reshape(length, -1)

def group_layer(activations, patch_size, weights):
    gain_attn, w_qkv, w_out, gain_mlp, w_up, w_down = weights
    length = activations.shape[0]
    image_id = segments(patch_size, length)
    attn_in = low(normalize(activations, gain_attn))
    qkv = low_back(low(matmul(attn_in, w_qkv))).reshape(length, HEADS, 3, HD)
    heads_out = attention(qkv[:, :, 0], qkv[:, :, 1], qkv[:, :, 2], image_id)
    heads_out = low_back(low(heads_out))
    resid = activations + low_back(matmul(heads_out, w_out))
    mlp_in = low(normalize(resid, gain_mlp))
    pre_act = low_back(matmul(mlp_in, w_up))
    act = low(jax.nn.gelu(pre_act, approximate=False))
    return resid + matmul(act, w_down)

def reference(tokens, patch_side, gain_attn, w_qkv, w_out, gain_mlp, w_up, w_down, cotangent):
    groups = patch_side.shape[0]
    activations = tokens.astype(jnp.float32).reshape(groups, TOK_GRP, D)
    grads_in = cotangent.astype(jnp.float32).reshape(groups, TOK_GRP, D)
    weights = (gain_attn, w_qkv.astype(jnp.float32), w_out.astype(jnp.float32), gain_mlp, w_up.astype(jnp.float32), w_down.astype(jnp.float32))

    def forward(inputs, params):

        def per_group(group_pair):
            return group_layer(group_pair[0], group_pair[1], params)
        return lax.map(jax.checkpoint(per_group), (inputs, patch_side))
    outputs, pullback = jax.vjp(forward, activations, weights)
    input_grad, weight_grads = pullback(grads_in)
    return (outputs.astype(jnp.bfloat16).reshape(TOKENS, D), input_grad.reshape(TOKENS, D), weight_grads[0], weight_grads[1], weight_grads[2], weight_grads[3], weight_grads[4], weight_grads[5])
```

```python
from functools import partial

import jax
import jax.numpy as jnp
from jax import lax
from jax.experimental import pallas as pl
from jax.experimental.pallas import tpu as pltpu
from jax.sharding import PartitionSpec as P

HD = 64
LANES = 128
IMAGE = 240
EXCLUDED = -1e30
MIB = 1024 * 1024
NT = (((1,), (1,)), ((), ()))
TN = (((0,), (0,)), ((), ()))

epsilon = 1e-06


def normalize(values, scaling):
    centred = values - jnp.mean(values, axis=1, keepdims=True)
    inverse = lax.rsqrt(jnp.mean(centred * centred, axis=1, keepdims=True) + epsilon)
    normed = centred * inverse
    return (normed * scaling, normed, inverse)


def restore(d_normed, normed, inverse, scaling):
    d_scaled = d_normed * scaling
    return inverse * (
        d_scaled
        - jnp.mean(d_scaled, axis=1, keepdims=True)
        - normed * jnp.mean(d_scaled * normed, axis=1, keepdims=True)
    )


def swap(value, distance, axis="tp"):
    size = lax.axis_size(axis)
    return lax.ppermute(value, axis, [(i, i ^ distance) for i in range(size)])


def add(left, right):
    return left.astype(jnp.float32) + right.astype(jnp.float32)


def gather_blocks(own):
    across = swap(own, 2)
    return [own, swap(own, 1), across, swap(across, 1)]


def scatter_blocks(parts):
    here = add(parts[0], swap(parts[1], 1))
    there = add(parts[2], swap(parts[3], 1)).astype(jnp.bfloat16)
    return here + swap(there, 2).astype(jnp.float32)


def attend_kernel(
    heads, bounds_ref, q_ref, k_ref, v_ref, id_q_ref, id_k_ref, out_ref, log_ref, turned, ids
):
    block = pl.program_id(0)
    width = q_ref.shape[0]

    @pl.when(block == 0)
    def _():
        for h in range(heads):
            value = v_ref[:, h * LANES : (h + 1) * LANES].astype(jnp.float32).T
            turned[h, :HD] = value[:HD].astype(jnp.bfloat16)
            turned[h, HD:] = jnp.ones((turned.shape[1] - HD, v_ref.shape[0]), jnp.bfloat16)
        ids[...] = jnp.broadcast_to(id_k_ref[...], ids.shape)

    id_q = id_q_ref[...]
    queries = [q_ref[:, h * LANES : (h + 1) * LANES] for h in range(heads)]

    def step(number, carry):
        at = pl.ds(pl.multiple_of((number ^ bounds_ref[0]) * width, width), width)
        mask = jnp.concatenate([ids[at, :]] * (width // LANES), axis=1) == id_q
        result = []
        for h in range(heads):
            largest, total = carry[h]
            scores = lax.dot_general(
                k_ref[at, h * LANES : (h + 1) * LANES],
                queries[h],
                NT,
                preferred_element_type=jnp.float32,
            )
            scores = jnp.where(mask, scores, EXCLUDED)
            top = jnp.maximum(largest, jnp.max(scores, axis=0, keepdims=True))
            exponent = jnp.exp(scores - top).astype(jnp.bfloat16)
            total = total * jnp.exp(largest - top) + jnp.dot(
                turned[h, :, at], exponent, preferred_element_type=jnp.float32
            )
            result.append((top, total))
        return tuple(result)

    start = tuple(
        (
            jnp.full((1, width), EXCLUDED, jnp.float32),
            jnp.zeros((turned.shape[1], width), jnp.float32),
        )
        for _ in range(heads)
    )
    result = lax.fori_loop(bounds_ref[1 + 2 * block], bounds_ref[2 + 2 * block], step, start)
    for h in range(heads):
        largest, total = result[h]
        denominator = total[HD : HD + 1]
        out_ref[:, h * HD : (h + 1) * HD] = (total[:HD] / denominator).T.astype(jnp.bfloat16)
        log_ref[h : h + 1, :] = largest + jnp.log(denominator)


def attend(qkv, image_id, bounds, heads):
    rows = qkv.shape[0]
    wide = heads * LANES
    width = rows // 4
    return pl.pallas_call(
        partial(attend_kernel, heads),
        grid_spec=pltpu.PrefetchScalarGridSpec(
            num_scalar_prefetch=1,
            grid=(4,),
            in_specs=[
                pl.BlockSpec((width, wide), lambda i, _: (i, 0)),
                pl.BlockSpec((rows, wide), lambda i, _: (0, 1)),
                pl.BlockSpec((rows, wide), lambda i, _: (0, 2)),
                pl.BlockSpec((1, width), lambda i, _: (0, i)),
                pl.BlockSpec((rows, 1), lambda i, _: (0, 0)),
            ],
            out_specs=[
                pl.BlockSpec((width, heads * HD), lambda i, _: (i, 0)),
                pl.BlockSpec((heads, width), lambda i, _: (0, i)),
            ],
            scratch_shapes=[
                pltpu.VMEM((heads, HD + 16, rows), jnp.bfloat16),
                pltpu.VMEM((rows, LANES), jnp.int32),
            ],
        ),
        out_shape=[
            jax.ShapeDtypeStruct((rows, heads * HD), jnp.bfloat16),
            jax.ShapeDtypeStruct((heads, rows), jnp.float32),
        ],
        compiler_params=pltpu.CompilerParams(vmem_limit_bytes=48 * MIB),
        cost_estimate=pl.CostEstimate(
            flops=heads * rows * rows * HD * 6, bytes_accessed=6 * MIB, transcendentals=0
        ),
        name="attend",
    )(bounds, qkv, qkv, qkv, image_id[None, :], image_id[:, None])


def attend_back_kernel(
    heads,
    bounds_ref,
    q_ref,
    k_ref,
    v_ref,
    grad_ref,
    out_ref,
    log_ref,
    id_q_ref,
    id_k_ref,
    d_ref,
    turned,
    ids,
    d_keys,
    d_values,
):
    block = pl.program_id(0)
    width = q_ref.shape[0]

    @pl.when(block == 0)
    def _():
        for h in range(heads):
            key = k_ref[:, h * LANES : (h + 1) * LANES].astype(jnp.float32).T
            turned[h] = key[:HD].astype(jnp.bfloat16)
        ids[...] = jnp.broadcast_to(id_k_ref[...], ids.shape)
        d_keys[...] = jnp.zeros_like(d_keys)
        d_values[...] = jnp.zeros_like(d_values)

    id_q = id_q_ref[...]
    ones = jnp.ones((8, HD), jnp.float32)
    queries = [q_ref[:, h * LANES : (h + 1) * LANES] for h in range(heads)]
    grads = [grad_ref[:, h * HD : (h + 1) * HD] for h in range(heads)]
    logs = [log_ref[h : h + 1, :] for h in range(heads)]
    inner = []
    for h in range(heads):
        product = grads[h].astype(jnp.float32) * out_ref[:, h * HD : (h + 1) * HD].astype(
            jnp.float32
        )
        inner.append(
            lax.dot_general(
                ones,
                product,
                NT,
                precision=lax.Precision.HIGHEST,
                preferred_element_type=jnp.float32,
            )[:1]
        )

    def step(number, carry):
        at = pl.ds(pl.multiple_of((number ^ bounds_ref[0]) * width, width), width)
        mask = jnp.concatenate([ids[at, :]] * (width // LANES), axis=1) == id_q
        result = []
        for h in range(heads):
            scores = lax.dot_general(
                k_ref[at, h * LANES : (h + 1) * LANES],
                queries[h],
                NT,
                preferred_element_type=jnp.float32,
            )
            probs = jnp.where(mask, jnp.exp(scores - logs[h]), 0.0)
            d_probs = lax.dot_general(
                v_ref[at, h * LANES : h * LANES + HD],
                grads[h],
                NT,
                preferred_element_type=jnp.float32,
            )
            d_scores = (probs * (d_probs - inner[h])).astype(jnp.bfloat16)
            d_values[h, at, :] += jnp.dot(
                probs.astype(jnp.bfloat16), grads[h], preferred_element_type=jnp.float32
            )
            d_keys[h, at, :] += jnp.dot(d_scores, queries[h], preferred_element_type=jnp.float32)[
                :, :HD
            ]
            result.append(
                carry[h]
                + jnp.dot(turned[h, :, at], d_scores, preferred_element_type=jnp.float32)
            )
        return tuple(result)

    start = tuple(jnp.zeros((HD, width), jnp.float32) for _ in range(heads))
    result = lax.fori_loop(bounds_ref[1 + 2 * block], bounds_ref[2 + 2 * block], step, start)
    here = pl.ds(pl.multiple_of(block * width, width), width)
    for h in range(heads):
        d_ref[here, 3 * h * HD : (3 * h + 1) * HD] = (result[h] * 0.125).T.astype(jnp.bfloat16)

    @pl.when(block == pl.num_programs(0) - 1)
    def _():
        for h in range(heads):
            d_ref[:, (3 * h + 1) * HD : (3 * h + 2) * HD] = d_keys[h].astype(jnp.bfloat16)
            d_ref[:, (3 * h + 2) * HD : (3 * h + 3) * HD] = d_values[h].astype(jnp.bfloat16)


def attend_back(qkv, d_heads, heads_out, log_total, image_id, bounds, heads):
    rows = qkv.shape[0]
    wide = heads * LANES
    width = rows // 4
    return pl.pallas_call(
        partial(attend_back_kernel, heads),
        grid_spec=pltpu.PrefetchScalarGridSpec(
            num_scalar_prefetch=1,
            grid=(4,),
            in_specs=[
                pl.BlockSpec((width, wide), lambda i, _: (i, 0)),
                pl.BlockSpec((rows, wide), lambda i, _: (0, 1)),
                pl.BlockSpec((rows, wide), lambda i, _: (0, 2)),
                pl.BlockSpec((width, heads * HD), lambda i, _: (i, 0)),
                pl.BlockSpec((width, heads * HD), lambda i, _: (i, 0)),
                pl.BlockSpec((heads, width), lambda i, _: (0, i)),
                pl.BlockSpec((1, width), lambda i, _: (0, i)),
                pl.BlockSpec((rows, 1), lambda i, _: (0, 0)),
            ],
            out_specs=pl.BlockSpec((rows, 3 * heads * HD), lambda i, _: (0, 0)),
            scratch_shapes=[
                pltpu.VMEM((heads, HD, rows), jnp.bfloat16),
                pltpu.VMEM((rows, LANES), jnp.int32),
                pltpu.VMEM((heads, rows, HD), jnp.float32),
                pltpu.VMEM((heads, rows, HD), jnp.float32),
            ],
        ),
        out_shape=jax.ShapeDtypeStruct((rows, 3 * heads * HD), jnp.bfloat16),
        compiler_params=pltpu.CompilerParams(vmem_limit_bytes=48 * MIB),
        cost_estimate=pl.CostEstimate(
            flops=heads * rows * rows * HD * 10, bytes_accessed=10 * MIB, transcendentals=0
        ),
        name="attend_back",
    )(bounds, qkv, qkv, qkv, d_heads, heads_out, log_total, image_id[None, :], image_id[:, None])


def mlp_kernel(
    steps,
    first,
    x_a_ref,
    x_b_ref,
    g_a_ref,
    g_b_ref,
    up_ref,
    down_ref,
    *refs,
):
    if first:
        y_a_ref, y_b_ref, m_a_ref, m_b_ref, d_up_ref, d_down_ref = refs
    else:
        old_up_ref, old_down_ref, y_a_ref, y_b_ref, m_a_ref, m_b_ref, d_up_ref, d_down_ref = refs
    number = pl.program_id(0)

    @pl.when(number == 0)
    def _():
        if first:
            d_up_ref[...] = jnp.zeros_like(d_up_ref)
            d_down_ref[...] = jnp.zeros_like(d_down_ref)
        else:
            d_up_ref[...] = old_up_ref[...]
            d_down_ref[...] = old_down_ref[...]

    def rows(x_ref, g_ref, y_ref, m_ref):
        mlp_in = x_ref[...]
        out_grads = g_ref[...]
        pre_act = jnp.dot(mlp_in, up_ref[...], preferred_element_type=jnp.float32)
        d_act = lax.dot_general(
            out_grads, down_ref[...], NT, preferred_element_type=jnp.float32
        )
        below = 0.5 + 0.5 * lax.erf(pre_act * 0.7071067811865476)
        density = 0.3989422804014327 * jnp.exp(-0.5 * pre_act * pre_act)
        act = (pre_act * below).astype(jnp.bfloat16)
        d_pre = (d_act * (below + pre_act * density)).astype(jnp.bfloat16)
        y_ref[...] = jnp.dot(act, down_ref[...], preferred_element_type=jnp.float32).astype(
            jnp.bfloat16
        )
        m_ref[...] = lax.dot_general(
            d_pre, up_ref[...], NT, preferred_element_type=jnp.float32
        ).astype(jnp.bfloat16)
        d_up_ref[...] += lax.dot_general(mlp_in, d_pre, TN, preferred_element_type=jnp.float32)
        d_down_ref[...] += lax.dot_general(out_grads, act, TN, preferred_element_type=jnp.float32)

    @pl.when(number < steps)
    def _():
        rows(x_a_ref, g_a_ref, y_a_ref, m_a_ref)

    @pl.when(number >= steps)
    def _():
        rows(x_b_ref, g_b_ref, y_b_ref, m_b_ref)


def mlp(x_a, x_b, g_a, g_b, skip, w_up, w_down, sums):
    length, model = x_a.shape
    hidden = w_up.shape[1]
    tile = min(256, length)
    steps = length // tile
    first = sums is None

    def in_a(i):
        return (jnp.minimum(i, steps - 1), 0)

    def in_b(i):
        return (jnp.maximum(i - steps, 0), 0)

    def grads_a(i):
        return (jnp.minimum(i, steps - 1) + skip // tile, 0)

    def grads_b(i):
        return (jnp.maximum(i - steps, 0) + skip // tile, 0)

    def whole(shape):
        return pl.BlockSpec(shape, lambda i: (0, 0))

    rows = jax.ShapeDtypeStruct((length, model), jnp.bfloat16)
    totals = [
        jax.ShapeDtypeStruct((model, hidden), jnp.float32),
        jax.ShapeDtypeStruct((model, hidden), jnp.float32),
    ]
    total_specs = [whole((model, hidden)), whole((model, hidden))]
    return pl.pallas_call(
        partial(mlp_kernel, steps, first),
        grid=(2 * steps,),
        in_specs=[
            pl.BlockSpec((tile, model), in_a),
            pl.BlockSpec((tile, model), in_b),
            pl.BlockSpec((tile, model), grads_a),
            pl.BlockSpec((tile, model), grads_b),
            whole((model, hidden)),
            whole((hidden, model)),
        ]
        + ([] if first else total_specs),
        out_specs=[
            pl.BlockSpec((tile, model), in_a),
            pl.BlockSpec((tile, model), in_b),
            pl.BlockSpec((tile, model), in_a),
            pl.BlockSpec((tile, model), in_b),
        ]
        + total_specs,
        out_shape=[rows, rows, rows, rows] + totals,
        input_output_aliases={} if first else {6: 4, 7: 5},
        compiler_params=pltpu.CompilerParams(vmem_limit_bytes=56 * MIB),
        cost_estimate=pl.CostEstimate(
            flops=2 * length * model * hidden * 12, bytes_accessed=16 * MIB, transcendentals=0
        ),
        name="mlp",
    )(x_a, x_b, g_a, g_b, w_up, w_down, *([] if first else sums))


def reduce_rows(arrays):
    count = lax.axis_size("dp")
    index = lax.axis_index("dp")
    widths = [a.shape[1] for a in arrays]
    kept = [a.reshape(count, a.shape[0] // count, a.shape[1]) for a in arrays]
    distance = 1
    while distance < count:
        bit = (index // distance) % 2
        pairs = [k.reshape(-1, 2, *k.shape[1:]) for k in kept]
        sent = jnp.concatenate(
            [
                lax.dynamic_index_in_dim(p, 1 - bit, 1, keepdims=False).astype(jnp.bfloat16)
                for p in pairs
            ],
            axis=2,
        )
        got = swap(sent, distance, "dp")
        first = 0
        summed = []
        for p, w in zip(pairs, widths):
            mine = lax.dynamic_index_in_dim(p, bit, 1, keepdims=False)
            summed.append(add(mine, got[:, :, first : first + w]))
            first += w
        kept = summed
        distance *= 2
    mine = jnp.concatenate([k[0].astype(jnp.bfloat16) for k in kept], axis=1)
    size = lax.axis_size("grp")
    total = mine
    for shift in range(1, size):
        total = add(total, lax.ppermute(mine, "grp", [(i, i ^ shift) for i in range(size)]))
    first = 0
    result = []
    for w in widths:
        result.append(total[:, first : first + w])
        first += w
    return result


def on_device(tokens, patch_side, gain_attn, w_qkv, w_out, gain_mlp, w_up, w_down, cotangent):
    rows, model = tokens.shape
    place = lax.axis_index("tp")
    group_rows = 4 * rows
    half = rows // 2
    heads = w_out.shape[0] // HD

    activations = tokens.astype(jnp.float32)
    normed_attn, unit_attn, inverse_attn = normalize(activations, gain_attn)
    attn_in = jnp.concatenate(gather_blocks(normed_attn.astype(jnp.bfloat16)), axis=0)

    cells = (IMAGE // patch_side[0]) ** 2
    full = group_rows // cells
    order = place ^ jnp.arange(4, dtype=jnp.int32)
    positions = (order[:, None] * rows + jnp.arange(rows, dtype=jnp.int32)).reshape(-1)
    image_id = jnp.minimum(positions // cells, full)
    first_id = jnp.minimum(order * rows // cells, full)
    last_id = jnp.minimum((order * rows + rows - 1) // cells, full)
    low = first_id * cells // rows
    stop = jnp.where(last_id == full, group_rows, (last_id + 1) * cells)
    high = (stop + rows - 1) // rows
    bounds = jnp.concatenate([place[None], jnp.stack([low, high], axis=1).reshape(-1)])

    by_head = w_qkv.reshape(model, heads, 3, HD)
    by_head = by_head * jnp.array([0.125, 1.0, 1.0], jnp.bfloat16)[:, None]
    spread = jnp.pad(by_head.transpose(0, 2, 1, 3), ((0, 0), (0, 0), (0, 0), (0, LANES - HD)))
    spread = spread.reshape(model, 3 * heads * LANES)
    qkv = jnp.dot(attn_in, spread, preferred_element_type=jnp.float32).astype(jnp.bfloat16)

    heads_out, log_total = attend(qkv, image_id, bounds, heads)

    w_outs = gather_blocks(w_out)
    pieces = [heads_out[j * rows : (j + 1) * rows] for j in range(4)]
    mine = [pieces[0]] + [swap(pieces[j], j) for j in range(1, 4)]
    branch = jnp.dot(mine[0], w_outs[0], preferred_element_type=jnp.float32)
    for j in range(1, 4):
        branch = branch + jnp.dot(mine[j], w_outs[j], preferred_element_type=jnp.float32)
    resid = activations + branch

    normed_mlp, unit_mlp, inverse_mlp = normalize(resid, gain_mlp)
    mlp_in = normed_mlp.astype(jnp.bfloat16)
    out_grads = gather_blocks(cotangent)
    near = swap(mlp_in, 1)
    across = [swap(mlp_in[:half], 2), swap(mlp_in[half:], 2)]
    diagonal = [swap(a, 1) for a in across]

    y_0, y_1, m_0, m_1, *sums = mlp(
        mlp_in, near, out_grads[0], out_grads[1], 0, w_up, w_down, None
    )
    far_y = []
    far_m = []
    for k in range(2):
        y_2, y_3, m_2, m_3, *sums = mlp(
            across[k], diagonal[k], out_grads[2], out_grads[3], k * half, w_up, w_down, sums
        )
        far_m.append(swap(add(m_2, swap(m_3, 1)).astype(jnp.bfloat16), 2))
        far_y.append((y_2, y_3))
    d_up, d_down = sums
    d_mlp_in = add(add(m_0, swap(m_1, 1)), jnp.concatenate(far_m, axis=0))
    d_resid = cotangent.astype(jnp.float32) + restore(d_mlp_in, unit_mlp, inverse_mlp, gain_mlp)

    d_branch = d_resid.astype(jnp.bfloat16)
    d_pieces = [
        lax.dot_general(d_branch, w, NT, preferred_element_type=jnp.float32).astype(jnp.bfloat16)
        for w in w_outs
    ]
    d_heads = [d_pieces[0]] + [swap(d_pieces[j], j) for j in range(1, 4)]
    d_heads = jnp.concatenate(d_heads, axis=0)

    mixed = scatter_blocks(
        [
            y_0,
            y_1,
            jnp.concatenate([far_y[0][0], far_y[1][0]], axis=0),
            jnp.concatenate([far_y[0][1], far_y[1][1]], axis=0),
        ]
    )
    mixed_rows = (resid + mixed).astype(jnp.bfloat16)

    d_out = scatter_blocks(
        [
            lax.dot_general(d_branch, h, TN, preferred_element_type=jnp.float32).astype(
                jnp.bfloat16
            )
            for h in mine
        ]
    )
    grad_up, grad_down, grad_out = reduce_rows([d_up, d_down, d_out])

    d_qkv = attend_back(qkv, d_heads, heads_out, log_total, image_id, bounds, heads)
    d_w_qkv = lax.dot_general(attn_in, d_qkv, TN, preferred_element_type=jnp.float32)
    (grad_qkv,) = reduce_rows([d_w_qkv])
    d_attn_in = scatter_blocks(
        [
            lax.dot_general(
                d_qkv[j * rows : (j + 1) * rows], w_qkv, NT, preferred_element_type=jnp.float32
            ).astype(jnp.bfloat16)
            for j in range(4)
        ]
    )
    input_grad = d_resid + restore(d_attn_in, unit_attn, inverse_attn, gain_attn)

    gain_parts = jnp.stack(
        [
            jnp.sum(d_w_qkv * w_qkv.astype(jnp.float32), axis=1) / gain_attn,
            jnp.sum(d_up * w_up.astype(jnp.float32), axis=1) / gain_mlp,
        ]
    )
    grad_gains = lax.psum(gain_parts, ("grp", "dp", "tp"))
    return (
        mixed_rows,
        input_grad,
        grad_gains[0],
        grad_qkv,
        grad_out.T,
        grad_gains[1],
        grad_up,
        grad_down.T,
    )


def solution(mesh):
    in_specs = (
        P(("grp", "dp", "tp"), None),
        P(("grp", "dp")),
        P(),
        P(None, "tp"),
        P("tp", None),
        P(),
        P(None, "tp"),
        P("tp", None),
        P(("grp", "dp", "tp"), None),
    )
    out_specs = (
        P(("grp", "dp", "tp"), None),
        P(("grp", "dp", "tp"), None),
        P(),
        P("dp", "tp"),
        P("tp", "dp"),
        P(),
        P("dp", "tp"),
        P("tp", "dp"),
    )
    return jax.shard_map(
        on_device, mesh=mesh, in_specs=in_specs, out_specs=out_specs, check_vma=False
    )
```

```python
from functools import partial

import jax
import jax.numpy as jnp
from jax import lax
from jax.experimental import pallas as pl
from jax.experimental.pallas import tpu as pltpu
from jax.sharding import PartitionSpec as P

HD = 64
LANES = 128
IMAGE = 240
EXCLUDED = -1e30
MIB = 1024 * 1024
NT = (((1,), (1,)), ((), ()))
TN = (((0,), (0,)), ((), ()))

epsilon = 1e-06


def normalize(values, scaling):
    centred = values - jnp.mean(values, axis=1, keepdims=True)
    inverse = lax.rsqrt(jnp.mean(centred * centred, axis=1, keepdims=True) + epsilon)
    normed = centred * inverse
    return (normed * scaling, normed, inverse)


def restore(d_normed, normed, inverse, scaling):
    d_scaled = d_normed * scaling
    return inverse * (
        d_scaled
        - jnp.mean(d_scaled, axis=1, keepdims=True)
        - normed * jnp.mean(d_scaled * normed, axis=1, keepdims=True)
    )


def swap(value, distance, axis="tp"):
    size = lax.axis_size(axis)
    return lax.ppermute(value, axis, [(i, i ^ distance) for i in range(size)])


def after(value, *earlier):
    return lax.optimization_barrier((value, *earlier))[0]


def join(*values):
    return lax.optimization_barrier(values)


def add(left, right):
    return left.astype(jnp.float32) + right.astype(jnp.float32)


def product(left, right, dims=(((1,), (0,)), ((), ()))):
    return lax.dot_general(left, right, dims, preferred_element_type=jnp.float32)


def low(value):
    return value.astype(jnp.bfloat16)


def settings(microseconds, limit=40):
    return dict(
        compiler_params=pltpu.CompilerParams(vmem_limit_bytes=limit * MIB),
        cost_estimate=pl.CostEstimate(
            flops=int(microseconds * 1.1e9), bytes_accessed=MIB, transcendentals=0
        ),
    )


def whole(array):
    return pl.BlockSpec(array.shape, lambda *_: (0,) * len(array.shape))


def shape(*dims, dtype=jnp.bfloat16):
    return jax.ShapeDtypeStruct(dims, dtype)


def far_shape(*dims, dtype=jnp.bfloat16):
    return pltpu.HBM(dims, dtype)


def left(array):
    return pltpu.with_memory_space_constraint(array, pltpu.HBM)


def norm_kernel(x_ref, gain_ref, out_ref):
    out_ref[...] = low(normalize(x_ref[...].astype(jnp.float32), gain_ref[...])[0])


def norm(tokens, gain):
    rows, model = tokens.shape
    tile = pl.BlockSpec((rows // 2, model), lambda i: (i, 0))
    return pl.pallas_call(
        norm_kernel,
        grid=(2,),
        in_specs=[tile, whole(gain)],
        out_specs=tile,
        out_shape=far_shape(rows, model),
        name="norm",
        **settings(2),
    )(left(tokens), gain)


def norm_back_kernel(x_ref, gain_ref, own_ref, pair_ref, far_0_ref, far_1_ref, d_ref, out_ref):
    far = jnp.where(pl.program_id(0) < 2, far_0_ref[...], far_1_ref[...])
    d_normed = add(own_ref[...], pair_ref[...]) + far.astype(jnp.float32)
    _, unit, inverse = normalize(x_ref[...].astype(jnp.float32), gain_ref[...])
    out_ref[...] = d_ref[...] + restore(d_normed, unit, inverse, gain_ref[...])


def norm_back(tokens, gain, own, pair, far, d_resid):
    rows, model = tokens.shape
    tile = pl.BlockSpec((rows // 4, model), lambda i: (i, 0))
    tile_0 = pl.BlockSpec((rows // 4, model), lambda i: (jnp.minimum(i, 1), 0))
    tile_1 = pl.BlockSpec((rows // 4, model), lambda i: (jnp.maximum(i - 2, 0), 0))
    return pl.pallas_call(
        norm_back_kernel,
        grid=(4,),
        in_specs=[tile, whole(gain), tile, tile, tile_0, tile_1, tile],
        out_specs=tile,
        out_shape=shape(rows, model, dtype=jnp.float32),
        name="norm_back",
        **settings(2),
    )(tokens, gain, own, pair, *far, d_resid)


def project_kernel(count, *refs):
    out_ref = refs[-1]
    for number in range(count):

        @pl.when(pl.program_id(0) == number)
        def _():
            out_ref[...] = low(product(refs[number][...], refs[count][...], NT))


def project(blocks, weights, base, earlier):
    rows = blocks[0].shape[0]
    wide = weights.shape[0]
    count = len(blocks)
    extra = [] if earlier is None else [earlier]
    return pl.pallas_call(
        partial(project_kernel, count),
        grid=(count,),
        in_specs=[whole(x) for x in blocks]
        + [whole(weights)]
        + [pl.BlockSpec(memory_space=pl.ANY)] * len(extra),
        out_specs=pl.BlockSpec((rows, wide), lambda i: (base + i, 0)),
        out_shape=far_shape(4 * rows, wide),
        input_output_aliases={count + 1: 0} if extra else {},
        name="project",
        **settings(2 * count),
    )(*blocks, weights, *extra)


def attend_kernel(
    heads, base, bounds_ref, q_ref, k_ref, v_ref, id_q_ref, id_k_ref, *refs
):
    out_refs = refs[:2]
    log_ref, turned, ids = refs[2:]
    block = pl.program_id(0)
    width = q_ref.shape[0]

    @pl.when(block == 0)
    def _():
        for h in range(heads):
            value = v_ref[:, h * LANES : (h + 1) * LANES].astype(jnp.float32).T
            turned[h, :HD] = low(value[:HD])
            turned[h, HD:] = jnp.ones((turned.shape[1] - HD, v_ref.shape[0]), jnp.bfloat16)
        ids[...] = jnp.broadcast_to(id_k_ref[...], ids.shape)

    id_q = id_q_ref[...]
    queries = [q_ref[:, h * LANES : (h + 1) * LANES] for h in range(heads)]

    def step(number, carry):
        at = pl.ds(pl.multiple_of((number ^ bounds_ref[0]) * width, width), width)
        mask = jnp.concatenate([ids[at, :]] * (width // LANES), axis=1) == id_q
        result = []
        for h in range(heads):
            largest, total = carry[h]
            scores = product(k_ref[at, h * LANES : (h + 1) * LANES], queries[h], NT)
            scores = jnp.where(mask, scores, EXCLUDED)
            top = jnp.maximum(largest, jnp.max(scores, axis=0, keepdims=True))
            exponent = low(jnp.exp(scores - top))
            total = total * jnp.exp(largest - top) + product(turned[h, :, at], exponent)
            result.append((top, total))
        return tuple(result)

    start = tuple(
        (
            jnp.full((1, width), EXCLUDED, jnp.float32),
            jnp.zeros((turned.shape[1], width), jnp.float32),
        )
        for _ in range(heads)
    )
    where = 1 + 2 * (base + block)
    result = lax.fori_loop(bounds_ref[where], bounds_ref[where + 1], step, start)
    for h in range(heads):
        largest, total = result[h]
        denominator = total[HD : HD + 1]
        rows_out = low((total[:HD] / denominator).T)
        log_ref[h : h + 1, :] = largest + jnp.log(denominator)
        for number in range(2):

            @pl.when(block == number)
            def _():
                out_refs[number][:, h * HD : (h + 1) * HD] = rows_out


def attend(qkv, image_id, bounds, heads, base):
    rows = qkv.shape[0]
    wide = heads * LANES
    width = rows // 4
    out = far_shape(width, heads * HD)
    return pl.pallas_call(
        partial(attend_kernel, heads, base),
        grid_spec=pltpu.PrefetchScalarGridSpec(
            num_scalar_prefetch=1,
            grid=(2,),
            in_specs=[
                pl.BlockSpec((width, wide), lambda i, _: (base + i, 0)),
                pl.BlockSpec((rows, wide), lambda i, _: (0, 1)),
                pl.BlockSpec((rows, wide), lambda i, _: (0, 2)),
                pl.BlockSpec((1, width), lambda i, _: (0, base + i)),
                pl.BlockSpec((rows, 1), lambda i, _: (0, 0)),
            ],
            out_specs=[whole(out), whole(out), pl.BlockSpec((heads, width), lambda i, _: (0, i))],
            scratch_shapes=[
                pltpu.VMEM((heads, HD + 16, rows), jnp.bfloat16),
                pltpu.VMEM((rows, LANES), jnp.int32),
            ],
        ),
        out_shape=[out, out, far_shape(heads, 2 * width, dtype=jnp.float32)],
        name="attend",
        **settings(14),
    )(bounds, *[left(qkv)] * 3, image_id[None, :], image_id[:, None])


def attend_back_kernel(heads, base, bounds_ref, q_ref, k_ref, v_ref, *refs):
    grad_refs = refs[0:2]
    out_refs = refs[2:4]
    log_ref, id_q_ref, id_k_ref = refs[4:7]
    if base == 0:
        d_q_ref, sums, turned, ids = refs[7:]
    else:
        near_q_ref, near_sums_ref, d_ref, turned, ids, sums = refs[7:]
    block = pl.program_id(0)
    width = q_ref.shape[0]

    @pl.when(block == 0)
    def _():
        for h in range(heads):
            key = k_ref[:, h * LANES : (h + 1) * LANES].astype(jnp.float32).T
            turned[h] = low(key[:HD])
        ids[...] = jnp.broadcast_to(id_k_ref[...], ids.shape)
        if base == 0:
            sums[...] = jnp.zeros_like(sums)
        else:
            sums[...] = near_sums_ref[...]

    id_q = id_q_ref[...]
    ones = jnp.ones((8, HD), jnp.float32)
    none = jnp.zeros((width, HD), jnp.bfloat16)
    queries = [q_ref[:, h * LANES : (h + 1) * LANES] for h in range(heads)]
    logs = [log_ref[h : h + 1, :] for h in range(heads)]
    all_grads = jnp.where(block == 0, grad_refs[0][...], grad_refs[1][...])
    all_out = jnp.where(block == 0, out_refs[0][...], out_refs[1][...])
    grads = [all_grads[:, h * HD : (h + 1) * HD] for h in range(heads)]
    placed = [jnp.concatenate([none, g], axis=1) for g in grads]
    inner = []
    for h in range(heads):
        terms = add(grads[h], jnp.zeros_like(none)) * all_out[:, h * HD : (h + 1) * HD].astype(
            jnp.float32
        )
        inner.append(
            lax.dot_general(
                ones,
                terms,
                NT,
                precision=lax.Precision.HIGHEST,
                preferred_element_type=jnp.float32,
            )[:1]
        )

    def step(number, carry):
        at = pl.ds(pl.multiple_of((number ^ bounds_ref[0]) * width, width), width)
        mask = jnp.concatenate([ids[at, :]] * (width // LANES), axis=1) == id_q
        result = []
        for h in range(heads):
            columns = slice(h * LANES, (h + 1) * LANES)
            scores = product(k_ref[at, columns], queries[h], NT)
            probs = jnp.where(mask, jnp.exp(scores - logs[h]), 0.0)
            d_probs = product(v_ref[at, h * LANES : h * LANES + HD], grads[h], NT)
            d_scores = low(probs * (d_probs - inner[h]))
            sums[at, columns] += product(low(probs), placed[h]) + product(d_scores, queries[h])
            result.append(carry[h] + product(turned[h, :, at], d_scores))
        return tuple(result)

    start = tuple(jnp.zeros((HD, width), jnp.float32) for _ in range(heads))
    where = 1 + 2 * (base + block)
    result = lax.fori_loop(bounds_ref[where], bounds_ref[where + 1], step, start)
    if base == 0:
        for h in range(heads):
            d_q_ref[:, h * HD : (h + 1) * HD] = low((result[h] * 0.125).T)
    else:
        here = pl.ds(pl.multiple_of((base + block) * width, width), width)
        for h in range(heads):
            d_ref[here, 3 * h * HD : (3 * h + 1) * HD] = low((result[h] * 0.125).T)

        @pl.when(block == 1)
        def _():
            for h in range(heads):
                d_ref[: 2 * width, 3 * h * HD : (3 * h + 1) * HD] = near_q_ref[
                    :, h * HD : (h + 1) * HD
                ]
                d_ref[:, (3 * h + 1) * HD : (3 * h + 3) * HD] = low(
                    sums[:, h * LANES : (h + 1) * LANES]
                )


def attend_back(qkv, d_heads, heads_out, log_total, image_id, bounds, heads, base, near):
    rows = qkv.shape[0]
    wide = heads * LANES
    width = rows // 4
    sums = shape(rows, wide, dtype=jnp.float32)
    near = list(near)
    if base == 0:
        out_shape = [shape(2 * width, heads * HD), sums]
        out_specs = [pl.BlockSpec((width, heads * HD), lambda i, _: (i, 0)), whole(sums)]
    else:
        out_shape = shape(rows, 3 * heads * HD)
        out_specs = whole(out_shape)
    return pl.pallas_call(
        partial(attend_back_kernel, heads, base),
        grid_spec=pltpu.PrefetchScalarGridSpec(
            num_scalar_prefetch=1,
            grid=(2,),
            in_specs=[
                pl.BlockSpec((width, wide), lambda i, _: (base + i, 0)),
                pl.BlockSpec((rows, wide), lambda i, _: (0, 1)),
                pl.BlockSpec((rows, wide), lambda i, _: (0, 2)),
            ]
            + [whole(a) for a in (*d_heads, *heads_out)]
            + [
                pl.BlockSpec((heads, width), lambda i, _: (0, i)),
                pl.BlockSpec((1, width), lambda i, _: (0, base + i)),
                pl.BlockSpec((rows, 1), lambda i, _: (0, 0)),
            ]
            + [whole(a) for a in near],
            out_specs=out_specs,
            scratch_shapes=[
                pltpu.VMEM((heads, HD, rows), jnp.bfloat16),
                pltpu.VMEM((rows, LANES), jnp.int32),
            ]
            + ([pltpu.VMEM(sums.shape, jnp.float32)] if near else []),
        ),
        out_shape=out_shape,
        name="attend_back",
        **settings(20),
    )(
        bounds,
        *[left(qkv)] * 3,
        *d_heads,
        *heads_out,
        log_total,
        image_id[None, :],
        image_id[:, None],
        *near,
    )


def branch_kernel(*refs):
    parts = refs[0:4]
    weights = refs[4:8]
    tokens_ref, gain_ref, resid_ref, in_0_ref, in_1_ref = refs[8:]
    half = in_0_ref.shape[0]
    for number, in_ref in enumerate((in_0_ref, in_1_ref)):
        at = slice(number * half, (number + 1) * half)
        resid = tokens_ref[at, :].astype(jnp.float32)
        branch = product(parts[0][at, :], weights[0][...])
        for j in range(1, 4):
            branch = branch + product(parts[j][at, :], weights[j][...])
        resid = resid + branch
        resid_ref[at, :] = resid
        in_ref[...] = low(normalize(resid, gain_ref[...])[0])


def branch(parts, weights, tokens, gain):
    rows, model = tokens.shape
    operands = (*parts, *weights, tokens, gain)
    half = far_shape(rows // 2, model)
    resid = far_shape(rows, model, dtype=jnp.float32)
    return pl.pallas_call(
        branch_kernel,
        grid=(1,),
        in_specs=[whole(a) for a in operands],
        out_specs=[whole(resid), whole(half), whole(half)],
        out_shape=[resid, half, half],
        name="branch",
        **settings(2),
    )(*operands)


def mlp_kernel(x_a_ref, x_b_ref, g_a_ref, g_b_ref, up_ref, down_ref, *refs):
    m_a_ref, m_b_ref, x_ref, act_ref, d_pre_ref = refs[-5:]

    def rows(x_in_ref, g_ref, m_ref):
        mlp_in = x_in_ref[...]
        pre_act = product(mlp_in, up_ref[...])
        d_act = product(g_ref[...], down_ref[...], NT)
        below = 0.5 + 0.5 * lax.erf(pre_act * 0.7071067811865476)
        density = 0.3989422804014327 * jnp.exp(-0.5 * pre_act * pre_act)
        d_pre = low(d_act * (below + pre_act * density))
        m_ref[...] = low(product(d_pre, up_ref[...], NT))
        x_ref[...] = mlp_in
        act_ref[...] = low(pre_act * below)
        d_pre_ref[...] = d_pre

    @pl.when(pl.program_id(0) == 0)
    def _():
        rows(x_b_ref, g_b_ref, m_b_ref)

    @pl.when(pl.program_id(0) == 1)
    def _():
        rows(x_a_ref, g_a_ref, m_a_ref)


def mlp(x_a, x_b, g_a, g_b, half, place, w_up, w_down, earlier):
    length, model = x_a.shape
    hidden = w_up.shape[1]
    extra = [] if earlier is None else list(earlier)

    def grads():
        return pl.BlockSpec((length, model), lambda i: (half, 0))

    def kept(width):
        return pl.BlockSpec((length, width), lambda i: (place + 1 - i, 0))

    return pl.pallas_call(
        mlp_kernel,
        grid=(2,),
        in_specs=[whole(x_a), whole(x_b), grads(), grads(), whole(w_up), whole(w_down)]
        + [pl.BlockSpec(memory_space=pl.ANY)] * len(extra),
        out_specs=[whole(x_a), whole(x_a), kept(model), kept(hidden), kept(hidden)],
        out_shape=[shape(length, model), far_shape(length, model)]
        + [far_shape(8 * length, w) for w in (model, hidden, hidden)],
        input_output_aliases={6 + i: 2 + i for i in range(len(extra))},
        name="mlp",
        **settings(5),
    )(x_a, x_b, g_a, g_b, w_up, w_down, *extra)


def part_rows(count, bit, total, kept_ref, sent_ref):
    share = total.shape[0] // count
    width = kept_ref.shape[2]
    for pair in range(count // 2):
        for side, ref in ((bit, kept_ref), (1 - bit, sent_ref)):
            at = pl.ds(pl.multiple_of((2 * pair + side) * share, 8), share)
            ref[pair] = total[at, :width].astype(ref.dtype)


def row_sums(values):
    sums = jnp.sum(values, axis=1, keepdims=True)
    return jnp.broadcast_to(sums, (values.shape[0], LANES)).T[:1]


def mlp_rest_kernel(count, bit_ref, x_ref, act_ref, d_pre_ref, *refs):
    near_refs, far_refs = refs[0:2], refs[2:6]
    up_ref, down_ref = refs[6:8]
    y_refs = refs[8:12]
    kept_refs, sent_refs, gain_ref, d_up, d_down = refs[12:14], refs[14:16], *refs[16:]
    number = pl.program_id(0)
    tile = y_refs[0].shape[0]

    @pl.when(number == 0)
    def _():
        d_up[...] = jnp.zeros_like(d_up)
        d_down[...] = jnp.zeros_like(d_down)

    d_up[...] += product(x_ref[...], d_pre_ref[...], TN)
    y = low(product(act_ref[...], down_ref[...]))
    for side in range(2):

        @pl.when(number % 2 == side)
        def _():
            first, second = 2 * side, 2 * side + 1
            y_refs[first][...] = y[:tile]
            y_refs[second][...] = y[tile:]
            if side == 0:
                grads = [near_refs[0][...], near_refs[1][...]]
            else:
                early = number < 2
                grads = [jnp.where(early, far_refs[j][...], far_refs[2 + j][...]) for j in range(2)]
            d_down[...] += product(jnp.concatenate(grads, axis=0), act_ref[...], TN)

    @pl.when(number == 3)
    def _():
        part_rows(count, bit_ref[0], d_up, kept_refs[0], sent_refs[0])
        part_rows(count, bit_ref[0], d_down, kept_refs[1], sent_refs[1])
        gain_ref[...] = row_sums(d_up[...] * up_ref[...].astype(jnp.float32))


def mlp_rest(x, act, d_pre, out_grads, w_up, w_down):
    rows, model = x.shape
    hidden = act.shape[1]
    tile = rows // 8
    count = lax.axis_size("dp")
    bit = lax.axis_index("dp") % 2

    def kept_rows(width):
        return pl.BlockSpec((2 * tile, width), lambda i, _: (i, 0))

    halves = [pl.BlockSpec((tile, model), lambda i, _: (i // 2, 0))] * 4
    kept = far_shape(count // 2, model // count, hidden, dtype=jnp.float32)
    sent = far_shape(*kept.shape)
    gain = shape(1, model, dtype=jnp.float32)
    return pl.pallas_call(
        partial(mlp_rest_kernel, count),
        grid_spec=pltpu.PrefetchScalarGridSpec(
            num_scalar_prefetch=1,
            grid=(4,),
            in_specs=[kept_rows(model), kept_rows(hidden), kept_rows(hidden)]
            + halves[:2]
            + [whole(g) for g in out_grads[2:]]
            + [whole(w_up), whole(w_down)],
            out_specs=halves + [whole(kept)] * 2 + [whole(sent)] * 2 + [whole(gain)],
            scratch_shapes=[pltpu.VMEM((model, hidden), jnp.float32)] * 2,
        ),
        out_shape=[far_shape(2 * tile, model)] * 4 + [kept] * 2 + [sent] * 2 + [gain],
        name="mlp_rest",
        **settings(0.1),
    )(bit[None], left(x), left(act), left(d_pre), *(left(g) for g in out_grads), w_up, w_down)


def branch_back_kernel(*refs):
    cotangent_ref, resid_ref, gain_ref = refs[6:9]
    weights = refs[9:13]
    d_resid_ref, d_branch_ref = refs[13:15]
    out_refs = refs[15:19]
    for half in range(2):

        @pl.when(pl.program_id(0) == half)
        def _():
            own_ref, pair_ref, far_ref = refs[half], refs[2 + half], refs[4 + half]
            d_mlp_in = add(own_ref[...], pair_ref[...]) + far_ref[...].astype(jnp.float32)
            _, unit, inverse = normalize(resid_ref[...], gain_ref[...])
            d_resid = cotangent_ref[...].astype(jnp.float32) + restore(
                d_mlp_in, unit, inverse, gain_ref[...]
            )
            d_resid_ref[...] = d_resid
            d_branch = low(d_resid)
            d_branch_ref[...] = d_branch
            for j in range(4):
                out_refs[j][...] = low(product(d_branch, weights[j][...], NT))


def branch_back(own, pair, far, cotangent, resid, gain, weights):
    rows, model = resid.shape
    width = weights[0].shape[0]

    def at(columns):
        return pl.BlockSpec((rows // 2, columns), lambda i: (i, 0))

    operands = (*own, *pair, *far, cotangent, resid, gain, *weights)
    specs = [whole(a) for a in operands]
    specs[6] = specs[7] = at(model)
    return pl.pallas_call(
        branch_back_kernel,
        grid=(2,),
        in_specs=specs,
        out_specs=[at(model), at(model)] + [at(width)] * 4,
        out_shape=[far_shape(rows, model, dtype=jnp.float32), shape(rows, model)]
        + [far_shape(rows, width)] * 4,
        name="branch_back",
        **settings(4),
    )(*operands)


def out_grads_kernel(d_ref, *refs):
    for j in range(4):
        refs[4 + j][...] = low(product(d_ref[...], refs[j][...], TN))


def out_weight_grads(d_branch, parts):
    model = d_branch.shape[1]
    out = far_shape(model, parts[0].shape[1])
    return pl.pallas_call(
        out_grads_kernel,
        in_specs=[whole(a) for a in (d_branch, *parts)],
        out_specs=[whole(out)] * 4,
        out_shape=[out] * 4,
        name="out_weight_grads",
        **settings(2),
    )(d_branch, *parts)


def qkv_grads_kernel(count, bit_ref, *refs):
    x_refs = refs[0:4]
    d_ref, w_ref, kept_ref, sent_ref, rest_ref, gain_ref, total = refs[4:]
    number = pl.program_id(0)
    for j in range(4):

        @pl.when(number == j)
        def _():
            part = product(x_refs[j][...], d_ref[...], TN)
            total[...] = part if j == 0 else total[...] + part

    @pl.when(number == 3)
    def _():
        part_rows(count, bit_ref[0], total, kept_ref, sent_ref)
        rest_ref[...] = low(total[:, kept_ref.shape[2] :])
        gain_ref[...] = row_sums(total[...] * w_ref[...].astype(jnp.float32).T)


def qkv_grads(attn_ins, d_qkv, w_qkv, first):
    rows, model = attn_ins[0].shape
    width = d_qkv.shape[1]
    count = lax.axis_size("dp")
    bit = lax.axis_index("dp") % 2
    kept = far_shape(count // 2, model // count, first, dtype=jnp.float32)
    sent = far_shape(*kept.shape)
    rest = far_shape(model, width - first)
    gain = shape(1, model, dtype=jnp.float32)
    return pl.pallas_call(
        partial(qkv_grads_kernel, count),
        grid_spec=pltpu.PrefetchScalarGridSpec(
            num_scalar_prefetch=1,
            grid=(4,),
            in_specs=[whole(x) for x in attn_ins]
            + [pl.BlockSpec((rows, width), lambda i, _: (i, 0)), whole(w_qkv)],
            out_specs=[whole(kept), whole(sent), whole(rest), whole(gain)],
            scratch_shapes=[pltpu.VMEM((model, width), jnp.float32)],
        ),
        out_shape=[kept, sent, rest, gain],
        name="qkv_grads",
        **settings(5),
    )(bit[None], *attn_ins, d_qkv, w_qkv)


def unproject_kernel(d_ref, w_ref, *out_refs):
    for number in range(2):

        @pl.when(pl.program_id(0) == number)
        def _():
            out_refs[number][...] = low(product(d_ref[...], w_ref[...]))


def unproject(d_qkv, w_qkv, base):
    rows = d_qkv.shape[0] // 4
    out = far_shape(rows, w_qkv.shape[1])
    return pl.pallas_call(
        unproject_kernel,
        grid=(2,),
        in_specs=[
            pl.BlockSpec((rows, d_qkv.shape[1]), lambda i: (base + i, 0)),
            whole(w_qkv),
        ],
        out_specs=[whole(out), whole(out)],
        out_shape=[out, out],
        name="unproject",
        **settings(0.1),
    )(d_qkv, w_qkv)


def parted(total, distance):
    bit = (lax.axis_index("dp") // distance) % 2
    total = total.reshape(-1, 2, *total.shape[1:])
    return (
        lax.dynamic_index_in_dim(total, bit, 1, keepdims=False),
        low(lax.dynamic_index_in_dim(total, 1 - bit, 1, keepdims=False)),
    )


def halve(kept, got, distance):
    bit = (lax.axis_index("dp") // distance) % 2
    kept = kept.reshape(-1, 2, *kept.shape[1:])
    got = got.reshape(kept.shape)

    def side(number):
        return add(
            lax.dynamic_index_in_dim(kept, number, 1, keepdims=False),
            lax.dynamic_index_in_dim(got, number, 1, keepdims=False),
        )

    return side(bit), low(side(1 - bit))


def to_last(kept, sent, distance):
    while True:
        got = swap(sent, distance, "dp")
        distance *= 2
        if distance >= lax.axis_size("dp"):
            return kept[0], got[0]
        kept, sent = halve(kept, got, distance)


def sum_steps(value, axis, first=1):
    distance = first
    while distance < lax.axis_size(axis):
        value = value + swap(value, distance, axis)
        distance *= 2
    return value


def on_device(tokens, patch_side, gain_attn, w_qkv, w_out, gain_mlp, w_up, w_down, cotangent):
    rows, model = tokens.shape
    place = lax.axis_index("tp")
    group_rows = 4 * rows
    heads = w_out.shape[0] // HD

    attn_in = norm(tokens, gain_attn)
    pair = swap(attn_in, 1)
    across = swap(attn_in, 2)

    cells = (IMAGE // patch_side[0]) ** 2
    full = group_rows // cells
    order = place ^ jnp.arange(4, dtype=jnp.int32)
    positions = (order[:, None] * rows + jnp.arange(rows, dtype=jnp.int32)).reshape(-1)
    image_id = jnp.minimum(positions // cells, full)
    first_id = jnp.minimum(order * rows // cells, full)
    last_id = jnp.minimum((order * rows + rows - 1) // cells, full)
    first_block = first_id * cells // rows
    stop = jnp.where(last_id == full, group_rows, (last_id + 1) * cells)
    last_block = (stop + rows - 1) // rows
    bounds = jnp.concatenate(
        [place[None], jnp.stack([first_block, last_block], axis=1).reshape(-1)]
    )

    turned_qkv = w_qkv.T
    by_head = turned_qkv.reshape(heads, 3, HD, model)
    by_head = by_head * jnp.array([0.125, 1.0, 1.0], jnp.bfloat16)[:, None, None]
    spread = jnp.pad(by_head.transpose(1, 0, 2, 3), ((0, 0), (0, 0), (0, LANES - HD), (0, 0)))
    spread = spread.reshape(3 * heads * LANES, model)
    qkv = project([attn_in, pair], spread, 0, None)
    across, qkv = join(across, qkv)
    diagonal = swap(across, 1)
    w_across = swap(after(w_out, across), 2)
    qkv = project([across], spread, 2, qkv)
    diagonal, qkv = join(diagonal, qkv)
    qkv = project([diagonal], spread, 3, qkv)
    attn_ins = [attn_in, pair, across, diagonal]

    middle = rows // 2
    w_pair = swap(after(w_out, across), 1)
    grads_pair = swap(after(cotangent, across), 1)
    grads_0 = swap(after(cotangent[:middle], diagonal), 2)
    far = attend(qkv, image_id, bounds, heads, 2)
    *far, w_across, w_pair, grads_pair, grads_0 = join(*far, w_across, w_pair, grads_pair, grads_0)
    out_2, out_3, logs_far = far
    got_2, got_3 = swap(out_2, 2), swap(out_3, 3)
    w_diagonal = swap(w_across, 1)
    grads_0_diagonal = swap(grads_0, 1)
    grads_1 = swap(after(cotangent[middle:], out_2), 2)
    near = attend(after(qkv, out_2), image_id, bounds, heads, 0)
    *near, got_2, got_3, w_diagonal, grads_0_diagonal, grads_1 = join(
        *near, got_2, got_3, w_diagonal, grads_0_diagonal, grads_1
    )
    out_0, out_1, logs_near = near
    got_1, grads_1_diagonal = join(swap(out_1, 1), swap(grads_1, 1))
    mine = [out_0, got_1, got_2, got_3]
    w_outs = [w_out, w_pair, w_across, w_diagonal]
    out_grads = [cotangent, grads_pair, grads_0, grads_0_diagonal, grads_1, grads_1_diagonal]
    resid, *mlp_in = branch(mine, w_outs, tokens, gain_mlp)

    pairs = [swap(m, 1) for m in mlp_in]
    across_0 = swap(mlp_in[0], 2)
    own_0, pair_0, *kept = mlp(
        mlp_in[0], pairs[0], cotangent, grads_pair, 0, 0, w_up, w_down, None
    )
    own_1, pair_1, *kept = mlp(
        mlp_in[1], pairs[1], cotangent, grads_pair, 1, 4, w_up, w_down, kept
    )
    across_0, own_1, pair_0, pair_1 = join(across_0, own_1, pair_0, pair_1)
    across_1 = swap(after(mlp_in[1], across_0), 2)
    diagonal_0, pair_0, pair_1 = join(swap(across_0, 1), swap(pair_0, 1), swap(pair_1, 1))
    m_2, m_3, *kept = mlp(
        across_0, diagonal_0, grads_0, grads_0_diagonal, 0, 2, w_up, w_down, kept
    )
    far_0 = low(add(m_2, swap(m_3, 1)))
    across_1 = after(across_1, far_0)
    m_2, m_3, *kept = mlp(
        across_1, swap(across_1, 1), grads_1, grads_1_diagonal, 0, 6, w_up, w_down, kept
    )
    far_0 = swap(far_0, 2)
    far_1 = low(add(m_2, swap(m_3, 1)))
    kept[0] = after(kept[0], far_1)
    far_1 = swap(far_1, 2)
    rest = mlp_rest(*kept, out_grads, w_up, w_down)
    *rest, far_0, far_1 = join(*rest, far_0, far_1)
    *y, kept_up, kept_down, sent_up, sent_down, gain_mlp_part = rest

    d_resid, d_branch, *d_pieces = branch_back(
        (own_0, own_1), (pair_0, pair_1), (far_0, far_1), cotangent, resid, gain_mlp, w_outs
    )
    d_1, d_2, d_3 = [swap(d_pieces[j], j) for j in range(1, 4)]
    d_outs = out_weight_grads(after(d_branch, d_pieces[0]), mine)
    out_far = low(add(d_outs[2], swap(d_outs[3], 1)))
    back = attend_back(
        after(qkv, out_far, y[1]),
        (d_pieces[0], d_1),
        (out_0, out_1),
        logs_near,
        image_id,
        bounds,
        heads,
        0,
        (),
    )
    *back, got_up, d_2, d_3, out_far, mixed_pair = join(
        *back, swap(sent_up, 1, "dp"), d_2, d_3, swap(out_far, 2), swap(after(y[1], d_1), 1)
    )
    count = lax.axis_size("dp")
    out_pair, mixed_far = join(
        swap(after(d_outs[1], back[0]), 1), swap(after(y[3], back[0]), 1)
    )
    kept_up, sent_up = halve(kept_up, got_up, 2)
    d_out = add(d_outs[0], out_pair) + out_far.astype(jnp.float32)
    kept_out, sent_out = parted(d_out.reshape(count, model // count, -1), 1)
    mixed_far = low(add(y[2], mixed_far))
    sent_down = after(sent_down, back[0])
    d_qkv = attend_back(
        after(qkv, sent_out, sent_up, mixed_far, sent_down),
        (d_2, d_3),
        (out_2, out_3),
        logs_far,
        image_id,
        bounds,
        heads,
        2,
        back,
    )
    d_qkv, got_down, kept_up, got_up, got_out, mixed_far = join(
        d_qkv,
        swap(sent_down, 1, "dp"),
        *to_last(kept_up, sent_up, 2),
        swap(sent_out, 1, "dp"),
        swap(mixed_far, 2),
    )

    width = w_qkv.shape[1]
    first = 2 * width // (3 * LANES) * LANES
    kept_down, sent_down = halve(kept_down, got_down, 2)
    grad_up = low(add(kept_up, got_up))
    kept, sent, rest, gain_attn_part = qkv_grads(
        attn_ins, after(d_qkv, sent_down, grad_up), turned_qkv, first
    )
    got_up = swap(grad_up, 1, "grp")
    kept_down, got_down = to_last(kept_down, sent_down, 2)
    part_2, part_3 = unproject(after(d_qkv, sent, rest), turned_qkv, 2)
    part_2, part_3, got_up = join(part_2, part_3, got_up)
    gains = jnp.concatenate(
        [gain_attn_part / gain_attn[None, :], gain_mlp_part / gain_mlp[None, :]], axis=0
    )
    part_0, part_1 = unproject(after(d_qkv, part_2, gains), turned_qkv, 0)
    part_0, part_1, part_3, gains_pair = join(part_0, part_1, swap(part_3, 1), swap(gains, 1))
    gains = sum_steps(gains + gains_pair, "tp", 2)
    d_far = [
        low(add(part_2[at], part_3[at])) for at in (slice(None, middle), slice(middle, None))
    ]
    got, got_rest, gains, pair, far_0, far_1, kept_down, got_down = join(
        swap(sent, 1, "dp"),
        swap(rest, 1, "grp"),
        gains,
        swap(part_1, 1),
        *d_far,
        kept_down,
        got_down,
    )

    kept, sent = halve(
        jnp.concatenate([kept, kept_out], axis=2), jnp.concatenate([got, got_out], axis=2), 2
    )
    kept_rest, sent_rest = parted(add(rest, got_rest).reshape(count, model // count, -1), 1)
    grad_down = low(add(kept_down, got_down))
    kept, got, got_rest, far_0, gains, far_1 = join(
        *to_last(kept, sent, 2),
        swap(sent_rest, 1, "dp"),
        swap(far_0, 2),
        sum_steps(gains, "grp"),
        far_1,
    )
    got_down = swap(grad_down, 1, "grp")
    grad_first = low(add(kept, got))
    got = swap(grad_first, 1, "grp")
    kept_rest, got_rest = to_last(*halve(kept_rest, got_rest, 2), 2)
    kept_rest, got_rest, far_1, gains, got = join(
        kept_rest, got_rest, swap(far_1, 2), gains + swap(gains, 1, "dp"), got
    )
    gains = sum_steps(gains, "dp", 2)
    mixed_rows = low(resid + (add(y[0], mixed_pair) + mixed_far.astype(jnp.float32)))
    input_grad = norm_back(tokens, gain_attn, part_0, pair, (far_0, far_1), d_resid)
    grad_first = add(grad_first, got)
    grad_rest = kept_rest + got_rest.astype(jnp.float32)
    return (
        mixed_rows,
        input_grad,
        gains[0],
        jnp.concatenate([grad_first[:, :first], grad_rest], axis=1),
        grad_first[:, first:].T,
        gains[1],
        add(grad_up, got_up),
        add(grad_down, got_down).T,
    )


def solution(mesh):
    in_specs = (
        P(("grp", "dp", "tp"), None),
        P(("grp", "dp")),
        P(),
        P(None, "tp"),
        P("tp", None),
        P(),
        P(None, "tp"),
        P("tp", None),
        P(("grp", "dp", "tp"), None),
    )
    out_specs = (
        P(("grp", "dp", "tp"), None),
        P(("grp", "dp", "tp"), None),
        P(),
        P("dp", "tp"),
        P("tp", "dp"),
        P(),
        P("dp", "tp"),
        P("tp", "dp"),
    )
    return jax.shard_map(
        on_device, mesh=mesh, in_specs=in_specs, out_specs=out_specs, check_vma=False
    )
```

```python
from functools import partial

import jax
import jax.numpy as jnp
from jax import lax
from jax.experimental import pallas as pl
from jax.experimental.pallas import tpu as pltpu
from jax.sharding import PartitionSpec as P

HD = 64
LANES = 128
IMAGE = 240
EXCLUDED = -1e30
MIB = 1024 * 1024
NT = (((1,), (1,)), ((), ()))
TN = (((0,), (0,)), ((), ()))

epsilon = 1e-06


def normalize(values, scaling):
    centred = values - jnp.mean(values, axis=1, keepdims=True)
    inverse = lax.rsqrt(jnp.mean(centred * centred, axis=1, keepdims=True) + epsilon)
    normed = centred * inverse
    return (normed * scaling, normed, inverse)


def restore(d_normed, normed, inverse, scaling):
    d_scaled = d_normed * scaling
    return inverse * (
        d_scaled
        - jnp.mean(d_scaled, axis=1, keepdims=True)
        - normed * jnp.mean(d_scaled * normed, axis=1, keepdims=True)
    )


def swap(value, distance, axis="tp"):
    size = lax.axis_size(axis)
    return lax.ppermute(value, axis, [(i, i ^ distance) for i in range(size)])


def after(value, *earlier):
    return lax.optimization_barrier((value, *earlier))[0]


def join(*values):
    return lax.optimization_barrier(values)


def add(left, right):
    return left.astype(jnp.float32) + right.astype(jnp.float32)


def product(left, right, dims=(((1,), (0,)), ((), ()))):
    return lax.dot_general(left, right, dims, preferred_element_type=jnp.float32)


def low(value):
    return value.astype(jnp.bfloat16)


def settings(limit, microseconds=0.1):
    return dict(
        compiler_params=pltpu.CompilerParams(vmem_limit_bytes=limit * MIB),
        cost_estimate=pl.CostEstimate(
            flops=int(microseconds * 1.1e9), bytes_accessed=MIB, transcendentals=0
        ),
    )


def whole(array):
    return pl.BlockSpec(array.shape, lambda *_: (0,) * len(array.shape))


def shape(*dims, dtype=jnp.bfloat16):
    return jax.ShapeDtypeStruct(dims, dtype)


def far_shape(*dims, dtype=jnp.bfloat16):
    return pltpu.HBM(dims, dtype)


def left(array):
    return pltpu.with_memory_space_constraint(array, pltpu.HBM)


def norm_kernel(x_ref, gain_ref, out_ref, *half_refs):
    normed = low(normalize(x_ref[...].astype(jnp.float32), gain_ref[...])[0])
    out_ref[...] = normed
    for half in range(2):

        @pl.when(pl.program_id(0) == half)
        def _():
            half_refs[half][...] = normed


def norm(tokens, gain):
    rows, model = tokens.shape
    tile = pl.BlockSpec((rows // 2, model), lambda i: (i, 0))
    return pl.pallas_call(
        norm_kernel,
        grid=(2,),
        in_specs=[tile, whole(gain)],
        out_specs=[tile] + [pl.BlockSpec((rows // 2, model), lambda i: (0, 0))] * 2,
        out_shape=[far_shape(rows, model)] + [far_shape(rows // 2, model)] * 2,
        name="norm",
        **settings(8, 2),
    )(left(tokens), left(gain))


def norm_back_kernel(x_ref, gain_ref, own_ref, pair_ref, far_ref, d_ref, out_ref):
    d_normed = add(own_ref[...], pair_ref[...]) + far_ref[...].astype(jnp.float32)
    _, unit, inverse = normalize(x_ref[...].astype(jnp.float32), gain_ref[...])
    out_ref[...] = d_ref[...] + restore(d_normed, unit, inverse, gain_ref[...])


def norm_back(tokens, gain, own, pair, far, d_resid):
    rows, model = tokens.shape
    tile = pl.BlockSpec((rows // 4, model), lambda i: (i, 0))
    return pl.pallas_call(
        norm_back_kernel,
        grid=(4,),
        in_specs=[tile, whole(gain)] + [tile] * 4,
        out_specs=tile,
        out_shape=shape(rows, model, dtype=jnp.float32),
        name="norm_back",
        **settings(16, 2),
    )(tokens, gain, own, pair, far, d_resid)


def project_kernel(count, *refs):
    out_ref = refs[-1]
    for number in range(count):

        @pl.when(pl.program_id(0) == number)
        def _():
            out_ref[...] = low(product(refs[number][...], refs[count][...], NT))


def project(blocks, weights, places, earlier):
    rows = blocks[0].shape[0]
    wide = weights.shape[0]
    count = len(blocks)
    group_rows = rows * 4 if earlier is None else earlier.shape[0]
    extra = [] if earlier is None else [earlier]
    return pl.pallas_call(
        partial(project_kernel, count),
        grid=(count,),
        in_specs=[whole(x) for x in blocks]
        + [whole(weights)]
        + [pl.BlockSpec(memory_space=pl.ANY)] * len(extra),
        out_specs=pl.BlockSpec(
            (rows, wide), lambda i: (places[0] + i * (places[-1] - places[0]), 0)
        ),
        out_shape=shape(group_rows, wide),
        input_output_aliases={count + 1: 0} if extra else {},
        name="project",
        **settings(16),
    )(*blocks, weights, *extra)


def attend_kernel(
    heads, base, bounds_ref, q_ref, k_ref, v_ref, id_q_ref, id_k_ref, *refs
):
    out_refs = refs[:2]
    log_ref, turned, ids = refs[2:]
    block = pl.program_id(0)
    width = q_ref.shape[0]

    @pl.when(block == 0)
    def _():
        for h in range(heads):
            value = v_ref[:, h * LANES : (h + 1) * LANES].astype(jnp.float32).T
            turned[h, :HD] = low(value[:HD])
            turned[h, HD:] = jnp.ones((turned.shape[1] - HD, v_ref.shape[0]), jnp.bfloat16)
        ids[...] = jnp.broadcast_to(id_k_ref[...], ids.shape)

    id_q = id_q_ref[...]
    queries = [q_ref[:, h * LANES : (h + 1) * LANES] for h in range(heads)]

    def step(number, carry):
        at = pl.ds(pl.multiple_of((number ^ bounds_ref[0]) * width, width), width)
        mask = jnp.concatenate([ids[at, :]] * (width // LANES), axis=1) == id_q
        result = []
        for h in range(heads):
            largest, total = carry[h]
            scores = product(k_ref[at, h * LANES : (h + 1) * LANES], queries[h], NT)
            scores = jnp.where(mask, scores, EXCLUDED)
            top = jnp.maximum(largest, jnp.max(scores, axis=0, keepdims=True))
            exponent = low(jnp.exp(scores - top))
            total = total * jnp.exp(largest - top) + product(turned[h, :, at], exponent)
            result.append((top, total))
        return tuple(result)

    start = tuple(
        (
            jnp.full((1, width), EXCLUDED, jnp.float32),
            jnp.zeros((turned.shape[1], width), jnp.float32),
        )
        for _ in range(heads)
    )
    where = 1 + 2 * (base + block)
    result = lax.fori_loop(bounds_ref[where], bounds_ref[where + 1], step, start)
    for h in range(heads):
        largest, total = result[h]
        denominator = total[HD : HD + 1]
        rows_out = low((total[:HD] / denominator).T)
        log_ref[h : h + 1, :] = largest + jnp.log(denominator)
        for number in range(2):

            @pl.when(block == number)
            def _():
                out_refs[number][:, h * HD : (h + 1) * HD] = rows_out


def attend(qkv, image_id, bounds, heads, base):
    rows = qkv.shape[0]
    wide = heads * LANES
    width = rows // 4
    out = far_shape(width, heads * HD)
    return pl.pallas_call(
        partial(attend_kernel, heads, base),
        grid_spec=pltpu.PrefetchScalarGridSpec(
            num_scalar_prefetch=1,
            grid=(2,),
            in_specs=[
                pl.BlockSpec((width, wide), lambda i, _: (base + i, 0)),
                pl.BlockSpec((rows, wide), lambda i, _: (0, 1)),
                pl.BlockSpec((rows, wide), lambda i, _: (0, 2)),
                pl.BlockSpec((1, width), lambda i, _: (0, base + i)),
                pl.BlockSpec((rows, 1), lambda i, _: (0, 0)),
            ],
            out_specs=[whole(out), whole(out), pl.BlockSpec((heads, width), lambda i, _: (0, i))],
            scratch_shapes=[
                pltpu.VMEM((heads, HD + 16, rows), jnp.bfloat16),
                pltpu.VMEM((rows, LANES), jnp.int32),
            ],
        ),
        out_shape=[out, out, far_shape(heads, 2 * width, dtype=jnp.float32)],
        name="attend",
        **settings(24, 14 if base else 3),
    )(bounds, *[qkv] * 3, image_id[None, :], image_id[:, None])


def attend_back_kernel(heads, base, bounds_ref, q_ref, k_ref, v_ref, *refs):
    grad_refs = refs[0:2]
    out_refs = refs[2:4]
    log_ref, id_q_ref, id_k_ref = refs[4:7]
    if base == 0:
        d_q_ref, sums, turned, ids = refs[7:]
    else:
        near_q_ref, near_sums_ref, d_ref, turned, ids, sums = refs[7:]
    block = pl.program_id(0)
    width = q_ref.shape[0]

    @pl.when(block == 0)
    def _():
        for h in range(heads):
            key = k_ref[:, h * LANES : (h + 1) * LANES].astype(jnp.float32).T
            turned[h] = low(key[:HD])
        ids[...] = jnp.broadcast_to(id_k_ref[...], ids.shape)
        if base == 0:
            sums[...] = jnp.zeros_like(sums)
        else:
            sums[...] = near_sums_ref[...]

    id_q = id_q_ref[...]
    ones = jnp.ones((8, HD), jnp.float32)
    none = jnp.zeros((width, HD), jnp.bfloat16)
    queries = [q_ref[:, h * LANES : (h + 1) * LANES] for h in range(heads)]
    logs = [log_ref[h : h + 1, :] for h in range(heads)]
    all_grads = jnp.where(block == 0, grad_refs[0][...], grad_refs[1][...])
    all_out = jnp.where(block == 0, out_refs[0][...], out_refs[1][...])
    grads = [all_grads[:, h * HD : (h + 1) * HD] for h in range(heads)]
    placed = [jnp.concatenate([none, g], axis=1) for g in grads]
    inner = []
    for h in range(heads):
        terms = add(grads[h], jnp.zeros_like(none)) * all_out[:, h * HD : (h + 1) * HD].astype(
            jnp.float32
        )
        inner.append(
            lax.dot_general(
                ones,
                terms,
                NT,
                precision=lax.Precision.HIGHEST,
                preferred_element_type=jnp.float32,
            )[:1]
        )

    def step(number, carry):
        at = pl.ds(pl.multiple_of((number ^ bounds_ref[0]) * width, width), width)
        mask = jnp.concatenate([ids[at, :]] * (width // LANES), axis=1) == id_q
        result = []
        for h in range(heads):
            columns = slice(h * LANES, (h + 1) * LANES)
            scores = product(k_ref[at, columns], queries[h], NT)
            probs = jnp.where(mask, jnp.exp(scores - logs[h]), 0.0)
            d_probs = product(v_ref[at, h * LANES : h * LANES + HD], grads[h], NT)
            d_scores = low(probs * (d_probs - inner[h]))
            sums[at, columns] += product(low(probs), placed[h]) + product(d_scores, queries[h])
            result.append(carry[h] + product(turned[h, :, at], d_scores))
        return tuple(result)

    start = tuple(jnp.zeros((HD, width), jnp.float32) for _ in range(heads))
    where = 1 + 2 * (base + block)
    result = lax.fori_loop(bounds_ref[where], bounds_ref[where + 1], step, start)
    if base == 0:
        for h in range(heads):
            d_q_ref[:, h * HD : (h + 1) * HD] = low((result[h] * 0.125).T)
    else:
        here = pl.ds(pl.multiple_of((base + block) * width, width), width)
        for h in range(heads):
            d_ref[here, 3 * h * HD : (3 * h + 1) * HD] = low((result[h] * 0.125).T)

        @pl.when(block == 1)
        def _():
            for h in range(heads):
                d_ref[: 2 * width, 3 * h * HD : (3 * h + 1) * HD] = near_q_ref[
                    :, h * HD : (h + 1) * HD
                ]
                d_ref[:, (3 * h + 1) * HD : (3 * h + 3) * HD] = low(
                    sums[:, h * LANES : (h + 1) * LANES]
                )


def attend_back(qkv, d_heads, heads_out, log_total, image_id, bounds, heads, base, near):
    rows = qkv.shape[0]
    wide = heads * LANES
    width = rows // 4
    sums = far_shape(rows, wide, dtype=jnp.float32)
    near = list(near)
    if base == 0:
        out_shape = [far_shape(2 * width, heads * HD), sums]
        out_specs = [pl.BlockSpec((width, heads * HD), lambda i, _: (i, 0)), whole(sums)]
    else:
        out_shape = shape(rows, 3 * heads * HD)
        out_specs = whole(out_shape)
    return pl.pallas_call(
        partial(attend_back_kernel, heads, base),
        grid_spec=pltpu.PrefetchScalarGridSpec(
            num_scalar_prefetch=1,
            grid=(2,),
            in_specs=[
                pl.BlockSpec((width, wide), lambda i, _: (base + i, 0)),
                pl.BlockSpec((rows, wide), lambda i, _: (0, 1)),
                pl.BlockSpec((rows, wide), lambda i, _: (0, 2)),
            ]
            + [whole(a) for a in (*d_heads, *heads_out)]
            + [
                pl.BlockSpec((heads, width), lambda i, _: (0, i)),
                pl.BlockSpec((1, width), lambda i, _: (0, base + i)),
                pl.BlockSpec((rows, 1), lambda i, _: (0, 0)),
            ]
            + [whole(a) for a in near],
            out_specs=out_specs,
            scratch_shapes=[
                pltpu.VMEM((heads, HD, rows), jnp.bfloat16),
                pltpu.VMEM((rows, LANES), jnp.int32),
            ]
            + ([pltpu.VMEM(sums.shape, jnp.float32)] if near else []),
        ),
        out_shape=out_shape,
        name="attend_back",
        **settings(32, 20 if base else 3),
    )(
        bounds,
        *[left(qkv)] * 3,
        *d_heads,
        *heads_out,
        log_total,
        image_id[None, :],
        image_id[:, None],
        *(left(a) for a in near),
    )


def branch_kernel(*refs):
    parts = refs[0:4]
    weights = refs[4:8]
    tokens_ref, gain_ref, resid_ref, in_0_ref, in_1_ref = refs[8:]
    half = in_0_ref.shape[0]
    for number, in_ref in enumerate((in_0_ref, in_1_ref)):
        at = slice(number * half, (number + 1) * half)
        resid = tokens_ref[at, :].astype(jnp.float32)
        branch = product(parts[0][at, :], weights[0][...])
        for j in range(1, 4):
            branch = branch + product(parts[j][at, :], weights[j][...])
        resid = resid + branch
        resid_ref[at, :] = resid
        in_ref[...] = low(normalize(resid, gain_ref[...])[0])


def branch(parts, weights, tokens, gain):
    rows, model = tokens.shape
    operands = (*parts, *weights, tokens, gain)
    half = far_shape(rows // 2, model)
    resid = far_shape(rows, model, dtype=jnp.float32)
    return pl.pallas_call(
        branch_kernel,
        grid=(1,),
        in_specs=[whole(a) for a in operands],
        out_specs=[whole(resid), whole(half), whole(half)],
        out_shape=[resid, half, half],
        name="branch",
        **settings(16, 2),
    )(left(parts[0]), *operands[1:])


def mlp_kernel(x_a_ref, x_b_ref, g_a_ref, g_b_ref, up_ref, down_ref, *refs):
    m_a_ref, m_b_ref, y_a_ref, y_b_ref, act_ref, d_pre_ref = refs[-6:]

    def rows(x_in_ref, g_in_ref, m_ref, y_ref):
        mlp_in = x_in_ref[...]
        out_grads = g_in_ref[...]
        pre_act = product(mlp_in, up_ref[...])
        d_act = product(out_grads, down_ref[...], NT)
        below = 0.5 + 0.5 * lax.erf(pre_act * 0.7071067811865476)
        density = 0.3989422804014327 * jnp.exp(-0.5 * pre_act * pre_act)
        d_pre = low(d_act * (below + pre_act * density))
        act = low(pre_act * below)
        m_ref[...] = low(product(d_pre, up_ref[...], NT))
        y_ref[...] = low(product(act, down_ref[...]))
        act_ref[...] = act
        d_pre_ref[...] = d_pre

    @pl.when(pl.program_id(0) == 0)
    def _():
        rows(x_b_ref, g_b_ref, m_b_ref, y_b_ref)

    @pl.when(pl.program_id(0) == 1)
    def _():
        rows(x_a_ref, g_a_ref, m_a_ref, y_a_ref)


def mlp(x_a, x_b, g_a, g_b, half, place, w_up, w_down, earlier, microseconds):
    length, model = x_a.shape
    hidden = w_up.shape[1]
    extra = [] if earlier is None else list(earlier)

    def grads():
        return pl.BlockSpec((length, model), lambda i: (half, 0))

    def kept(width):
        return pl.BlockSpec((length, width), lambda i: (2 * place + 1 - i, 0))

    return pl.pallas_call(
        mlp_kernel,
        grid=(2,),
        in_specs=[whole(x_a), whole(x_b), grads(), grads(), whole(w_up), whole(w_down)]
        + [pl.BlockSpec(memory_space=pl.ANY)] * len(extra),
        out_specs=[whole(x_a)] * 4 + [kept(hidden)] * 2,
        out_shape=[far_shape(length, model)] * 4
        + [far_shape(4 * length, hidden)] * 2,
        input_output_aliases={6 + i: 4 + i for i in range(len(extra))},
        name="mlp",
        **settings(20, microseconds),
    )(x_a, x_b, g_a, g_b, w_up, w_down, *extra)


def part_rows(count, bit, totals, kept_ref, sent_ref):
    share = totals[0].shape[0] // count
    for pair in range(count // 2):
        for side, ref in ((bit, kept_ref), (1 - bit, sent_ref)):
            at = pl.ds(pl.multiple_of((2 * pair + side) * share, 8), share)
            first = 0
            for total in totals:
                width = min(total.shape[1], ref.shape[2] - first)
                ref[pair, :, first : first + width] = total[at, :width].astype(ref.dtype)
                first += width


def row_sums(values):
    sums = jnp.sum(values, axis=1, keepdims=True)
    return jnp.broadcast_to(sums, (values.shape[0], LANES)).T[:1]


def mlp_grads_kernel(count, bit_ref, act_ref, d_pre_ref, g_a_ref, g_b_ref, *refs):
    number = pl.program_id(0)
    x_refs = refs[0:4]
    if count:
        up_ref, old_up_ref, old_down_ref, kept_ref, sent_ref, gain_ref, d_up, d_down = refs[4:]
    else:
        d_up, d_down = refs[4:]

    @pl.when(number == 0)
    def _():
        if count:
            d_up[...] = old_up_ref[...]
            d_down[...] = old_down_ref[...]
        else:
            d_up[...] = jnp.zeros_like(d_up)
            d_down[...] = jnp.zeros_like(d_down)

    for half in range(2):

        @pl.when(number == half)
        def _():
            x = jnp.concatenate([x_refs[2 * half][...], x_refs[2 * half + 1][...]], axis=0)
            d_up[...] += product(x, d_pre_ref[...], TN)

    grads = jnp.concatenate([g_a_ref[...], g_b_ref[...]], axis=0)
    d_down[...] += product(grads, act_ref[...], TN)

    @pl.when(number == 1)
    def _():
        if count:
            part_rows(count, bit_ref[0], (d_up, d_down), kept_ref, sent_ref)
            gain_ref[...] = row_sums(d_up[...] * up_ref[...].astype(jnp.float32))


def mlp_grads(act, d_pre, g_a, g_b, blocks, w_up, earlier):
    rows, hidden = act.shape
    model = g_a.shape[1]
    tile = rows // 4
    count = lax.axis_size("dp")
    bit = lax.axis_index("dp") % 2
    total = shape(model, hidden, dtype=jnp.float32)
    kept = far_shape(count // 2, model // count, 2 * hidden, dtype=jnp.float32)
    sent = far_shape(*kept.shape)
    gain = shape(1, model, dtype=jnp.float32)
    extra = [] if earlier is None else [w_up, *earlier]
    outs = [kept, sent, gain] if extra else [total, total]

    def half(rows, columns):
        return pl.BlockSpec((rows, columns), lambda i, _: (i, 0))

    return pl.pallas_call(
        partial(mlp_grads_kernel, count if extra else 0),
        grid_spec=pltpu.PrefetchScalarGridSpec(
            num_scalar_prefetch=1,
            grid=(2,),
            in_specs=[half(2 * tile, hidden)] * 2
            + [half(tile, model)] * 2
            + [whole(a) for a in (*blocks, *extra)],
            out_specs=[whole(a) for a in outs],
            scratch_shapes=[pltpu.VMEM((model, hidden), jnp.float32)] * 2 if extra else [],
        ),
        out_shape=outs,
        name="mlp_grads",
        **settings(40),
    )(bit[None], *(left(a) for a in (act, d_pre, g_a, g_b, *blocks)), *extra)


def branch_back_kernel(*refs):
    cotangent_ref, resid_ref, gain_ref = refs[6:9]
    weights = refs[9:13]
    d_resid_ref, d_branch_ref = refs[13:15]
    out_refs = refs[15:19]
    for half in range(2):

        @pl.when(pl.program_id(0) == half)
        def _():
            own_ref, pair_ref, far_ref = refs[half], refs[2 + half], refs[4 + half]
            d_mlp_in = add(own_ref[...], pair_ref[...]) + far_ref[...].astype(jnp.float32)
            _, unit, inverse = normalize(resid_ref[...], gain_ref[...])
            d_resid = cotangent_ref[...].astype(jnp.float32) + restore(
                d_mlp_in, unit, inverse, gain_ref[...]
            )
            d_resid_ref[...] = d_resid
            d_branch = low(d_resid)
            d_branch_ref[...] = d_branch
            for j in range(4):
                out_refs[j][...] = low(product(d_branch, weights[j][...], NT))


def branch_back(own, pair, far, cotangent, resid, gain, weights):
    rows, model = resid.shape
    width = weights[0].shape[0]

    def at(columns):
        return pl.BlockSpec((rows // 2, columns), lambda i: (i, 0))

    operands = (*own, *pair, *far, cotangent, resid, gain, *weights)
    specs = [whole(a) for a in operands]
    specs[6] = specs[7] = at(model)
    return pl.pallas_call(
        branch_back_kernel,
        grid=(2,),
        in_specs=specs,
        out_specs=[at(model), at(model)] + [at(width)] * 4,
        out_shape=[far_shape(rows, model, dtype=jnp.float32), shape(rows, model)]
        + [far_shape(rows, width)] * 4,
        name="branch_back",
        **settings(16),
    )(*operands)


def out_grads_kernel(d_ref, *refs):
    for j in range(4):
        refs[4 + j][...] = low(product(d_ref[...], refs[j][...], TN))


def out_weight_grads(d_branch, parts):
    model = d_branch.shape[1]
    out = far_shape(model, parts[0].shape[1])
    return pl.pallas_call(
        out_grads_kernel,
        in_specs=[whole(a) for a in (d_branch, *parts)],
        out_specs=[whole(out)] * 4,
        out_shape=[out] * 4,
        name="out_weight_grads",
        **settings(16),
    )(d_branch, *parts)


def qkv_grads_kernel(count, bit_ref, *refs):
    x_refs = refs[0:6]
    d_ref, w_ref, kept_ref, sent_ref, gain_ref, total = refs[6:]
    number = pl.program_id(0)
    for j in range(4):

        @pl.when(number == j)
        def _():
            if j < 2:
                block = x_refs[j][...]
            else:
                block = jnp.concatenate([r[...] for r in x_refs[2 * j - 2 : 2 * j]], axis=0)
            part = product(block, d_ref[...], TN)
            total[...] = part if j == 0 else total[...] + part

    @pl.when(number == 3)
    def _():
        part_rows(count, bit_ref[0], (total,), kept_ref, sent_ref)
        gain_ref[...] = row_sums(total[...] * w_ref[...].astype(jnp.float32).T)


def qkv_grads(attn_ins, d_qkv, w_qkv):
    rows, model = attn_ins[0].shape
    width = d_qkv.shape[1]
    count = lax.axis_size("dp")
    bit = lax.axis_index("dp") % 2
    kept = far_shape(count // 2, model // count, width, dtype=jnp.float32)
    sent = far_shape(*kept.shape)
    gain = shape(1, model, dtype=jnp.float32)
    return pl.pallas_call(
        partial(qkv_grads_kernel, count),
        grid_spec=pltpu.PrefetchScalarGridSpec(
            num_scalar_prefetch=1,
            grid=(4,),
            in_specs=[whole(x) for x in attn_ins]
            + [pl.BlockSpec((rows, width), lambda i, _: (i, 0)), whole(w_qkv)],
            out_specs=[whole(kept), whole(sent), whole(gain)],
            scratch_shapes=[pltpu.VMEM((model, width), jnp.float32)],
        ),
        out_shape=[kept, sent, gain],
        name="qkv_grads",
        **settings(24),
    )(bit[None], *attn_ins, d_qkv, w_qkv)


def unproject_kernel(d_ref, w_ref, *out_refs):
    for number in range(2):

        @pl.when(pl.program_id(0) == number)
        def _():
            out_refs[number][...] = low(product(d_ref[...], w_ref[...]))


def unproject(d_qkv, w_qkv, base):
    rows = d_qkv.shape[0] // 4
    out = far_shape(rows, w_qkv.shape[1])
    return pl.pallas_call(
        unproject_kernel,
        grid=(2,),
        in_specs=[
            pl.BlockSpec((rows, d_qkv.shape[1]), lambda i: (base + i, 0)),
            whole(w_qkv),
        ],
        out_specs=[whole(out), whole(out)],
        out_shape=[out, out],
        name="unproject",
        **settings(16),
    )(d_qkv, w_qkv)


def parted(total, distance):
    bit = (lax.axis_index("dp") // distance) % 2
    total = total.reshape(-1, 2, *total.shape[1:])
    return (
        lax.dynamic_index_in_dim(total, bit, 1, keepdims=False),
        low(lax.dynamic_index_in_dim(total, 1 - bit, 1, keepdims=False)),
    )


def halve(kept, got, distance):
    bit = (lax.axis_index("dp") // distance) % 2
    kept = kept.reshape(-1, 2, *kept.shape[1:])
    got = got.reshape(kept.shape)

    def side(number):
        return add(
            lax.dynamic_index_in_dim(kept, number, 1, keepdims=False),
            lax.dynamic_index_in_dim(got, number, 1, keepdims=False),
        )

    return side(bit), low(side(1 - bit))


def to_last(kept, sent, distance):
    while True:
        got = swap(sent, distance, "dp")
        distance *= 2
        if distance >= lax.axis_size("dp"):
            return kept[0], got[0]
        kept, sent = halve(kept, got, distance)


def sum_steps(value, axis, first=1):
    distance = first
    while distance < lax.axis_size(axis):
        value = value + swap(value, distance, axis)
        distance *= 2
    return value


def on_device(tokens, patch_side, gain_attn, w_qkv, w_out, gain_mlp, w_up, w_down, cotangent):
    rows, model = tokens.shape
    place = lax.axis_index("tp")
    group_rows = 4 * rows
    heads = w_out.shape[0] // HD

    attn_in, *halves = norm(tokens, gain_attn)
    pair = swap(attn_in, 1)
    across_0 = swap(halves[0], 2)
    across_1 = swap(after(halves[1], pair), 2)

    cells = (IMAGE // patch_side[0]) ** 2
    full = group_rows // cells
    order = place ^ jnp.arange(4, dtype=jnp.int32)
    positions = (order[:, None] * rows + jnp.arange(rows, dtype=jnp.int32)).reshape(-1)
    image_id = jnp.minimum(positions // cells, full)
    first_id = jnp.minimum(order * rows // cells, full)
    last_id = jnp.minimum((order * rows + rows - 1) // cells, full)
    first_block = first_id * cells // rows
    stop = jnp.where(last_id == full, group_rows, (last_id + 1) * cells)
    last_block = (stop + rows - 1) // rows
    bounds = jnp.concatenate(
        [place[None], jnp.stack([first_block, last_block], axis=1).reshape(-1)]
    )

    turned_qkv = w_qkv.T
    by_head = turned_qkv.reshape(heads, 3, HD, model)
    by_head = by_head * jnp.array([0.125, 1.0, 1.0], jnp.bfloat16)[:, None, None]
    spread = jnp.pad(by_head.transpose(1, 0, 2, 3), ((0, 0), (0, 0), (0, LANES - HD), (0, 0)))
    spread = spread.reshape(3 * heads * LANES, model)
    qkv = project([attn_in, pair], spread, (0, 1), None)
    across_0, qkv = join(across_0, qkv)
    diagonal_0 = swap(across_0, 1)
    qkv = project([across_0, diagonal_0], spread, (4, 6), qkv)
    across_1, qkv = join(across_1, qkv)
    diagonal_1 = swap(across_1, 1)
    w_across = swap(after(w_out, across_1), 2)
    qkv = project([across_1], spread, (5,), qkv)
    diagonal_1, qkv = join(diagonal_1, qkv)
    qkv = project([diagonal_1], spread, (7,), qkv)
    attn_ins = [attn_in, pair, across_0, across_1, diagonal_0, diagonal_1]

    middle = rows // 2
    w_pair = swap(after(w_out, across_1), 1)
    grads_pair = swap(after(cotangent, across_1), 1)
    grads_across = swap(after(cotangent, diagonal_1), 2)
    far = attend(qkv, image_id, bounds, heads, 2)
    *far, w_across, w_pair, grads_pair = join(*far, w_across, w_pair, grads_pair)
    out_2, out_3, logs_far = far
    got_2, got_3 = swap(out_2, 2), swap(out_3, 3)
    w_diagonal = swap(w_across, 1)
    near = attend(after(qkv, out_2), image_id, bounds, heads, 0)
    *near, got_2, got_3, w_diagonal, grads_across = join(
        *near, got_2, got_3, w_diagonal, grads_across
    )
    out_0, out_1, logs_near = near
    got_1 = swap(out_1, 1)
    mine = [out_0, got_1, got_2, got_3]
    w_outs = [w_out, w_pair, w_across, w_diagonal]
    resid, *mlp_in = branch(mine, w_outs, tokens, gain_mlp)
    grads_diagonal = swap(after(grads_across, got_1), 1)

    pairs = [swap(m, 1) for m in mlp_in]
    across_0 = swap(mlp_in[0], 2)
    own_0, pair_0, y_00, y_10, *near = mlp(
        mlp_in[0], pairs[0], cotangent, grads_pair, 0, 0, w_up, w_down, None, 5
    )
    own_1, pair_1, y_01, y_11, *near = mlp(
        mlp_in[1], pairs[1], cotangent, grads_pair, 1, 1, w_up, w_down, near, 5
    )
    across_0, own_1, pair_0, pair_1 = join(across_0, own_1, pair_0, pair_1)
    across_1 = swap(after(mlp_in[1], across_0), 2)
    diagonal_0, pair_0, pair_1 = join(swap(across_0, 1), swap(pair_0, 1), swap(pair_1, 1))
    m_2, m_3, y_20, y_30, *kept = mlp(
        across_0, diagonal_0, grads_across, grads_diagonal, 0, 0, w_up, w_down, None, 0.1
    )
    sums = mlp_grads(
        after(near[0], m_2),
        near[1],
        cotangent,
        grads_pair,
        (mlp_in[0], pairs[0], mlp_in[1], pairs[1]),
        w_up,
        None,
    )
    across_1, m_2, *sums = join(across_1, m_2, *sums)
    far_0 = low(add(m_2, swap(m_3, 1)))
    diagonal_1 = swap(across_1, 1)
    m_2, m_3, y_21, y_31, *kept = mlp(
        across_1, diagonal_1, grads_across, grads_diagonal, 1, 1, w_up, w_down, kept, 0.1
    )
    far_0, m_2 = join(swap(far_0, 2), m_2)
    far_1 = low(add(m_2, swap(m_3, 1)))
    kept_mlp, sent_mlp, gain_mlp_part = mlp_grads(
        after(kept[0], far_1),
        kept[1],
        grads_across,
        grads_diagonal,
        (across_0, diagonal_0, across_1, diagonal_1),
        w_up,
        sums,
    )
    mixed_far = [
        low(add(after(y, sent_mlp), swap(after(y_pair, far_1), 1)))
        for y, y_pair in ((y_20, y_30), (y_21, y_31))
    ]
    mixed_far, kept_mlp, sent_mlp, far_1 = join(
        jnp.concatenate(mixed_far, axis=0), kept_mlp, sent_mlp, swap(far_1, 2)
    )

    d_resid, d_branch, *d_pieces = branch_back(
        (own_0, own_1), (pair_0, pair_1), (far_0, far_1), cotangent, resid, gain_mlp, w_outs
    )
    d_1, d_2, d_3 = [swap(d_pieces[j], j) for j in range(1, 4)]
    d_outs = out_weight_grads(after(d_branch, d_pieces[0]), mine)
    out_far = low(add(d_outs[2], swap(d_outs[3], 1)))
    back = attend_back(
        after(qkv, out_far),
        (d_pieces[0], d_1),
        (out_0, out_1),
        logs_near,
        image_id,
        bounds,
        heads,
        0,
        (),
    )
    *back, got_mlp, d_2, d_3, out_far = join(
        *back, swap(sent_mlp, 1, "dp"), d_2, d_3, swap(out_far, 2)
    )
    count = lax.axis_size("dp")
    out_pair = swap(after(d_outs[1], back[0]), 1)
    kept_mlp, sent_mlp = halve(kept_mlp, got_mlp, 2)
    d_out = add(d_outs[0], out_pair) + out_far.astype(jnp.float32)
    kept_out, sent_out = parted(d_out.reshape(count, model // count, -1), 1)
    d_qkv = attend_back(
        after(qkv, sent_out, sent_mlp),
        (d_2, d_3),
        (out_2, out_3),
        logs_far,
        image_id,
        bounds,
        heads,
        2,
        back,
    )
    kept_mlp, got_mlp = to_last(kept_mlp, sent_mlp, 2)
    d_qkv, got_out, mixed_far, mixed_0, mixed_1 = join(
        d_qkv,
        swap(sent_out, 1, "dp"),
        swap(after(mixed_far, sent_out), 2),
        swap(after(y_10, sent_out), 1),
        swap(after(y_11, sent_out), 1),
    )

    kept, sent, gain_attn_part = qkv_grads(attn_ins, d_qkv, turned_qkv)
    part_2, part_3, kept_mlp, got_mlp = join(
        *unproject(after(d_qkv, sent), turned_qkv, 2), kept_mlp, got_mlp
    )
    grad_mlp = low(add(kept_mlp, got_mlp))
    gains = jnp.concatenate(
        [gain_attn_part / gain_attn[None, :], gain_mlp_part / gain_mlp[None, :]], axis=0
    )
    gains, part_3, part_0, part_1 = join(
        gains + swap(gains, 1),
        swap(part_3, 1),
        *unproject(after(d_qkv, part_2, grad_mlp), turned_qkv, 0),
    )
    d_far = low(add(part_2, part_3))
    pair = swap(part_1, 1)
    kept_out, got_out = to_last(*halve(kept_out, got_out, 2), 2)
    got, gains, d_far, kept_out, got_out = join(
        swap(sent, 1, "dp"), sum_steps(gains, "tp", 2), d_far, kept_out, got_out
    )

    kept, sent = halve(kept, got, 2)
    far = swap(after(d_far, sent), 2)
    kept, got, gains, pair, got_mlp = join(
        *to_last(kept, sent, 2), sum_steps(gains, "grp"), pair, swap(grad_mlp, 1, "grp")
    )
    grad_rest = jnp.concatenate([low(add(kept, got)), low(add(kept_out, got_out))], axis=1)
    grad_mlp = add(grad_mlp, got_mlp)
    mixed_near = jnp.concatenate([add(y_00, mixed_0), add(y_01, mixed_1)], axis=0)
    mixed_rows = low(resid + (mixed_near + mixed_far.astype(jnp.float32)))
    got, gains, far = join(swap(grad_rest, 1, "grp"), gains + swap(gains, 1, "dp"), far)
    gains = sum_steps(gains, "dp", 2)
    input_grad = norm_back(tokens, gain_attn, part_0, pair, far, d_resid)
    grad_rest = add(grad_rest, got)
    width = w_qkv.shape[1]
    hidden = w_up.shape[1]
    return (
        mixed_rows,
        input_grad,
        gains[0],
        grad_rest[:, :width],
        grad_rest[:, width:].T,
        gains[1],
        grad_mlp[:, :hidden],
        grad_mlp[:, hidden:].T,
    )


def solution(mesh):
    in_specs = (
        P(("grp", "dp", "tp"), None),
        P(("grp", "dp")),
        P(),
        P(None, "tp"),
        P("tp", None),
        P(),
        P(None, "tp"),
        P("tp", None),
        P(("grp", "dp", "tp"), None),
    )
    out_specs = (
        P(("grp", "dp", "tp"), None),
        P(("grp", "dp", "tp"), None),
        P(),
        P("dp", "tp"),
        P("tp", "dp"),
        P(),
        P("dp", "tp"),
        P("tp", "dp"),
    )
    return jax.shard_map(
        on_device, mesh=mesh, in_specs=in_specs, out_specs=out_specs, check_vma=False
    )
```

```python
from functools import partial

import jax
import jax.numpy as jnp
from jax import lax
from jax.experimental import pallas as pl
from jax.experimental.pallas import tpu as pltpu
from jax.sharding import PartitionSpec as P

HD = 64
LANES = 128
IMAGE = 240
EXCLUDED = -1e30
MIB = 1024 * 1024
NT = (((1,), (1,)), ((), ()))
TN = (((0,), (0,)), ((), ()))

epsilon = 1e-06


def normalize(values, scaling):
    centred = values - jnp.mean(values, axis=1, keepdims=True)
    inverse = lax.rsqrt(jnp.mean(centred * centred, axis=1, keepdims=True) + epsilon)
    normed = centred * inverse
    return (normed * scaling, normed, inverse)


def restore(d_normed, normed, inverse, scaling):
    d_scaled = d_normed * scaling
    return inverse * (
        d_scaled
        - jnp.mean(d_scaled, axis=1, keepdims=True)
        - normed * jnp.mean(d_scaled * normed, axis=1, keepdims=True)
    )


def swap(value, distance, axis="tp"):
    size = lax.axis_size(axis)
    return lax.ppermute(value, axis, [(i, i ^ distance) for i in range(size)])


def after(value, *earlier):
    return lax.optimization_barrier((value, *earlier))[0]


def join(*values):
    return lax.optimization_barrier(values)


def add(left, right):
    return left.astype(jnp.float32) + right.astype(jnp.float32)


def product(left, right, dims=(((1,), (0,)), ((), ()))):
    return lax.dot_general(left, right, dims, preferred_element_type=jnp.float32)


def low(value):
    return value.astype(jnp.bfloat16)


def settings(limit, microseconds=0.1):
    return dict(
        compiler_params=pltpu.CompilerParams(vmem_limit_bytes=limit * MIB),
        cost_estimate=pl.CostEstimate(
            flops=int(microseconds * 1.1e9), bytes_accessed=MIB, transcendentals=0
        ),
    )


def whole(array):
    return pl.BlockSpec(array.shape, lambda *_: (0,) * len(array.shape))


def shape(*dims, dtype=jnp.bfloat16):
    return jax.ShapeDtypeStruct(dims, dtype)


def far_shape(*dims, dtype=jnp.bfloat16):
    return pltpu.HBM(dims, dtype)


def left(array):
    return pltpu.with_memory_space_constraint(array, pltpu.HBM)


def chosen(number, refs):
    value = refs[0][...]
    for other in range(1, len(refs)):
        value = jnp.where(number == other, refs[other][...], value)
    return value


def norm_kernel(x_ref, gain_ref, out_ref):
    out_ref[...] = low(normalize(x_ref[...].astype(jnp.float32), gain_ref[...])[0])


def norm(tokens, gain, half):
    rows, model = tokens.shape
    return pl.pallas_call(
        norm_kernel,
        grid=(1,),
        in_specs=[pl.BlockSpec((rows // 2, model), lambda i: (half, 0)), whole(gain)],
        out_specs=pl.BlockSpec((rows // 2, model), lambda i: (0, 0)),
        out_shape=far_shape(rows // 2, model),
        name="norm",
        **settings(8, 2),
    )(left(tokens), left(gain))


def norm_back_kernel(x_ref, gain_ref, own_ref, pair_ref, far_ref, d_ref, out_ref):
    d_normed = add(own_ref[...], pair_ref[...]) + far_ref[...].astype(jnp.float32)
    _, unit, inverse = normalize(x_ref[...].astype(jnp.float32), gain_ref[...])
    out_ref[...] = d_ref[...] + restore(d_normed, unit, inverse, gain_ref[...])


def norm_back(tokens, gain, own, pair, far, d_resid):
    rows, model = tokens.shape
    tile = pl.BlockSpec((rows // 4, model), lambda i: (i, 0))
    return pl.pallas_call(
        norm_back_kernel,
        grid=(4,),
        in_specs=[tile, whole(gain)] + [tile] * 4,
        out_specs=tile,
        out_shape=shape(rows, model, dtype=jnp.float32),
        name="norm_back",
        **settings(16, 2),
    )(tokens, gain, own, pair, far, d_resid)


def project_kernel(count, *refs):
    out_ref = refs[-1]
    out_ref[...] = low(product(chosen(pl.program_id(0), refs[:count]), refs[count][...], NT))


def project(blocks, weights, places, earlier):
    rows = blocks[0].shape[0]
    wide = weights.shape[0]
    count = len(blocks)
    group_rows = rows * 8 if earlier is None else earlier.shape[0]
    extra = [] if earlier is None else [earlier]
    return pl.pallas_call(
        partial(project_kernel, count),
        grid=(count,),
        in_specs=[whole(x) for x in blocks]
        + [whole(weights)]
        + [pl.BlockSpec(memory_space=pl.ANY)] * len(extra),
        out_specs=pl.BlockSpec(
            (rows, wide), lambda i: (places[0] + i * (places[-1] - places[0]) // max(count - 1, 1), 0)
        ),
        out_shape=shape(group_rows, wide),
        input_output_aliases={count + 1: 0} if extra else {},
        name="project",
        **settings(16),
    )(*blocks, weights, *extra)


def tiles_of(bounds_ref, base):
    where = 1 + 2 * base
    first, second = bounds_ref[where], bounds_ref[where + 2]
    count = bounds_ref[where + 1] - first
    total = count + bounds_ref[where + 3] - second

    def tile(number):
        late = (number >= count).astype(jnp.int32)
        key = jnp.where(late == 1, second + number - count, first + number)
        key = jnp.minimum(key, bounds_ref[where + 3] - 1 + (1 - late) * 4)
        return late, key ^ bounds_ref[0], number < total

    return tile, total


def block_at(number, width):
    return pl.ds(pl.multiple_of(number * width, width), width)


def mask_of(ids, id_q_ref, query, key, used, width):
    id_q = id_q_ref[:, block_at(query, width)] + jnp.where(used, 0, 1 << 20)
    return jnp.concatenate([ids[block_at(key, width), :]] * (width // LANES), axis=1) == id_q


TILE = 256
MOST = 40


def plan_of(place, order, rows, cells):
    group_rows = 4 * rows
    per = rows // TILE
    full = group_rows // cells
    inside = jnp.arange(per, dtype=jnp.int32) * TILE
    first = (order[:, None] * rows + inside).reshape(2, 1, 2 * per)
    first_id = jnp.minimum(first // cells, full)
    last_id = jnp.minimum((first + TILE - 1) // cells, full)
    low_key = first_id * cells // TILE
    stop = jnp.where(last_id == full, group_rows, (last_id + 1) * cells)
    turn = jnp.arange(4 * per, dtype=jnp.int32)[None, :, None]
    key = low_key + turn
    used = (key * TILE < stop).reshape(2, -1)
    key = ((key // per) ^ place) * per + key % per
    code = (key + 64 * jnp.arange(2 * per, dtype=jnp.int32)).reshape(2, -1)
    number = jnp.cumsum(used.astype(jnp.int32), axis=1)
    wanted = jnp.arange(1, MOST + 1, dtype=jnp.int32)[None, :, None]
    chosen = used[:, None, :] & (number[:, None, :] == wanted)
    listed = jnp.sum(jnp.where(chosen, code[:, None, :], 0), axis=2)
    return jnp.concatenate([number[:, -1:], listed], axis=1)


def tile_of(plan_ref, base, number):
    code = plan_ref[base // 2, 1 + number]
    return code // 64, code % 64, number < plan_ref[base // 2, 0]


def tile_at(number):
    return pl.ds(pl.multiple_of(number * TILE, TILE), TILE)


def tile_mask(ids, id_q_ref, query, key, used):
    id_q = id_q_ref[:, tile_at(query)] + jnp.where(used, 0, 1 << 20)
    return jnp.concatenate([ids[tile_at(key), :]] * (TILE // LANES), axis=1) == id_q


def in_turn(total, prepare, absorb):
    for number in range(2):
        prepare(number, 0, number)

    def step(number, carry):
        for side in range(2):
            for part in range(2):
                prepare(4 * number + 2 * side + 2 + part, 1 - side, part)
            for part in range(2):
                absorb(4 * number + 2 * side + part, side, part)
        return carry

    lax.fori_loop(0, (total + 3) // 4, step, 0)


def attend_kernel(heads, base, plan_ref, q_ref, k_ref, v_ref, id_q_ref, id_k_ref, *refs):
    out_refs = refs[:2]
    log_ref, turned, ids, scores_a, scores_b, tops, totals = refs[2:]
    scores_refs = (scores_a, scores_b)
    width = q_ref.shape[0] // 2
    for h in range(heads):
        value = v_ref[:, h * LANES : (h + 1) * LANES].astype(jnp.float32).T
        turned[h, :HD] = low(value[:HD])
        turned[h, HD:] = jnp.ones((turned.shape[1] - HD, v_ref.shape[0]), jnp.bfloat16)
    ids[...] = jnp.broadcast_to(id_k_ref[...], ids.shape)
    tops[...] = jnp.full(tops.shape, EXCLUDED, jnp.float32)
    totals[...] = jnp.zeros_like(totals)

    def prepare(number, side, part):
        query, key, _ = tile_of(plan_ref, base, number)
        for h in range(heads):
            columns = slice(h * LANES, (h + 1) * LANES)
            scores_refs[side][part, h] = product(
                k_ref[tile_at(key), columns], q_ref[tile_at(query), columns], NT
            )

    def absorb(number, side, part):
        query, key, used = tile_of(plan_ref, base, number)
        mask = tile_mask(ids, id_q_ref, query, key, used)
        for h in range(heads):
            scores = jnp.where(mask, scores_refs[side][part, h], EXCLUDED)
            largest = tops[query, h]
            top = jnp.maximum(largest, jnp.max(scores, axis=0, keepdims=True))
            exponent = low(jnp.exp(scores - top))
            tops[query, h] = top
            totals[query, h] = totals[query, h] * jnp.exp(largest - top) + product(
                turned[h, :, tile_at(key)], exponent
            )

    in_turn(plan_ref[base // 2, 0], prepare, absorb)
    for query in range(tops.shape[0]):
        block, at = divmod(query * TILE, width)
        for h in range(heads):
            sums = totals[query, h]
            denominator = sums[HD : HD + 1]
            out_refs[block][at : at + TILE, h * HD : (h + 1) * HD] = low(
                (sums[:HD] / denominator).T
            )
            log_ref[h : h + 1, query * TILE : (query + 1) * TILE] = tops[query, h] + jnp.log(
                denominator
            )


def attend(qkv, image_id, plan, heads, base):
    rows = qkv.shape[0]
    wide = heads * LANES
    width = rows // 4
    out = far_shape(width, heads * HD)
    log = far_shape(heads, 2 * width, dtype=jnp.float32)
    return pl.pallas_call(
        partial(attend_kernel, heads, base),
        grid_spec=pltpu.PrefetchScalarGridSpec(
            num_scalar_prefetch=1,
            grid=(1,),
            in_specs=[
                pl.BlockSpec((2 * width, wide), lambda i, _: (base // 2, 0)),
                pl.BlockSpec((rows, wide), lambda i, _: (0, 1)),
                pl.BlockSpec((rows, wide), lambda i, _: (0, 2)),
                pl.BlockSpec((1, 2 * width), lambda i, _: (0, base // 2)),
                pl.BlockSpec((rows, 1), lambda i, _: (0, 0)),
            ],
            out_specs=[whole(out), whole(out), whole(log)],
            scratch_shapes=[
                pltpu.VMEM((heads, HD + 16, rows), jnp.bfloat16),
                pltpu.VMEM((rows, LANES), jnp.int32),
                pltpu.VMEM((2, heads, TILE, TILE), jnp.float32),
                pltpu.VMEM((2, heads, TILE, TILE), jnp.float32),
                pltpu.VMEM((2 * width // TILE, heads, 1, TILE), jnp.float32),
                pltpu.VMEM((2 * width // TILE, heads, HD + 16, TILE), jnp.float32),
            ],
        ),
        out_shape=[out, out, log],
        name="attend",
        **settings(32, 14 if base else 3),
    )(plan, *[qkv] * 3, image_id[None, :], image_id[:, None])


def attend_back_kernel(heads, base, bounds_ref, q_ref, k_ref, v_ref, *refs):
    grad_refs = refs[0:2]
    out_refs = refs[2:4]
    log_ref, id_q_ref, id_k_ref = refs[4:7]
    if base == 0:
        d_q_ref, sums = refs[7:9]
    else:
        near_q_ref, near_sums_ref, d_ref = refs[7:10]
        sums = refs[-1]
    first = 9 if base == 0 else 10
    turned, ids, grads, placed, inner, d_q = refs[first : first + 6]
    width = q_ref.shape[0] // 2
    tile, total = tiles_of(bounds_ref, base)
    for h in range(heads):
        key = k_ref[:, h * LANES : (h + 1) * LANES].astype(jnp.float32).T
        turned[h] = low(key[:HD])
    ids[...] = jnp.broadcast_to(id_k_ref[...], ids.shape)
    d_q[...] = jnp.zeros_like(d_q)
    if base == 0:
        sums[...] = jnp.zeros_like(sums)
    else:
        sums[...] = near_sums_ref[...]
    ones = jnp.ones((8, HD), jnp.float32)
    none = jnp.zeros((width, HD), jnp.bfloat16)
    for query in range(2):
        for h in range(heads):
            grad = grad_refs[query][:, h * HD : (h + 1) * HD]
            grads[query, h] = jnp.concatenate([grad, none], axis=1)
            placed[query, h] = jnp.concatenate([none, grad], axis=1)
            terms = grad.astype(jnp.float32) * out_refs[query][
                :, h * HD : (h + 1) * HD
            ].astype(jnp.float32)
            inner[query, h] = lax.dot_general(
                ones,
                terms,
                NT,
                precision=lax.Precision.HIGHEST,
                preferred_element_type=jnp.float32,
            )[:1]

    def absorb(number):
        query, key, used = tile(number)
        at = block_at(key, width)
        mask = mask_of(ids, id_q_ref, query, key, used, width)
        for h in range(heads):
            columns = slice(h * LANES, (h + 1) * LANES)
            logs = log_ref[h : h + 1, block_at(query, width)]
            queries = q_ref[block_at(query, width), columns]
            scores = product(k_ref[at, columns], queries, NT)
            d_probs = product(v_ref[at, columns], grads[query, h], NT)
            probs = jnp.where(mask, jnp.exp(scores - logs), 0.0)
            d_scores = low(probs * (d_probs - inner[query, h]))
            sums[at, columns] += product(low(probs), placed[query, h]) + product(d_scores, queries)
            d_q[query, h] += product(turned[h, :, at], d_scores)

    def step(number, carry):
        absorb(number)
        return carry

    lax.fori_loop(0, total, step, 0)
    for query in range(2):
        for h in range(heads):
            part = low((d_q[query, h] * 0.125).T)
            if base == 0:
                d_q_ref[query * width : (query + 1) * width, h * HD : (h + 1) * HD] = part
            else:
                here = slice((base + query) * width, (base + query + 1) * width)
                d_ref[here, 3 * h * HD : (3 * h + 1) * HD] = part
    if base:
        for h in range(heads):
            d_ref[: 2 * width, 3 * h * HD : (3 * h + 1) * HD] = near_q_ref[
                :, h * HD : (h + 1) * HD
            ]
            d_ref[:, (3 * h + 1) * HD : (3 * h + 3) * HD] = low(
                sums[:, h * LANES : (h + 1) * LANES]
            )


def attend_back(qkv, d_heads, heads_out, log_total, image_id, bounds, heads, base, near):
    rows = qkv.shape[0]
    wide = heads * LANES
    width = rows // 4
    sums = far_shape(rows, wide, dtype=jnp.float32)
    near = list(near)
    if base == 0:
        outs = [far_shape(2 * width, heads * HD), sums]
    else:
        outs = [shape(rows, 3 * heads * HD)]
    padded = pltpu.VMEM((2, heads, width, LANES), jnp.bfloat16)
    result = pl.pallas_call(
        partial(attend_back_kernel, heads, base),
        grid_spec=pltpu.PrefetchScalarGridSpec(
            num_scalar_prefetch=1,
            grid=(1,),
            in_specs=[
                pl.BlockSpec((2 * width, wide), lambda i, _: (base // 2, 0)),
                pl.BlockSpec((rows, wide), lambda i, _: (0, 1)),
                pl.BlockSpec((rows, wide), lambda i, _: (0, 2)),
            ]
            + [whole(a) for a in (*d_heads, *heads_out, log_total)]
            + [
                pl.BlockSpec((1, 2 * width), lambda i, _: (0, base // 2)),
                pl.BlockSpec((rows, 1), lambda i, _: (0, 0)),
            ]
            + [whole(a) for a in near],
            out_specs=[whole(a) for a in outs],
            scratch_shapes=[
                pltpu.VMEM((heads, HD, rows), jnp.bfloat16),
                pltpu.VMEM((rows, LANES), jnp.int32),
                padded,
                padded,
                pltpu.VMEM((2, heads, 1, width), jnp.float32),
                pltpu.VMEM((2, heads, HD, width), jnp.float32),
            ]
            + ([pltpu.VMEM(sums.shape, jnp.float32)] if near else []),
        ),
        out_shape=outs,
        name="attend_back",
        **settings(36, 20 if base else 3),
    )(
        bounds,
        *[left(qkv)] * 3,
        *d_heads,
        *heads_out,
        log_total,
        image_id[None, :],
        image_id[:, None],
        *(left(a) for a in near),
    )
    return result[0] if near else result


def last_rows(refs, number):
    size = refs[number].shape[0]
    return refs[number][size - refs[0].shape[0] :, :]


def branch_kernel(*refs):
    parts = refs[0:4]
    weights = refs[4:8]
    tokens_ref, gain_ref, resid_ref, in_0_ref, in_1_ref = refs[8:]
    resid = tokens_ref[...].astype(jnp.float32)
    branch = product(parts[0][...], last_rows(weights, 0))
    for j in range(1, 4):
        branch = branch + product(parts[j][...], last_rows(weights, j))
    resid = resid + branch
    resid_ref[...] = resid
    normed = low(normalize(resid, gain_ref[...])[0])
    for half, in_ref in enumerate((in_0_ref, in_1_ref)):

        @pl.when(pl.program_id(0) == half)
        def _():
            in_ref[...] = normed


def branch(parts, weights, tokens, gain):
    rows, model = tokens.shape
    operands = (*parts, *weights, tokens, gain)
    half = far_shape(rows // 2, model)
    resid = far_shape(rows, model, dtype=jnp.float32)

    def halves(array):
        return pl.BlockSpec((rows // 2, array.shape[1]), lambda i: (i, 0))

    specs = [whole(a) for a in operands]
    specs[:4] = [halves(p) for p in parts]
    specs[8] = halves(tokens)
    return pl.pallas_call(
        branch_kernel,
        grid=(2,),
        in_specs=specs,
        out_specs=[halves(resid), whole(half), whole(half)],
        out_shape=[resid, half, half],
        name="branch",
        **settings(16),
    )(left(parts[0]), *operands[1:])


def mlp_kernel(together, x_a_ref, x_b_ref, g_a_ref, g_b_ref, up_ref, down_ref, *refs):
    act_ref, d_pre_ref = refs[-2:]
    length = x_a_ref.shape[0]
    if together:
        m_a_ref, y_a_ref, both_ref = refs[-5:-2]
        m_b_ref, y_b_ref = both_ref.at[:length], both_ref.at[length:]
    else:
        m_a_ref, y_a_ref, m_b_ref, y_b_ref = refs[-6:-2]

    number = pl.program_id(0)
    mlp_in = chosen(number, (x_b_ref, x_a_ref))
    out_grads = chosen(number, (g_b_ref, g_a_ref))
    pre_act = product(mlp_in, up_ref[...])
    d_act = product(out_grads, down_ref[...], NT)
    below = 0.5 + 0.5 * lax.erf(pre_act * 0.7071067811865476)
    density = 0.3989422804014327 * jnp.exp(-0.5 * pre_act * pre_act)
    d_pre = low(d_act * (below + pre_act * density))
    act = low(pre_act * below)
    m = low(product(d_pre, up_ref[...], NT))
    y = low(product(act, down_ref[...]))
    act_ref[...] = act
    d_pre_ref[...] = d_pre
    for block, (m_ref, y_ref) in enumerate(((m_b_ref, y_b_ref), (m_a_ref, y_a_ref))):

        @pl.when(number == block)
        def _():
            m_ref[...] = m
            y_ref[...] = y


def mlp(x_a, x_b, g_a, g_b, half, place, w_up, w_down, earlier, near):
    length, model = x_a.shape
    hidden = w_up.shape[1]
    extra = [] if earlier is None else list(earlier)

    def grads():
        return pl.BlockSpec((length, model), lambda i: (half, 0))

    def kept(width):
        return pl.BlockSpec((length, width), lambda i: (2 * place + 1 - i, 0))

    one = far_shape(length, model)
    outs = [one, one, far_shape(2 * length, model)] if near else [one] * 4
    return pl.pallas_call(
        partial(mlp_kernel, near),
        grid=(2,),
        in_specs=[whole(x_a), whole(x_b), grads(), grads(), whole(w_up), whole(w_down)]
        + [pl.BlockSpec(memory_space=pl.ANY)] * len(extra),
        out_specs=[whole(a) for a in outs] + [kept(hidden)] * 2,
        out_shape=outs
        + [far_shape(4 * length, hidden)] * 2,
        input_output_aliases={6 + i: len(outs) + i for i in range(len(extra))},
        name="mlp",
        **settings(20),
    )(x_a, x_b, g_a, g_b, w_up, w_down, *extra)


def part_rows(count, bit, totals, kept_ref, sent_ref):
    share = totals[0].shape[0] // count
    for pair in range(count // 2):
        for side, ref in ((bit, kept_ref), (1 - bit, sent_ref)):
            at = pl.ds(pl.multiple_of((2 * pair + side) * share, 8), share)
            first = 0
            for total in totals:
                width = min(total.shape[1], ref.shape[2] - first)
                ref[pair, :, first : first + width] = total[at, :width].astype(ref.dtype)
                first += width


def row_sums(values):
    sums = jnp.sum(values, axis=1, keepdims=True)
    return jnp.broadcast_to(sums, (values.shape[0], LANES)).T[:1]


def mlp_grads_kernel(count, bit_ref, act_ref, d_pre_ref, *refs):
    number = pl.program_id(0)
    x_refs, g_refs = refs[0:4], refs[4:8]
    if count:
        up_ref, old_up_ref, old_down_ref, kept_ref, sent_ref, gain_ref, d_up, d_down = refs[8:]
    else:
        d_up, d_down = refs[8:]

    @pl.when(number == 0)
    def _():
        if count:
            d_up[...] = old_up_ref[...]
            d_down[...] = old_down_ref[...]
        else:
            d_up[...] = jnp.zeros_like(d_up)
            d_down[...] = jnp.zeros_like(d_down)

    x = jnp.concatenate([chosen(number, x_refs[j::2]) for j in range(2)], axis=0)
    d_up[...] += product(x, d_pre_ref[...], TN)
    grads = jnp.concatenate([chosen(number, g_refs[j::2]) for j in range(2)], axis=0)
    d_down[...] += product(grads, act_ref[...], TN)

    @pl.when(number == 1)
    def _():
        if count:
            part_rows(count, bit_ref[0], (d_up, d_down), kept_ref, sent_ref)
            gain_ref[...] = row_sums(d_up[...] * up_ref[...].astype(jnp.float32))


def mlp_grads(act, d_pre, blocks, grads, w_up, earlier):
    rows, hidden = act.shape
    model = blocks[0].shape[1]
    tile = rows // 4
    count = lax.axis_size("dp")
    bit = lax.axis_index("dp") % 2
    total = shape(model, hidden, dtype=jnp.float32)
    kept = far_shape(count // 2, model // count, 2 * hidden, dtype=jnp.float32)
    sent = far_shape(*kept.shape)
    gain = shape(1, model, dtype=jnp.float32)
    extra = [] if earlier is None else [w_up, *earlier]
    outs = [kept, sent, gain] if extra else [total, total]

    def half(rows, columns):
        return pl.BlockSpec((rows, columns), lambda i, _: (i, 0))

    return pl.pallas_call(
        partial(mlp_grads_kernel, count if extra else 0),
        grid_spec=pltpu.PrefetchScalarGridSpec(
            num_scalar_prefetch=1,
            grid=(2,),
            in_specs=[half(2 * tile, hidden)] * 2
            + [whole(a) for a in blocks]
            + [
                pl.BlockSpec((tile, model), lambda i, _, at=at: (at, 0)) for at, _ in grads
            ]
            + [whole(a) for a in extra],
            out_specs=[whole(a) for a in outs],
            scratch_shapes=[pltpu.VMEM((model, hidden), jnp.float32)] * 2 if extra else [],
        ),
        out_shape=outs,
        name="mlp_grads",
        **settings(40),
    )(bit[None], *(left(a) for a in (act, d_pre, *blocks, *(g for _, g in grads))), *extra)


def branch_back_kernel(*refs):
    cotangent_ref, resid_ref, gain_ref = refs[6:9]
    weights = refs[9:13]
    d_resid_ref, d_branch_ref = refs[13:15]
    out_refs = refs[15:19]
    own, pair, far = (chosen(pl.program_id(0), refs[j : j + 2]) for j in (0, 2, 4))
    d_mlp_in = add(own, pair) + far.astype(jnp.float32)
    _, unit, inverse = normalize(resid_ref[...], gain_ref[...])
    d_resid = cotangent_ref[...].astype(jnp.float32) + restore(
        d_mlp_in, unit, inverse, gain_ref[...]
    )
    d_resid_ref[...] = d_resid
    d_branch = low(d_resid)
    d_branch_ref[...] = d_branch
    for j in range(4):
        out_refs[j][...] = low(product(d_branch, last_rows(weights, j), NT))


def branch_back(own, pair, far, cotangent, resid, gain, weights):
    rows, model = resid.shape
    width = weights[0].shape[0]

    def at(columns):
        return pl.BlockSpec((rows // 2, columns), lambda i: (i, 0))

    operands = (*own, *pair, *far, cotangent, resid, gain, *weights)
    specs = [whole(a) for a in operands]
    specs[2] = specs[3] = pl.BlockSpec((rows // 2, model), lambda i: (0, 0))
    specs[6] = specs[7] = at(model)
    return pl.pallas_call(
        branch_back_kernel,
        grid=(2,),
        in_specs=specs,
        out_specs=[at(model), at(model)] + [at(width)] * 4,
        out_shape=[far_shape(rows, model, dtype=jnp.float32), shape(rows, model)]
        + [far_shape(rows, width)] * 4,
        name="branch_back",
        **settings(16),
    )(*(left(a) for a in operands[:9]), *operands[9:])


def out_grads_kernel(d_ref, *refs):
    for j in range(4):
        refs[4 + j][...] = low(product(d_ref[...], refs[j][...], TN))


def out_weight_grads(d_branch, parts):
    model = d_branch.shape[1]
    out = far_shape(model, parts[0].shape[1])
    return pl.pallas_call(
        out_grads_kernel,
        in_specs=[whole(a) for a in (d_branch, *parts)],
        out_specs=[whole(out)] * 4,
        out_shape=[out] * 4,
        name="out_weight_grads",
        **settings(16),
    )(d_branch, *parts)


def qkv_grads_kernel(count, bit_ref, *refs):
    x_refs = refs[0:8]
    d_ref, w_ref, kept_ref, sent_ref, gain_ref, total = refs[8:]
    number = pl.program_id(0)
    block = jnp.concatenate([chosen(number, x_refs[j::2]) for j in range(2)], axis=0)
    part = product(block, d_ref[...], TN)

    @pl.when(number == 0)
    def _():
        total[...] = part

    @pl.when(number > 0)
    def _():
        total[...] += part

    @pl.when(number == 3)
    def _():
        part_rows(count, bit_ref[0], (total,), kept_ref, sent_ref)
        gain_ref[...] = row_sums(total[...] * w_ref[...].astype(jnp.float32).T)


def qkv_grads(attn_ins, d_qkv, w_qkv):
    rows, model = attn_ins[0].shape
    width = d_qkv.shape[1]
    count = lax.axis_size("dp")
    bit = lax.axis_index("dp") % 2
    kept = far_shape(count // 2, model // count, width, dtype=jnp.float32)
    sent = far_shape(*kept.shape)
    gain = shape(1, model, dtype=jnp.float32)
    return pl.pallas_call(
        partial(qkv_grads_kernel, count),
        grid_spec=pltpu.PrefetchScalarGridSpec(
            num_scalar_prefetch=1,
            grid=(4,),
            in_specs=[whole(x) for x in attn_ins]
            + [pl.BlockSpec((2 * rows, width), lambda i, _: (i, 0)), whole(w_qkv)],
            out_specs=[whole(kept), whole(sent), whole(gain)],
            scratch_shapes=[pltpu.VMEM((model, width), jnp.float32)],
        ),
        out_shape=[kept, sent, gain],
        name="qkv_grads",
        **settings(24),
    )(bit[None], *attn_ins, d_qkv, w_qkv)


def unproject_kernel(d_ref, w_ref, *out_refs):
    part = low(product(d_ref[...], w_ref[...]))
    for number in range(2):

        @pl.when(pl.program_id(0) == number)
        def _():
            out_refs[number][...] = part


def unproject(d_qkv, w_qkv, base):
    rows = d_qkv.shape[0] // 4
    out = far_shape(rows, w_qkv.shape[1])
    return pl.pallas_call(
        unproject_kernel,
        grid=(2,),
        in_specs=[
            pl.BlockSpec((rows, d_qkv.shape[1]), lambda i: (base + i, 0)),
            whole(w_qkv),
        ],
        out_specs=[whole(out), whole(out)],
        out_shape=[out, out],
        name="unproject",
        **settings(16),
    )(d_qkv, w_qkv)


def parted(total, distance):
    bit = (lax.axis_index("dp") // distance) % 2
    total = total.reshape(-1, 2, *total.shape[1:])
    return (
        lax.dynamic_index_in_dim(total, bit, 1, keepdims=False),
        low(lax.dynamic_index_in_dim(total, 1 - bit, 1, keepdims=False)),
    )


def halve(kept, got, distance):
    bit = (lax.axis_index("dp") // distance) % 2
    kept = kept.reshape(-1, 2, *kept.shape[1:])
    got = got.reshape(kept.shape)

    def side(number):
        return add(
            lax.dynamic_index_in_dim(kept, number, 1, keepdims=False),
            lax.dynamic_index_in_dim(got, number, 1, keepdims=False),
        )

    return side(bit), low(side(1 - bit))


def to_last(kept, sent, distance):
    while True:
        got = swap(sent, distance, "dp")
        distance *= 2
        if distance >= lax.axis_size("dp"):
            return kept[0], got[0]
        kept, sent = halve(kept, got, distance)


def sum_steps(value, axis, first=1):
    distance = first
    while distance < lax.axis_size(axis):
        value = value + swap(value, distance, axis)
        distance *= 2
    return value


def on_device(tokens, patch_side, gain_attn, w_qkv, w_out, gain_mlp, w_up, w_down, cotangent):
    rows, model = tokens.shape
    place = lax.axis_index("tp")
    group_rows = 4 * rows
    heads = w_out.shape[0] // HD

    own_0 = norm(tokens, gain_attn, 0)
    own_1 = norm(after(tokens, own_0), gain_attn, 1)
    across_0, across_1 = swap(own_0, 2), swap(own_1, 2)
    pair_0, pair_1 = swap(own_0, 1), swap(own_1, 1)

    cells = (IMAGE // patch_side[0]) ** 2
    full = group_rows // cells
    order = place ^ jnp.arange(4, dtype=jnp.int32)
    positions = (order[:, None] * rows + jnp.arange(rows, dtype=jnp.int32)).reshape(-1)
    image_id = jnp.minimum(positions // cells, full)
    first_id = jnp.minimum(order * rows // cells, full)
    last_id = jnp.minimum((order * rows + rows - 1) // cells, full)
    first_block = first_id * cells // rows
    stop = jnp.where(last_id == full, group_rows, (last_id + 1) * cells)
    last_block = (stop + rows - 1) // rows
    plan = plan_of(place, order, rows, cells)
    bounds = jnp.concatenate(
        [place[None], jnp.stack([first_block, last_block], axis=1).reshape(-1)]
    )

    turned_qkv = w_qkv.T
    by_head = turned_qkv.reshape(heads, 3, HD, model)
    by_head = by_head * jnp.array([0.125, 1.0, 1.0], jnp.bfloat16)[:, None, None]
    spread = jnp.pad(by_head.transpose(1, 0, 2, 3), ((0, 0), (0, 0), (0, LANES - HD), (0, 0)))
    spread = spread.reshape(3 * heads * LANES, model)
    qkv = project([own_0, own_1, pair_0, pair_1], spread, (0, 1, 2, 3), None)
    across_0, qkv = join(across_0, qkv)
    diagonal_0 = swap(across_0, 1)
    qkv = project([across_0, diagonal_0], spread, (4, 6), qkv)
    across_1, qkv = join(across_1, qkv)
    diagonal_1 = swap(across_1, 1)
    qkv = project([across_1], spread, (5,), qkv)
    diagonal_1, qkv = join(diagonal_1, qkv)
    qkv = project([diagonal_1], spread, (7,), qkv)
    attn_ins = [own_0, own_1, pair_0, pair_1, across_0, across_1, diagonal_0, diagonal_1]

    middle = rows // 2
    w_pair = swap(after(w_out, across_1), 1)
    grads_pair = swap(after(cotangent, across_1), 1)
    mixed_in = jnp.concatenate([cotangent[:middle], w_out], axis=0)
    in_across = swap(after(mixed_in, across_1), 2)
    far = attend(qkv, image_id, plan, heads, 2)
    *far, w_pair, grads_pair, in_across = join(*far, w_pair, grads_pair, in_across)
    out_2, out_3, logs_far = far
    got_2, got_3 = swap(out_2, 2), swap(out_3, 3)
    in_diagonal = swap(in_across, 1)
    grads_1 = swap(after(cotangent[middle:], out_2), 2)
    near = attend(after(qkv, out_2), image_id, plan, heads, 0)
    *near, got_2, got_3, in_diagonal = join(*near, got_2, got_3, in_diagonal)
    out_0, out_1, logs_near = near
    got_1 = swap(out_1, 1)
    mine = [out_0, got_1, got_2, got_3]
    w_outs = [w_out, w_pair, in_across, in_diagonal]
    resid, *mlp_in = branch(mine, w_outs, tokens, gain_mlp)
    mlp_in[0], grads_1 = join(mlp_in[0], grads_1)
    grads_1_diagonal = swap(grads_1, 1)

    pairs = [swap(m, 1) for m in mlp_in]
    across_0 = swap(mlp_in[0], 2)
    own_0, y_0, pair_0, *near = mlp(
        mlp_in[0], pairs[0], cotangent, grads_pair, 0, 0, w_up, w_down, None, True
    )
    own_1, y_1, pair_1, *near = mlp(
        mlp_in[1], pairs[1], cotangent, grads_pair, 1, 1, w_up, w_down, near, True
    )
    across_0, own_1, pair_0, pair_1, grads_1_diagonal = join(
        across_0, own_1, pair_0, pair_1, grads_1_diagonal
    )
    across_1 = swap(after(mlp_in[1], across_0), 2)
    diagonal_0, pair_0, pair_1 = join(swap(across_0, 1), swap(pair_0, 1), swap(pair_1, 1))
    m_2, y_20, m_3, y_30, *kept = mlp(
        across_0, diagonal_0, in_across, in_diagonal, 0, 0, w_up, w_down, None, False
    )
    across_1, m_2, y_30 = join(across_1, m_2, swap(y_30, 1))
    far_0 = low(add(m_2, swap(m_3, 1)))
    diagonal_1 = swap(across_1, 1)
    m_2, y_21, m_3, y_31, *kept = mlp(
        across_1, diagonal_1, grads_1, grads_1_diagonal, 0, 1, w_up, w_down, kept, False
    )
    sums = mlp_grads(
        after(near[0], m_2),
        near[1],
        (mlp_in[0], pairs[0], mlp_in[1], pairs[1]),
        ((0, cotangent), (0, grads_pair), (1, cotangent), (1, grads_pair)),
        w_up,
        None,
    )
    far_0, m_2, y_31, *sums = join(swap(far_0, 2), m_2, swap(y_31, 1), *sums)
    far_1 = low(add(m_2, swap(m_3, 1)))
    kept_mlp, sent_mlp, gain_mlp_part = mlp_grads(
        after(kept[0], far_1),
        kept[1],
        (across_0, diagonal_0, across_1, diagonal_1),
        ((0, in_across), (0, in_diagonal), (0, grads_1), (0, grads_1_diagonal)),
        w_up,
        sums,
    )
    mixed_far = [low(add(after(y_20, sent_mlp), y_30)), low(add(after(y_21, sent_mlp), y_31))]
    mixed_far, kept_mlp, sent_mlp, far_1 = join(
        jnp.concatenate(mixed_far, axis=0), kept_mlp, sent_mlp, swap(far_1, 2)
    )

    d_resid, d_branch, *d_pieces = branch_back(
        (own_0, own_1), (pair_0, pair_1), (far_0, far_1), cotangent, resid, gain_mlp, w_outs
    )
    d_1, d_2, d_3 = [swap(d_pieces[j], j) for j in range(1, 4)]
    d_outs = out_weight_grads(after(d_branch, d_pieces[0]), mine)
    out_far = low(add(d_outs[2], swap(d_outs[3], 1)))
    back = attend_back(
        after(qkv, out_far),
        (d_pieces[0], d_1),
        (out_0, out_1),
        logs_near,
        image_id,
        bounds,
        heads,
        0,
        (),
    )
    *back, got_mlp, d_2, d_3, out_far = join(
        *back, swap(sent_mlp, 1, "dp"), d_2, d_3, swap(out_far, 2)
    )
    count = lax.axis_size("dp")
    out_pair = swap(after(d_outs[1], back[0]), 1)
    kept_mlp, sent_mlp = halve(kept_mlp, got_mlp, 2)
    d_out = add(d_outs[0], out_pair) + out_far.astype(jnp.float32)
    kept_out, sent_out = parted(d_out.reshape(count, model // count, -1), 1)
    d_qkv = attend_back(
        after(qkv, sent_out, sent_mlp),
        (d_2, d_3),
        (out_2, out_3),
        logs_far,
        image_id,
        bounds,
        heads,
        2,
        back,
    )
    kept_mlp, got_mlp = to_last(kept_mlp, sent_mlp, 2)
    d_qkv, got_out, mixed_far = join(
        d_qkv, swap(sent_out, 1, "dp"), swap(after(mixed_far, sent_out), 2)
    )

    kept, sent, gain_attn_part = qkv_grads(attn_ins, d_qkv, turned_qkv)
    part_2, part_3, kept_mlp, got_mlp = join(
        *unproject(after(d_qkv, sent), turned_qkv, 2), kept_mlp, got_mlp
    )
    grad_mlp = low(add(kept_mlp, got_mlp))
    gains = jnp.concatenate(
        [gain_attn_part / gain_attn[None, :], gain_mlp_part / gain_mlp[None, :]], axis=0
    )
    gains, part_3, part_0, part_1 = join(
        gains + swap(gains, 1),
        swap(part_3, 1),
        *unproject(after(d_qkv, part_2, grad_mlp), turned_qkv, 0),
    )
    d_far = low(add(part_2, part_3))
    pair = swap(part_1, 1)
    kept_out, got_out = to_last(*halve(kept_out, got_out, 2), 2)
    gains = sum_steps(gains, "tp", 2)
    d_far = after(d_far, gains)
    got, gains, kept_out, got_out = join(swap(sent, 1, "dp"), gains, kept_out, got_out)

    kept, sent = halve(kept, got, 2)
    far = swap(d_far, 2)
    kept, got, gains, pair, got_mlp = join(
        *to_last(kept, sent, 2), sum_steps(gains, "grp"), pair, swap(grad_mlp, 1, "grp")
    )
    grad_rest = jnp.concatenate([low(add(kept, got)), low(add(kept_out, got_out))], axis=1)
    grad_mlp = add(grad_mlp, got_mlp)
    mixed_near = jnp.concatenate(
        [add(y_0, pair_0[middle:]), add(y_1, pair_1[middle:])], axis=0
    )
    mixed_rows = low(resid + (mixed_near + mixed_far.astype(jnp.float32)))
    got, gains, far = join(swap(grad_rest, 1, "grp"), gains + swap(gains, 1, "dp"), far)
    gains = sum_steps(gains, "dp", 2)
    input_grad = norm_back(tokens, gain_attn, part_0, pair, far, d_resid)
    grad_rest = add(grad_rest, got)
    width = w_qkv.shape[1]
    hidden = w_up.shape[1]
    return (
        mixed_rows,
        input_grad,
        gains[0],
        grad_rest[:, :width],
        grad_rest[:, width:].T,
        gains[1],
        grad_mlp[:, :hidden],
        grad_mlp[:, hidden:].T,
    )


def solution(mesh):
    in_specs = (
        P(("grp", "dp", "tp"), None),
        P(("grp", "dp")),
        P(),
        P(None, "tp"),
        P("tp", None),
        P(),
        P(None, "tp"),
        P("tp", None),
        P(("grp", "dp", "tp"), None),
    )
    out_specs = (
        P(("grp", "dp", "tp"), None),
        P(("grp", "dp", "tp"), None),
        P(),
        P("dp", "tp"),
        P("tp", "dp"),
        P(),
        P("dp", "tp"),
        P("tp", "dp"),
    )
    return jax.shard_map(
        on_device, mesh=mesh, in_specs=in_specs, out_specs=out_specs, check_vma=False
    )
```

```python
from functools import partial

import jax
import jax.numpy as jnp
from jax import lax
from jax.experimental import pallas as pl
from jax.experimental.pallas import tpu as pltpu
from jax.sharding import PartitionSpec as P

HD = 64
LANES = 128
IMAGE = 240
EXCLUDED = -1e30
MIB = 1024 * 1024
NT = (((1,), (1,)), ((), ()))
TN = (((0,), (0,)), ((), ()))

epsilon = 1e-06


def normalize(values, scaling):
    centred = values - jnp.mean(values, axis=1, keepdims=True)
    inverse = lax.rsqrt(jnp.mean(centred * centred, axis=1, keepdims=True) + epsilon)
    normed = centred * inverse
    return (normed * scaling, normed, inverse)


def restore(d_normed, normed, inverse, scaling):
    d_scaled = d_normed * scaling
    return inverse * (
        d_scaled
        - jnp.mean(d_scaled, axis=1, keepdims=True)
        - normed * jnp.mean(d_scaled * normed, axis=1, keepdims=True)
    )


def swap(value, distance, axis="tp"):
    size = lax.axis_size(axis)
    return lax.ppermute(value, axis, [(i, i ^ distance) for i in range(size)])


def after(value, *earlier):
    return lax.optimization_barrier((value, *earlier))[0]


def join(*values):
    return lax.optimization_barrier(values)


def add(left, right):
    return left.astype(jnp.float32) + right.astype(jnp.float32)


def product(left, right, dims=(((1,), (0,)), ((), ()))):
    return lax.dot_general(left, right, dims, preferred_element_type=jnp.float32)


def low(value):
    return value.astype(jnp.bfloat16)


def settings(limit, microseconds=0.1):
    return dict(
        compiler_params=pltpu.CompilerParams(vmem_limit_bytes=limit * MIB),
        cost_estimate=pl.CostEstimate(
            flops=int(microseconds * 1.1e9), bytes_accessed=MIB, transcendentals=0
        ),
    )


def whole(array):
    return pl.BlockSpec(array.shape, lambda *_: (0,) * len(array.shape))


def shape(*dims, dtype=jnp.bfloat16):
    return jax.ShapeDtypeStruct(dims, dtype)


def far_shape(*dims, dtype=jnp.bfloat16):
    return pltpu.HBM(dims, dtype)


def left(array):
    return pltpu.with_memory_space_constraint(array, pltpu.HBM)


def chosen(number, refs):
    value = refs[0][...]
    for other in range(1, len(refs)):
        value = jnp.where(number == other, refs[other][...], value)
    return value


def norm_kernel(x_ref, gain_ref, out_ref):
    out_ref[...] = low(normalize(x_ref[...].astype(jnp.float32), gain_ref[...])[0])


def norm(tokens, gain, half):
    rows, model = tokens.shape
    return pl.pallas_call(
        norm_kernel,
        grid=(1,),
        in_specs=[pl.BlockSpec((rows // 2, model), lambda i: (half, 0)), whole(gain)],
        out_specs=pl.BlockSpec((rows // 2, model), lambda i: (0, 0)),
        out_shape=far_shape(rows // 2, model),
        name="norm",
        **settings(8, 2),
    )(left(tokens), left(gain))


def norm_back_kernel(x_ref, gain_ref, own_ref, pair_ref, far_ref, d_ref, out_ref):
    d_normed = add(own_ref[...], pair_ref[...]) + far_ref[...].astype(jnp.float32)
    _, unit, inverse = normalize(x_ref[...].astype(jnp.float32), gain_ref[...])
    out_ref[...] = d_ref[...] + restore(d_normed, unit, inverse, gain_ref[...])


def norm_back(tokens, gain, own, pair, far, d_resid):
    rows, model = tokens.shape
    tile = pl.BlockSpec((rows // 4, model), lambda i: (i, 0))
    return pl.pallas_call(
        norm_back_kernel,
        grid=(4,),
        in_specs=[tile, whole(gain)] + [tile] * 4,
        out_specs=tile,
        out_shape=shape(rows, model, dtype=jnp.float32),
        name="norm_back",
        **settings(16, 2),
    )(tokens, gain, own, pair, far, d_resid)


def project_kernel(count, *refs):
    out_ref = refs[-1]
    out_ref[...] = low(product(chosen(pl.program_id(0), refs[:count]), refs[count][...], NT))


def project(blocks, weights, places, earlier):
    rows = blocks[0].shape[0]
    wide = weights.shape[0]
    count = len(blocks)
    group_rows = rows * 8 if earlier is None else earlier.shape[0]
    extra = [] if earlier is None else [earlier]
    return pl.pallas_call(
        partial(project_kernel, count),
        grid=(count,),
        in_specs=[whole(x) for x in blocks]
        + [whole(weights)]
        + [pl.BlockSpec(memory_space=pl.ANY)] * len(extra),
        out_specs=pl.BlockSpec(
            (rows, wide), lambda i: (places[0] + i * (places[-1] - places[0]) // max(count - 1, 1), 0)
        ),
        out_shape=shape(group_rows, wide),
        input_output_aliases={count + 1: 0} if extra else {},
        name="project",
        **settings(16),
    )(*blocks, weights, *extra)


def tiles_of(bounds_ref, base):
    where = 1 + 2 * base
    first, second = bounds_ref[where], bounds_ref[where + 2]
    count = bounds_ref[where + 1] - first
    total = count + bounds_ref[where + 3] - second

    def tile(number):
        late = (number >= count).astype(jnp.int32)
        key = jnp.where(late == 1, second + number - count, first + number)
        key = jnp.minimum(key, bounds_ref[where + 3] - 1 + (1 - late) * 4)
        return late, key ^ bounds_ref[0], number < total

    return tile, total


def block_at(number, width):
    return pl.ds(pl.multiple_of(number * width, width), width)


def mask_of(ids, id_q_ref, query, key, used, width):
    id_q = id_q_ref[:, block_at(query, width)] + jnp.where(used, 0, 1 << 20)
    return jnp.concatenate([ids[block_at(key, width), :]] * (width // LANES), axis=1) == id_q


TILE = 256
MOST = 40


def plan_of(place, order, rows, cells):
    group_rows = 4 * rows
    per = rows // TILE
    full = group_rows // cells
    inside = jnp.arange(per, dtype=jnp.int32) * TILE
    first = (order[:, None] * rows + inside).reshape(2, 1, 2 * per)
    first_id = jnp.minimum(first // cells, full)
    last_id = jnp.minimum((first + TILE - 1) // cells, full)
    low_key = first_id * cells // TILE
    stop = jnp.where(last_id == full, group_rows, (last_id + 1) * cells)
    turn = jnp.arange(4 * per, dtype=jnp.int32)[None, :, None]
    key = low_key + turn
    used = (key * TILE < stop).reshape(2, -1)
    key = ((key // per) ^ place) * per + key % per
    code = (key + 64 * jnp.arange(2 * per, dtype=jnp.int32)).reshape(2, -1)
    number = jnp.cumsum(used.astype(jnp.int32), axis=1)
    wanted = jnp.arange(1, MOST + 1, dtype=jnp.int32)[None, :, None]
    chosen = used[:, None, :] & (number[:, None, :] == wanted)
    listed = jnp.sum(jnp.where(chosen, code[:, None, :], 0), axis=2)
    return jnp.concatenate([number[:, -1:], listed], axis=1)


def tile_of(plan_ref, base, number):
    code = plan_ref[base // 2, 1 + number]
    return code // 64, code % 64, number < plan_ref[base // 2, 0]


def tile_at(number):
    return pl.ds(pl.multiple_of(number * TILE, TILE), TILE)


def tile_mask(ids, id_q_ref, query, key, used):
    id_q = id_q_ref[:, tile_at(query)] + jnp.where(used, 0, 1 << 20)
    return jnp.concatenate([ids[tile_at(key), :]] * (TILE // LANES), axis=1) == id_q


def in_turn(total, prepare, absorb):
    for number in range(2):
        prepare(number, 0, number)

    def step(number, carry):
        for side in range(2):
            for part in range(2):
                prepare(4 * number + 2 * side + 2 + part, 1 - side, part)
            for part in range(2):
                absorb(4 * number + 2 * side + part, side, part)
        return carry

    lax.fori_loop(0, (total + 3) // 4, step, 0)


def attend_kernel(heads, base, plan_ref, q_ref, k_ref, v_ref, id_q_ref, id_k_ref, *refs):
    out_refs = refs[:2]
    log_ref, turned, ids, scores_a, scores_b, tops, totals = refs[2:]
    scores_refs = (scores_a, scores_b)
    width = q_ref.shape[0] // 2
    for h in range(heads):
        value = v_ref[:, h * LANES : (h + 1) * LANES].astype(jnp.float32).T
        turned[h, :HD] = low(value[:HD])
        turned[h, HD:] = jnp.ones((turned.shape[1] - HD, v_ref.shape[0]), jnp.bfloat16)
    ids[...] = jnp.broadcast_to(id_k_ref[...], ids.shape)
    tops[...] = jnp.full(tops.shape, EXCLUDED, jnp.float32)
    totals[...] = jnp.zeros_like(totals)

    def prepare(number, side, part):
        query, key, _ = tile_of(plan_ref, base, number)
        for h in range(heads):
            columns = slice(h * LANES, (h + 1) * LANES)
            scores_refs[side][part, h] = product(
                k_ref[tile_at(key), columns], q_ref[tile_at(query), columns], NT
            )

    def absorb(number, side, part):
        query, key, used = tile_of(plan_ref, base, number)
        mask = tile_mask(ids, id_q_ref, query, key, used)
        for h in range(heads):
            scores = jnp.where(mask, scores_refs[side][part, h], EXCLUDED)
            largest = tops[query, h]
            top = jnp.maximum(largest, jnp.max(scores, axis=0, keepdims=True))
            exponent = low(jnp.exp(scores - top))
            tops[query, h] = top
            totals[query, h] = totals[query, h] * jnp.exp(largest - top) + product(
                turned[h, :, tile_at(key)], exponent
            )

    in_turn(plan_ref[base // 2, 0], prepare, absorb)
    for query in range(tops.shape[0]):
        block, at = divmod(query * TILE, width)
        for h in range(heads):
            sums = totals[query, h]
            denominator = sums[HD : HD + 1]
            out_refs[block][at : at + TILE, h * HD : (h + 1) * HD] = low(
                (sums[:HD] / denominator).T
            )
            log_ref[h : h + 1, query * TILE : (query + 1) * TILE] = tops[query, h] + jnp.log(
                denominator
            )


def attend(qkv, image_id, plan, heads, base):
    rows = qkv.shape[0]
    wide = heads * LANES
    width = rows // 4
    out = far_shape(width, heads * HD)
    log = far_shape(heads, 2 * width, dtype=jnp.float32)
    return pl.pallas_call(
        partial(attend_kernel, heads, base),
        grid_spec=pltpu.PrefetchScalarGridSpec(
            num_scalar_prefetch=1,
            grid=(1,),
            in_specs=[
                pl.BlockSpec((2 * width, wide), lambda i, _: (base // 2, 0)),
                pl.BlockSpec((rows, wide), lambda i, _: (0, 1)),
                pl.BlockSpec((rows, wide), lambda i, _: (0, 2)),
                pl.BlockSpec((1, 2 * width), lambda i, _: (0, base // 2)),
                pl.BlockSpec((rows, 1), lambda i, _: (0, 0)),
            ],
            out_specs=[whole(out), whole(out), whole(log)],
            scratch_shapes=[
                pltpu.VMEM((heads, HD + 16, rows), jnp.bfloat16),
                pltpu.VMEM((rows, LANES), jnp.int32),
                pltpu.VMEM((2, heads, TILE, TILE), jnp.float32),
                pltpu.VMEM((2, heads, TILE, TILE), jnp.float32),
                pltpu.VMEM((2 * width // TILE, heads, 1, TILE), jnp.float32),
                pltpu.VMEM((2 * width // TILE, heads, HD + 16, TILE), jnp.float32),
            ],
        ),
        out_shape=[out, out, log],
        name="attend",
        **settings(32, 14 if base else 0.1),
    )(plan, *[qkv] * 3, image_id[None, :], image_id[:, None])


def attend_back_kernel(heads, base, bounds_ref, q_ref, k_ref, v_ref, *refs):
    grad_refs = refs[0:2]
    out_refs = refs[2:4]
    log_ref, id_q_ref, id_k_ref = refs[4:7]
    if base == 0:
        d_q_ref, sums = refs[7:9]
    else:
        near_q_ref, near_sums_ref, d_ref = refs[7:10]
        sums = refs[-1]
    first = 9 if base == 0 else 10
    turned, ids, grads, placed, inner, d_q = refs[first : first + 6]
    width = q_ref.shape[0] // 2
    tile, total = tiles_of(bounds_ref, base)
    for h in range(heads):
        key = k_ref[:, h * LANES : (h + 1) * LANES].astype(jnp.float32).T
        turned[h] = low(key[:HD])
    ids[...] = jnp.broadcast_to(id_k_ref[...], ids.shape)
    d_q[...] = jnp.zeros_like(d_q)
    if base == 0:
        sums[...] = jnp.zeros_like(sums)
    else:
        sums[...] = near_sums_ref[...]
    ones = jnp.ones((8, HD), jnp.float32)
    none = jnp.zeros((width, HD), jnp.bfloat16)
    for query in range(2):
        for h in range(heads):
            grad = grad_refs[query][:, h * HD : (h + 1) * HD]
            grads[query, h] = jnp.concatenate([grad, none], axis=1)
            placed[query, h] = jnp.concatenate([none, grad], axis=1)
            terms = grad.astype(jnp.float32) * out_refs[query][
                :, h * HD : (h + 1) * HD
            ].astype(jnp.float32)
            inner[query, h] = lax.dot_general(
                ones,
                terms,
                NT,
                precision=lax.Precision.HIGHEST,
                preferred_element_type=jnp.float32,
            )[:1]

    def absorb(number):
        query, key, used = tile(number)
        at = block_at(key, width)
        mask = mask_of(ids, id_q_ref, query, key, used, width)
        for h in range(heads):
            columns = slice(h * LANES, (h + 1) * LANES)
            logs = log_ref[h : h + 1, block_at(query, width)]
            queries = q_ref[block_at(query, width), columns]
            scores = product(k_ref[at, columns], queries, NT)
            d_probs = product(v_ref[at, columns], grads[query, h], NT)
            probs = jnp.where(mask, jnp.exp(scores - logs), 0.0)
            d_scores = low(probs * (d_probs - inner[query, h]))
            sums[at, columns] += product(low(probs), placed[query, h]) + product(d_scores, queries)
            d_q[query, h] += product(turned[h, :, at], d_scores)

    def step(number, carry):
        absorb(number)
        return carry

    lax.fori_loop(0, total, step, 0)
    for query in range(2):
        for h in range(heads):
            part = low((d_q[query, h] * 0.125).T)
            if base == 0:
                d_q_ref[query * width : (query + 1) * width, h * HD : (h + 1) * HD] = part
            else:
                here = slice((base + query) * width, (base + query + 1) * width)
                d_ref[here, 3 * h * HD : (3 * h + 1) * HD] = part
    if base:
        for h in range(heads):
            d_ref[: 2 * width, 3 * h * HD : (3 * h + 1) * HD] = near_q_ref[
                :, h * HD : (h + 1) * HD
            ]
            d_ref[:, (3 * h + 1) * HD : (3 * h + 3) * HD] = low(
                sums[:, h * LANES : (h + 1) * LANES]
            )


def attend_back(qkv, d_heads, heads_out, log_total, image_id, bounds, heads, base, near):
    rows = qkv.shape[0]
    wide = heads * LANES
    width = rows // 4
    sums = far_shape(rows, wide, dtype=jnp.float32)
    near = list(near)
    if base == 0:
        outs = [far_shape(2 * width, heads * HD), sums]
    else:
        outs = [shape(rows, 3 * heads * HD)]
    padded = pltpu.VMEM((2, heads, width, LANES), jnp.bfloat16)
    result = pl.pallas_call(
        partial(attend_back_kernel, heads, base),
        grid_spec=pltpu.PrefetchScalarGridSpec(
            num_scalar_prefetch=1,
            grid=(1,),
            in_specs=[
                pl.BlockSpec((2 * width, wide), lambda i, _: (base // 2, 0)),
                pl.BlockSpec((rows, wide), lambda i, _: (0, 1)),
                pl.BlockSpec((rows, wide), lambda i, _: (0, 2)),
            ]
            + [whole(a) for a in (*d_heads, *heads_out, log_total)]
            + [
                pl.BlockSpec((1, 2 * width), lambda i, _: (0, base // 2)),
                pl.BlockSpec((rows, 1), lambda i, _: (0, 0)),
            ]
            + [whole(a) for a in near],
            out_specs=[whole(a) for a in outs],
            scratch_shapes=[
                pltpu.VMEM((heads, HD, rows), jnp.bfloat16),
                pltpu.VMEM((rows, LANES), jnp.int32),
                padded,
                padded,
                pltpu.VMEM((2, heads, 1, width), jnp.float32),
                pltpu.VMEM((2, heads, HD, width), jnp.float32),
            ]
            + ([pltpu.VMEM(sums.shape, jnp.float32)] if near else []),
        ),
        out_shape=outs,
        name="attend_back",
        **settings(36, 20 if base else 3),
    )(
        bounds,
        *[left(qkv)] * 3,
        *d_heads,
        *heads_out,
        log_total,
        image_id[None, :],
        image_id[:, None],
        *(left(a) for a in near),
    )
    return result[0] if near else result


def last_rows(refs, number):
    size = refs[number].shape[0]
    return refs[number][size - refs[0].shape[0] :, :]


def branch_kernel(*refs):
    parts = refs[0:4]
    weights = refs[4:8]
    tokens_ref, gain_ref, resid_ref, in_0_ref, in_1_ref = refs[8:]
    resid = tokens_ref[...].astype(jnp.float32)
    branch = product(parts[0][...], last_rows(weights, 0))
    for j in range(1, 4):
        branch = branch + product(parts[j][...], last_rows(weights, j))
    resid = resid + branch
    resid_ref[...] = resid
    normed = low(normalize(resid, gain_ref[...])[0])
    for half, in_ref in enumerate((in_0_ref, in_1_ref)):

        @pl.when(pl.program_id(0) == half)
        def _():
            in_ref[...] = normed


def branch(parts, weights, tokens, gain):
    rows, model = tokens.shape
    operands = (*parts, *weights, tokens, gain)
    half = far_shape(rows // 2, model)
    resid = far_shape(rows, model, dtype=jnp.float32)

    def halves(array):
        return pl.BlockSpec((rows // 2, array.shape[1]), lambda i: (i, 0))

    specs = [whole(a) for a in operands]
    specs[:4] = [halves(p) for p in parts]
    specs[8] = halves(tokens)
    return pl.pallas_call(
        branch_kernel,
        grid=(2,),
        in_specs=specs,
        out_specs=[halves(resid), whole(half), whole(half)],
        out_shape=[resid, half, half],
        name="branch",
        **settings(16),
    )(*operands)


def mlp_kernel(together, x_a_ref, x_b_ref, g_a_ref, g_b_ref, up_ref, down_ref, *refs):
    act_ref, d_pre_ref = refs[-2:]
    length = x_a_ref.shape[0]
    if together:
        m_a_ref, y_a_ref, both_ref = refs[-5:-2]
        m_b_ref, y_b_ref = both_ref.at[:length], both_ref.at[length:]
    else:
        m_a_ref, y_a_ref, m_b_ref, y_b_ref = refs[-6:-2]

    number = pl.program_id(0)
    mlp_in = chosen(number, (x_b_ref, x_a_ref))
    out_grads = chosen(number, (g_b_ref, g_a_ref))
    pre_act = product(mlp_in, up_ref[...])
    d_act = product(out_grads, down_ref[...], NT)
    below = 0.5 + 0.5 * lax.erf(pre_act * 0.7071067811865476)
    density = 0.3989422804014327 * jnp.exp(-0.5 * pre_act * pre_act)
    d_pre = low(d_act * (below + pre_act * density))
    act = low(pre_act * below)
    m = low(product(d_pre, up_ref[...], NT))
    y = low(product(act, down_ref[...]))
    act_ref[...] = act
    d_pre_ref[...] = d_pre
    for block, (m_ref, y_ref) in enumerate(((m_b_ref, y_b_ref), (m_a_ref, y_a_ref))):

        @pl.when(number == block)
        def _():
            m_ref[...] = m
            y_ref[...] = y


def mlp(x_a, x_b, g_a, g_b, half, place, w_up, w_down, earlier, near):
    length, model = x_a.shape
    hidden = w_up.shape[1]
    extra = [] if earlier is None else list(earlier)

    def grads():
        return pl.BlockSpec((length, model), lambda i: (half, 0))

    def kept(width):
        return pl.BlockSpec((length, width), lambda i: (2 * place + 1 - i, 0))

    one = far_shape(length, model)
    outs = [one, one, far_shape(2 * length, model)] if near else [one] * 4
    return pl.pallas_call(
        partial(mlp_kernel, near),
        grid=(2,),
        in_specs=[whole(x_a), whole(x_b), grads(), grads(), whole(w_up), whole(w_down)]
        + [pl.BlockSpec(memory_space=pl.ANY)] * len(extra),
        out_specs=[whole(a) for a in outs] + [kept(hidden)] * 2,
        out_shape=outs
        + [far_shape(4 * length, hidden)] * 2,
        input_output_aliases={6 + i: len(outs) + i for i in range(len(extra))},
        name="mlp",
        **settings(20),
    )(x_a, x_b, g_a, g_b, w_up, w_down, *extra)


def part_rows(count, bit, totals, kept_ref, sent_ref):
    share = totals[0].shape[0] // count
    for pair in range(count // 2):
        for side, ref in ((bit, kept_ref), (1 - bit, sent_ref)):
            at = pl.ds(pl.multiple_of((2 * pair + side) * share, 8), share)
            first = 0
            for total in totals:
                width = min(total.shape[1], ref.shape[2] - first)
                ref[pair, :, first : first + width] = total[at, :width].astype(ref.dtype)
                first += width


def row_sums(values):
    sums = jnp.sum(values, axis=1, keepdims=True)
    return jnp.broadcast_to(sums, (values.shape[0], LANES)).T[:1]


def mlp_grads_kernel(count, bit_ref, act_ref, d_pre_ref, *refs):
    number = pl.program_id(0)
    x_refs, g_refs = refs[0:4], refs[4:8]
    if count:
        up_ref, old_up_ref, old_down_ref, kept_ref, sent_ref, gain_ref, d_up, d_down = refs[8:]
    else:
        d_up, d_down = refs[8:]

    @pl.when(number == 0)
    def _():
        if count:
            d_up[...] = old_up_ref[...]
            d_down[...] = old_down_ref[...]
        else:
            d_up[...] = jnp.zeros_like(d_up)
            d_down[...] = jnp.zeros_like(d_down)

    x = jnp.concatenate([chosen(number, x_refs[j::2]) for j in range(2)], axis=0)
    d_up[...] += product(x, d_pre_ref[...], TN)
    grads = jnp.concatenate([chosen(number, g_refs[j::2]) for j in range(2)], axis=0)
    d_down[...] += product(grads, act_ref[...], TN)

    @pl.when(number == 1)
    def _():
        if count:
            part_rows(count, bit_ref[0], (d_up, d_down), kept_ref, sent_ref)
            gain_ref[...] = row_sums(d_up[...] * up_ref[...].astype(jnp.float32))


def mlp_grads(act, d_pre, blocks, grads, w_up, earlier):
    rows, hidden = act.shape
    model = blocks[0].shape[1]
    tile = rows // 4
    count = lax.axis_size("dp")
    bit = lax.axis_index("dp") % 2
    total = shape(model, hidden, dtype=jnp.float32)
    kept = far_shape(count // 2, model // count, 2 * hidden, dtype=jnp.float32)
    sent = far_shape(*kept.shape)
    gain = shape(1, model, dtype=jnp.float32)
    extra = [] if earlier is None else [w_up, *earlier]
    outs = [kept, sent, gain] if extra else [total, total]

    def half(rows, columns):
        return pl.BlockSpec((rows, columns), lambda i, _: (i, 0))

    return pl.pallas_call(
        partial(mlp_grads_kernel, count if extra else 0),
        grid_spec=pltpu.PrefetchScalarGridSpec(
            num_scalar_prefetch=1,
            grid=(2,),
            in_specs=[half(2 * tile, hidden)] * 2
            + [whole(a) for a in blocks]
            + [
                pl.BlockSpec((tile, model), lambda i, _, at=at: (at, 0)) for at, _ in grads
            ]
            + [whole(a) for a in extra],
            out_specs=[whole(a) for a in outs],
            scratch_shapes=[pltpu.VMEM((model, hidden), jnp.float32)] * 2 if extra else [],
        ),
        out_shape=outs,
        name="mlp_grads",
        **settings(40),
    )(bit[None], *(left(a) for a in (act, d_pre, *blocks, *(g for _, g in grads))), *extra)


def branch_back_kernel(*refs):
    cotangent_ref, resid_ref, gain_ref = refs[6:9]
    weights = refs[9:13]
    d_resid_ref, d_branch_ref = refs[13:15]
    out_refs = refs[15:19]
    own, pair, far = (chosen(pl.program_id(0), refs[j : j + 2]) for j in (0, 2, 4))
    d_mlp_in = add(own, pair) + far.astype(jnp.float32)
    _, unit, inverse = normalize(resid_ref[...], gain_ref[...])
    d_resid = cotangent_ref[...].astype(jnp.float32) + restore(
        d_mlp_in, unit, inverse, gain_ref[...]
    )
    d_resid_ref[...] = d_resid
    d_branch = low(d_resid)
    d_branch_ref[...] = d_branch
    for j in range(4):
        out_refs[j][...] = low(product(d_branch, last_rows(weights, j), NT))


def branch_back(own, pair, far, cotangent, resid, gain, weights):
    rows, model = resid.shape
    width = weights[0].shape[0]

    def at(columns):
        return pl.BlockSpec((rows // 2, columns), lambda i: (i, 0))

    operands = (*own, *pair, *far, cotangent, resid, gain, *weights)
    specs = [whole(a) for a in operands]
    specs[2] = specs[3] = pl.BlockSpec((rows // 2, model), lambda i: (0, 0))
    specs[6] = specs[7] = at(model)
    return pl.pallas_call(
        branch_back_kernel,
        grid=(2,),
        in_specs=specs,
        out_specs=[at(model), at(model)] + [at(width)] * 4,
        out_shape=[far_shape(rows, model, dtype=jnp.float32), shape(rows, model)]
        + [far_shape(rows, width)] * 4,
        name="branch_back",
        **settings(16),
    )(*(left(a) for a in operands))


def out_grads_kernel(d_ref, *refs):
    for j in range(4):
        refs[4 + j][...] = low(product(d_ref[...], refs[j][...], TN))


def out_weight_grads(d_branch, parts):
    model = d_branch.shape[1]
    out = far_shape(model, parts[0].shape[1])
    return pl.pallas_call(
        out_grads_kernel,
        in_specs=[whole(a) for a in (d_branch, *parts)],
        out_specs=[whole(out)] * 4,
        out_shape=[out] * 4,
        name="out_weight_grads",
        **settings(16),
    )(d_branch, *parts)


def qkv_grads_kernel(count, bit_ref, *refs):
    x_refs = refs[0:8]
    d_ref, w_ref, kept_ref, sent_ref, gain_ref, total = refs[8:]
    number = pl.program_id(0)
    block = jnp.concatenate([chosen(number, x_refs[j::4]) for j in range(4)], axis=0)
    part = product(block, d_ref[...], TN)

    @pl.when(number == 0)
    def _():
        total[...] = part

    @pl.when(number > 0)
    def _():
        total[...] += part

    @pl.when(number == 1)
    def _():
        part_rows(count, bit_ref[0], (total,), kept_ref, sent_ref)
        gain_ref[...] = row_sums(total[...] * w_ref[...].astype(jnp.float32).T)


def qkv_grads(attn_ins, d_qkv, w_qkv):
    rows, model = attn_ins[0].shape
    width = d_qkv.shape[1]
    count = lax.axis_size("dp")
    bit = lax.axis_index("dp") % 2
    kept = far_shape(count // 2, model // count, width, dtype=jnp.float32)
    sent = far_shape(*kept.shape)
    gain = shape(1, model, dtype=jnp.float32)
    return pl.pallas_call(
        partial(qkv_grads_kernel, count),
        grid_spec=pltpu.PrefetchScalarGridSpec(
            num_scalar_prefetch=1,
            grid=(2,),
            in_specs=[whole(x) for x in attn_ins]
            + [pl.BlockSpec((4 * rows, width), lambda i, _: (i, 0)), whole(w_qkv)],
            out_specs=[whole(kept), whole(sent), whole(gain)],
            scratch_shapes=[pltpu.VMEM((model, width), jnp.float32)],
        ),
        out_shape=[kept, sent, gain],
        name="qkv_grads",
        **settings(24),
    )(bit[None], *attn_ins, d_qkv, w_qkv)


def unproject_kernel(d_ref, w_ref, *out_refs):
    part = low(product(d_ref[...], w_ref[...]))
    for number in range(2):

        @pl.when(pl.program_id(0) == number)
        def _():
            out_refs[number][...] = part


def unproject(d_qkv, w_qkv, base):
    rows = d_qkv.shape[0] // 4
    out = far_shape(rows, w_qkv.shape[1])
    return pl.pallas_call(
        unproject_kernel,
        grid=(2,),
        in_specs=[
            pl.BlockSpec((rows, d_qkv.shape[1]), lambda i: (base + i, 0)),
            whole(w_qkv),
        ],
        out_specs=[whole(out), whole(out)],
        out_shape=[out, out],
        name="unproject",
        **settings(16),
    )(d_qkv, w_qkv)


def parted(total, distance):
    bit = (lax.axis_index("dp") // distance) % 2
    total = total.reshape(-1, 2, *total.shape[1:])
    return (
        lax.dynamic_index_in_dim(total, bit, 1, keepdims=False),
        low(lax.dynamic_index_in_dim(total, 1 - bit, 1, keepdims=False)),
    )


def halve(kept, got, distance):
    bit = (lax.axis_index("dp") // distance) % 2
    kept = kept.reshape(-1, 2, *kept.shape[1:])
    got = got.reshape(kept.shape)

    def side(number):
        return add(
            lax.dynamic_index_in_dim(kept, number, 1, keepdims=False),
            lax.dynamic_index_in_dim(got, number, 1, keepdims=False),
        )

    return side(bit), low(side(1 - bit))


def to_last(kept, sent, distance):
    while True:
        got = swap(sent, distance, "dp")
        distance *= 2
        if distance >= lax.axis_size("dp"):
            return kept[0], got[0]
        kept, sent = halve(kept, got, distance)


def sum_steps(value, axis, first=1):
    distance = first
    while distance < lax.axis_size(axis):
        value = value + swap(value, distance, axis)
        distance *= 2
    return value


def on_device(tokens, patch_side, gain_attn, w_qkv, w_out, gain_mlp, w_up, w_down, cotangent):
    rows, model = tokens.shape
    place = lax.axis_index("tp")
    group_rows = 4 * rows
    heads = w_out.shape[0] // HD

    own_0 = norm(tokens, gain_attn, 0)
    own_1 = norm(after(tokens, own_0), gain_attn, 1)
    across_0, across_1 = swap(own_0, 2), swap(own_1, 2)
    pair_0, pair_1 = swap(own_0, 1), swap(own_1, 1)

    cells = (IMAGE // patch_side[0]) ** 2
    full = group_rows // cells
    order = place ^ jnp.arange(4, dtype=jnp.int32)
    positions = (order[:, None] * rows + jnp.arange(rows, dtype=jnp.int32)).reshape(-1)
    image_id = jnp.minimum(positions // cells, full)
    first_id = jnp.minimum(order * rows // cells, full)
    last_id = jnp.minimum((order * rows + rows - 1) // cells, full)
    first_block = first_id * cells // rows
    stop = jnp.where(last_id == full, group_rows, (last_id + 1) * cells)
    last_block = (stop + rows - 1) // rows
    plan = plan_of(place, order, rows, cells)
    bounds = jnp.concatenate(
        [place[None], jnp.stack([first_block, last_block], axis=1).reshape(-1)]
    )

    turned_qkv = w_qkv.T
    by_head = turned_qkv.reshape(heads, 3, HD, model)
    by_head = by_head * jnp.array([0.125, 1.0, 1.0], jnp.bfloat16)[:, None, None]
    spread = jnp.pad(by_head.transpose(1, 0, 2, 3), ((0, 0), (0, 0), (0, LANES - HD), (0, 0)))
    spread = spread.reshape(3 * heads * LANES, model)
    qkv = project([own_0, own_1, pair_0, pair_1], spread, (0, 1, 2, 3), None)
    across_0, qkv = join(across_0, qkv)
    diagonal_0 = swap(across_0, 1)
    qkv = project([across_0, diagonal_0], spread, (4, 6), qkv)
    across_1, qkv = join(across_1, qkv)
    diagonal_1 = swap(across_1, 1)
    qkv = project([across_1], spread, (5,), qkv)
    diagonal_1, qkv = join(diagonal_1, qkv)
    qkv = project([diagonal_1], spread, (7,), qkv)
    attn_ins = [own_0, own_1, pair_0, pair_1, across_0, across_1, diagonal_0, diagonal_1]

    middle = rows // 2
    w_pair = swap(after(w_out, across_1), 1)
    grads_pair = swap(after(cotangent, across_1), 1)
    mixed_in = jnp.concatenate([cotangent[:middle], w_out], axis=0)
    in_across = swap(after(mixed_in, across_1), 2)
    far = attend(qkv, image_id, plan, heads, 2)
    *far, w_pair, grads_pair = join(*far, w_pair, grads_pair)
    out_2, out_3, logs_far = far
    got_2, got_3 = swap(out_2, 2), swap(out_3, 3)
    grads_1 = swap(after(cotangent[middle:], out_2), 2)
    near = attend(after(qkv, out_2), image_id, plan, heads, 0)
    *near, got_2, got_3, in_across = join(*near, got_2, got_3, in_across)
    in_diagonal = swap(in_across, 1)
    out_0, out_1, logs_near = near
    got_1 = swap(out_1, 1)
    mine = [out_0, got_1, got_2, got_3]
    w_outs = [w_out, w_pair, in_across, in_diagonal]
    resid, *mlp_in = branch(mine, w_outs, tokens, gain_mlp)
    mlp_in[0], grads_1 = join(mlp_in[0], grads_1)
    grads_1_diagonal = swap(grads_1, 1)

    pairs = [swap(m, 1) for m in mlp_in]
    across_0 = swap(mlp_in[0], 2)
    own_0, y_0, pair_0, *near = mlp(
        mlp_in[0], pairs[0], cotangent, grads_pair, 0, 0, w_up, w_down, None, True
    )
    own_1, y_1, pair_1, *near = mlp(
        mlp_in[1], pairs[1], cotangent, grads_pair, 1, 1, w_up, w_down, near, True
    )
    across_0, own_1, pair_0, pair_1, grads_1_diagonal = join(
        across_0, own_1, pair_0, pair_1, grads_1_diagonal
    )
    across_1 = swap(after(mlp_in[1], across_0), 2)
    diagonal_0, pair_0, pair_1 = join(swap(across_0, 1), swap(pair_0, 1), swap(pair_1, 1))
    m_2, y_20, m_3, y_30, *kept = mlp(
        across_0, diagonal_0, in_across, in_diagonal, 0, 0, w_up, w_down, None, False
    )
    across_1, m_2, y_30 = join(across_1, m_2, swap(y_30, 1))
    far_0 = low(add(m_2, swap(m_3, 1)))
    diagonal_1 = swap(across_1, 1)
    m_2, y_21, m_3, y_31, *kept = mlp(
        across_1, diagonal_1, grads_1, grads_1_diagonal, 0, 1, w_up, w_down, kept, False
    )
    sums = mlp_grads(
        after(near[0], m_2),
        near[1],
        (mlp_in[0], pairs[0], mlp_in[1], pairs[1]),
        ((0, cotangent), (0, grads_pair), (1, cotangent), (1, grads_pair)),
        w_up,
        None,
    )
    far_0, m_2, y_31, *sums = join(swap(far_0, 2), m_2, swap(y_31, 1), *sums)
    far_1 = low(add(m_2, swap(m_3, 1)))
    kept_mlp, sent_mlp, gain_mlp_part = mlp_grads(
        after(kept[0], far_1),
        kept[1],
        (across_0, diagonal_0, across_1, diagonal_1),
        ((0, in_across), (0, in_diagonal), (0, grads_1), (0, grads_1_diagonal)),
        w_up,
        sums,
    )
    mixed_far = [low(add(after(y_20, sent_mlp), y_30)), low(add(after(y_21, sent_mlp), y_31))]
    mixed_far, kept_mlp, sent_mlp, far_1 = join(
        jnp.concatenate(mixed_far, axis=0), kept_mlp, sent_mlp, swap(far_1, 2)
    )

    d_resid, d_branch, *d_pieces = branch_back(
        (own_0, own_1), (pair_0, pair_1), (far_0, far_1), cotangent, resid, gain_mlp, w_outs
    )
    d_1, d_2, d_3 = [swap(d_pieces[j], j) for j in range(1, 4)]
    d_outs = out_weight_grads(after(d_branch, d_pieces[0]), mine)
    out_far = low(add(d_outs[2], swap(d_outs[3], 1)))
    back = attend_back(
        after(qkv, out_far),
        (d_pieces[0], d_1),
        (out_0, out_1),
        logs_near,
        image_id,
        bounds,
        heads,
        0,
        (),
    )
    *back, got_mlp, d_2, d_3, out_far = join(
        *back, swap(sent_mlp, 1, "dp"), d_2, d_3, swap(out_far, 2)
    )
    count = lax.axis_size("dp")
    out_pair = swap(after(d_outs[1], back[0]), 1)
    kept_mlp, sent_mlp = halve(kept_mlp, got_mlp, 2)
    d_out = add(d_outs[0], out_pair) + out_far.astype(jnp.float32)
    kept_out, sent_out = parted(d_out.reshape(count, model // count, -1), 1)
    d_qkv = attend_back(
        after(qkv, sent_out, sent_mlp),
        (d_2, d_3),
        (out_2, out_3),
        logs_far,
        image_id,
        bounds,
        heads,
        2,
        back,
    )
    kept_mlp, got_mlp = to_last(kept_mlp, sent_mlp, 2)
    d_qkv, got_out, mixed_far = join(
        d_qkv, swap(sent_out, 1, "dp"), swap(after(mixed_far, sent_out), 2)
    )

    kept, sent, gain_attn_part = qkv_grads(attn_ins, d_qkv, turned_qkv)
    part_2, part_3, kept_mlp, got_mlp = join(
        *unproject(after(d_qkv, sent), turned_qkv, 2), kept_mlp, got_mlp
    )
    grad_mlp = low(add(kept_mlp, got_mlp))
    gains = jnp.concatenate(
        [gain_attn_part / gain_attn[None, :], gain_mlp_part / gain_mlp[None, :]], axis=0
    )
    gains, part_3, part_0, part_1 = join(
        gains + swap(gains, 1),
        swap(part_3, 1),
        *unproject(after(d_qkv, part_2, grad_mlp), turned_qkv, 0),
    )
    d_far = low(add(part_2, part_3))
    pair = swap(part_1, 1)
    kept_out, got_out = to_last(*halve(kept_out, got_out, 2), 2)
    gains = sum_steps(gains, "tp", 2)
    d_far = after(d_far, gains)
    got, gains, kept_out, got_out = join(swap(sent, 1, "dp"), gains, kept_out, got_out)

    kept, sent = halve(kept, got, 2)
    far = swap(d_far, 2)
    gains = sum_steps(gains, "grp")
    kept, got, gains, pair, got_mlp = join(
        *to_last(kept, sent, 2),
        gains + swap(gains, 1, "dp"),
        pair,
        swap(grad_mlp, 1, "grp"),
    )
    grad_rest = jnp.concatenate([low(add(kept, got)), low(add(kept_out, got_out))], axis=1)
    grad_mlp = add(grad_mlp, got_mlp)
    mixed_near = jnp.concatenate(
        [add(y_0, pair_0[middle:]), add(y_1, pair_1[middle:])], axis=0
    )
    mixed_rows = low(resid + (mixed_near + mixed_far.astype(jnp.float32)))
    input_grad = norm_back(tokens, gain_attn, part_0, pair, far, d_resid)
    got, gains, input_grad = join(
        swap(grad_rest, 1, "grp"), sum_steps(gains, "dp", 2), input_grad
    )
    grad_rest = add(grad_rest, got)
    width = w_qkv.shape[1]
    hidden = w_up.shape[1]
    return (
        mixed_rows,
        input_grad,
        gains[0],
        grad_rest[:, :width],
        grad_rest[:, width:].T,
        gains[1],
        grad_mlp[:, :hidden],
        grad_mlp[:, hidden:].T,
    )


def solution(mesh):
    in_specs = (
        P(("grp", "dp", "tp"), None),
        P(("grp", "dp")),
        P(),
        P(None, "tp"),
        P("tp", None),
        P(),
        P(None, "tp"),
        P("tp", None),
        P(("grp", "dp", "tp"), None),
    )
    out_specs = (
        P(("grp", "dp", "tp"), None),
        P(("grp", "dp", "tp"), None),
        P(),
        P("dp", "tp"),
        P("tp", "dp"),
        P(),
        P("dp", "tp"),
        P("tp", "dp"),
    )
    return jax.shard_map(
        on_device, mesh=mesh, in_specs=in_specs, out_specs=out_specs, check_vma=False
    )
```

```python
from functools import partial

import jax
import jax.numpy as jnp
from jax import lax
from jax.experimental import pallas as pl
from jax.experimental.pallas import tpu as pltpu
from jax.sharding import PartitionSpec as P

HD = 64
LANES = 128
IMAGE = 240
EXCLUDED = -1e30
MIB = 1024 * 1024
NT = (((1,), (1,)), ((), ()))
TN = (((0,), (0,)), ((), ()))

epsilon = 1e-06


def normalize(values, scaling):
    centred = values - jnp.mean(values, axis=1, keepdims=True)
    inverse = lax.rsqrt(jnp.mean(centred * centred, axis=1, keepdims=True) + epsilon)
    normed = centred * inverse
    return (normed * scaling, normed, inverse)


def restore(d_normed, normed, inverse, scaling):
    d_scaled = d_normed * scaling
    return inverse * (
        d_scaled
        - jnp.mean(d_scaled, axis=1, keepdims=True)
        - normed * jnp.mean(d_scaled * normed, axis=1, keepdims=True)
    )


def swap(value, distance, axis="tp"):
    size = lax.axis_size(axis)
    return lax.ppermute(value, axis, [(i, i ^ distance) for i in range(size)])


def after(value, *earlier):
    return lax.optimization_barrier((value, *earlier))[0]


def join(*values):
    return lax.optimization_barrier(values)


def add(left, right):
    return left.astype(jnp.float32) + right.astype(jnp.float32)


def product(left, right, dims=(((1,), (0,)), ((), ()))):
    return lax.dot_general(left, right, dims, preferred_element_type=jnp.float32)


def low(value):
    return value.astype(jnp.bfloat16)


def settings(limit, microseconds=0.1):
    return dict(
        compiler_params=pltpu.CompilerParams(vmem_limit_bytes=limit * MIB),
        cost_estimate=pl.CostEstimate(
            flops=int(microseconds * 1.1e9), bytes_accessed=MIB, transcendentals=0
        ),
    )


def whole(array):
    return pl.BlockSpec(array.shape, lambda *_: (0,) * len(array.shape))


def shape(*dims, dtype=jnp.bfloat16):
    return jax.ShapeDtypeStruct(dims, dtype)


def far_shape(*dims, dtype=jnp.bfloat16):
    return pltpu.HBM(dims, dtype)


def left(array):
    return pltpu.with_memory_space_constraint(array, pltpu.HBM)


def chosen(number, refs):
    value = refs[0][...]
    for other in range(1, len(refs)):
        value = jnp.where(number == other, refs[other][...], value)
    return value


def norm_kernel(x_ref, gain_ref, out_ref):
    out_ref[...] = low(normalize(x_ref[...].astype(jnp.float32), gain_ref[...])[0])


def norm(tokens, gain, half):
    rows, model = tokens.shape
    return pl.pallas_call(
        norm_kernel,
        grid=(1,),
        in_specs=[pl.BlockSpec((rows // 2, model), lambda i: (half, 0)), whole(gain)],
        out_specs=pl.BlockSpec((rows // 2, model), lambda i: (0, 0)),
        out_shape=far_shape(rows // 2, model),
        name="norm",
        **settings(8, 2),
    )(left(tokens), left(gain))


def norm_back_kernel(x_ref, gain_ref, own_ref, pair_ref, far_ref, d_ref, out_ref):
    d_normed = add(own_ref[...], pair_ref[...]) + far_ref[...].astype(jnp.float32)
    _, unit, inverse = normalize(x_ref[...].astype(jnp.float32), gain_ref[...])
    out_ref[...] = d_ref[...] + restore(d_normed, unit, inverse, gain_ref[...])


def norm_back(tokens, gain, own, pair, far, d_resid):
    rows, model = tokens.shape
    tile = pl.BlockSpec((rows // 4, model), lambda i: (i, 0))
    return pl.pallas_call(
        norm_back_kernel,
        grid=(4,),
        in_specs=[tile, whole(gain)] + [tile] * 4,
        out_specs=tile,
        out_shape=shape(rows, model, dtype=jnp.float32),
        name="norm_back",
        **settings(16, 2),
    )(tokens, gain, own, pair, far, d_resid)


def project_kernel(count, *refs):
    out_ref = refs[-1]
    out_ref[...] = low(product(chosen(pl.program_id(0), refs[:count]), refs[count][...], NT))


def project(blocks, weights, places, earlier):
    rows = blocks[0].shape[0]
    wide = weights.shape[0]
    count = len(blocks)
    group_rows = rows * 8 if earlier is None else earlier.shape[0]
    extra = [] if earlier is None else [earlier]
    return pl.pallas_call(
        partial(project_kernel, count),
        grid=(count,),
        in_specs=[whole(x) for x in blocks]
        + [whole(weights)]
        + [pl.BlockSpec(memory_space=pl.ANY)] * len(extra),
        out_specs=pl.BlockSpec(
            (rows, wide), lambda i: (places[0] + i * (places[-1] - places[0]) // max(count - 1, 1), 0)
        ),
        out_shape=shape(group_rows, wide),
        input_output_aliases={count + 1: 0} if extra else {},
        name="project",
        **settings(16),
    )(*blocks, weights, *extra)


def tiles_of(bounds_ref, base):
    where = 1 + 2 * base
    first, second = bounds_ref[where], bounds_ref[where + 2]
    count = bounds_ref[where + 1] - first
    total = count + bounds_ref[where + 3] - second

    def tile(number):
        late = (number >= count).astype(jnp.int32)
        key = jnp.where(late == 1, second + number - count, first + number)
        key = jnp.minimum(key, bounds_ref[where + 3] - 1 + (1 - late) * 4)
        return late, key ^ bounds_ref[0], number < total

    return tile, total


def block_at(number, width):
    return pl.ds(pl.multiple_of(number * width, width), width)


def mask_of(ids, id_q_ref, query, key, used, width):
    id_q = id_q_ref[:, block_at(query, width)] + jnp.where(used, 0, 1 << 20)
    return jnp.concatenate([ids[block_at(key, width), :]] * (width // LANES), axis=1) == id_q


TILE = 256
MOST = 40


def plan_of(place, order, rows, cells):
    group_rows = 4 * rows
    per = rows // TILE
    full = group_rows // cells
    inside = jnp.arange(per, dtype=jnp.int32) * TILE
    first = (order[:, None] * rows + inside).reshape(2, 1, 2 * per)
    first_id = jnp.minimum(first // cells, full)
    last_id = jnp.minimum((first + TILE - 1) // cells, full)
    low_key = first_id * cells // TILE
    stop = jnp.where(last_id == full, group_rows, (last_id + 1) * cells)
    turn = jnp.arange(4 * per, dtype=jnp.int32)[None, :, None]
    key = low_key + turn
    used = (key * TILE < stop).reshape(2, -1)
    key = ((key // per) ^ place) * per + key % per
    code = (key + 64 * jnp.arange(2 * per, dtype=jnp.int32)).reshape(2, -1)
    number = jnp.cumsum(used.astype(jnp.int32), axis=1)
    wanted = jnp.arange(1, MOST + 1, dtype=jnp.int32)[None, :, None]
    chosen = used[:, None, :] & (number[:, None, :] == wanted)
    listed = jnp.sum(jnp.where(chosen, code[:, None, :], 0), axis=2)
    return jnp.concatenate([number[:, -1:], listed], axis=1)


def tile_of(plan_ref, base, number):
    code = plan_ref[base // 2, 1 + number]
    return code // 64, code % 64, number < plan_ref[base // 2, 0]


def tile_at(number):
    return pl.ds(pl.multiple_of(number * TILE, TILE), TILE)


def tile_mask(ids, id_q_ref, query, key, used):
    id_q = id_q_ref[:, tile_at(query)] + jnp.where(used, 0, 1 << 20)
    return jnp.concatenate([ids[tile_at(key), :]] * (TILE // LANES), axis=1) == id_q


def in_turn(total, prepare, absorb):
    for number in range(2):
        prepare(number, 0, number)

    def step(number, carry):
        for side in range(2):
            for part in range(2):
                prepare(4 * number + 2 * side + 2 + part, 1 - side, part)
            for part in range(2):
                absorb(4 * number + 2 * side + part, side, part)
        return carry

    lax.fori_loop(0, (total + 3) // 4, step, 0)


def attend_kernel(heads, base, plan_ref, q_ref, k_ref, v_ref, id_q_ref, id_k_ref, *refs):
    out_refs = refs[:2]
    log_ref, turned, ids, scores_a, scores_b, tops, totals = refs[2:]
    scores_refs = (scores_a, scores_b)
    width = q_ref.shape[0] // 2
    for h in range(heads):
        value = v_ref[:, h * LANES : (h + 1) * LANES].astype(jnp.float32).T
        turned[h, :HD] = low(value[:HD])
        turned[h, HD:] = jnp.ones((turned.shape[1] - HD, v_ref.shape[0]), jnp.bfloat16)
    ids[...] = jnp.broadcast_to(id_k_ref[...], ids.shape)
    tops[...] = jnp.full(tops.shape, EXCLUDED, jnp.float32)
    totals[...] = jnp.zeros_like(totals)

    def prepare(number, side, part):
        query, key, _ = tile_of(plan_ref, base, number)
        for h in range(heads):
            columns = slice(h * LANES, (h + 1) * LANES)
            scores_refs[side][part, h] = product(
                k_ref[tile_at(key), columns], q_ref[tile_at(query), columns], NT
            )

    def absorb(number, side, part):
        query, key, used = tile_of(plan_ref, base, number)
        mask = tile_mask(ids, id_q_ref, query, key, used)
        for h in range(heads):
            scores = jnp.where(mask, scores_refs[side][part, h], EXCLUDED)
            largest = tops[query, h]
            top = jnp.maximum(largest, jnp.max(scores, axis=0, keepdims=True))
            exponent = low(jnp.exp(scores - top))
            tops[query, h] = top
            totals[query, h] = totals[query, h] * jnp.exp(largest - top) + product(
                turned[h, :, tile_at(key)], exponent
            )

    in_turn(plan_ref[base // 2, 0], prepare, absorb)
    for query in range(tops.shape[0]):
        block, at = divmod(query * TILE, width)
        for h in range(heads):
            sums = totals[query, h]
            denominator = sums[HD : HD + 1]
            out_refs[block][at : at + TILE, h * HD : (h + 1) * HD] = low(
                (sums[:HD] / denominator).T
            )
            log_ref[h : h + 1, query * TILE : (query + 1) * TILE] = tops[query, h] + jnp.log(
                denominator
            )


def attend(qkv, image_id, plan, heads, base):
    rows = qkv.shape[0]
    wide = heads * LANES
    width = rows // 4
    out = far_shape(width, heads * HD)
    log = far_shape(heads, 2 * width, dtype=jnp.float32)
    return pl.pallas_call(
        partial(attend_kernel, heads, base),
        grid_spec=pltpu.PrefetchScalarGridSpec(
            num_scalar_prefetch=1,
            grid=(1,),
            in_specs=[
                pl.BlockSpec((2 * width, wide), lambda i, _: (base // 2, 0)),
                pl.BlockSpec((rows, wide), lambda i, _: (0, 1)),
                pl.BlockSpec((rows, wide), lambda i, _: (0, 2)),
                pl.BlockSpec((1, 2 * width), lambda i, _: (0, base // 2)),
                pl.BlockSpec((rows, 1), lambda i, _: (0, 0)),
            ],
            out_specs=[whole(out), whole(out), whole(log)],
            scratch_shapes=[
                pltpu.VMEM((heads, HD + 16, rows), jnp.bfloat16),
                pltpu.VMEM((rows, LANES), jnp.int32),
                pltpu.VMEM((2, heads, TILE, TILE), jnp.float32),
                pltpu.VMEM((2, heads, TILE, TILE), jnp.float32),
                pltpu.VMEM((2 * width // TILE, heads, 1, TILE), jnp.float32),
                pltpu.VMEM((2 * width // TILE, heads, HD + 16, TILE), jnp.float32),
            ],
        ),
        out_shape=[out, out, log],
        name="attend",
        **settings(32, 14 if base else 0.1),
    )(plan, *[qkv] * 3, image_id[None, :], image_id[:, None])


def attend_back_kernel(heads, base, bounds_ref, q_ref, k_ref, v_ref, *refs):
    grad_refs = refs[0:2]
    out_refs = refs[2:4]
    log_ref, id_q_ref, id_k_ref = refs[4:7]
    if base == 0:
        d_q_ref, sums = refs[7:9]
    else:
        near_q_ref, near_sums_ref, d_ref = refs[7:10]
        sums = refs[-1]
    first = 9 if base == 0 else 10
    turned, ids, grads, placed, inner, d_q = refs[first : first + 6]
    width = q_ref.shape[0] // 2
    tile, total = tiles_of(bounds_ref, base)
    for h in range(heads):
        key = k_ref[:, h * LANES : (h + 1) * LANES].astype(jnp.float32).T
        turned[h] = low(key[:HD])
    ids[...] = jnp.broadcast_to(id_k_ref[...], ids.shape)
    d_q[...] = jnp.zeros_like(d_q)
    if base == 0:
        sums[...] = jnp.zeros_like(sums)
    else:
        sums[...] = near_sums_ref[...]
    ones = jnp.ones((8, HD), jnp.float32)
    none = jnp.zeros((width, HD), jnp.bfloat16)
    for query in range(2):
        for h in range(heads):
            grad = grad_refs[query][:, h * HD : (h + 1) * HD]
            grads[query, h] = jnp.concatenate([grad, none], axis=1)
            placed[query, h] = jnp.concatenate([none, grad], axis=1)
            terms = grad.astype(jnp.float32) * out_refs[query][
                :, h * HD : (h + 1) * HD
            ].astype(jnp.float32)
            inner[query, h] = lax.dot_general(
                ones,
                terms,
                NT,
                precision=lax.Precision.HIGHEST,
                preferred_element_type=jnp.float32,
            )[:1]

    def absorb(number):
        query, key, used = tile(number)
        at = block_at(key, width)
        mask = mask_of(ids, id_q_ref, query, key, used, width)
        for h in range(heads):
            columns = slice(h * LANES, (h + 1) * LANES)
            logs = log_ref[h : h + 1, block_at(query, width)]
            queries = q_ref[block_at(query, width), columns]
            scores = product(k_ref[at, columns], queries, NT)
            d_probs = product(v_ref[at, columns], grads[query, h], NT)
            probs = jnp.where(mask, jnp.exp(scores - logs), 0.0)
            d_scores = low(probs * (d_probs - inner[query, h]))
            sums[at, columns] += product(low(probs), placed[query, h]) + product(d_scores, queries)
            d_q[query, h] += product(turned[h, :, at], d_scores)

    def step(number, carry):
        absorb(number)
        return carry

    lax.fori_loop(0, total, step, 0)
    for query in range(2):
        for h in range(heads):
            part = low((d_q[query, h] * 0.125).T)
            if base == 0:
                d_q_ref[query * width : (query + 1) * width, h * HD : (h + 1) * HD] = part
            else:
                here = slice((base + query) * width, (base + query + 1) * width)
                d_ref[here, 3 * h * HD : (3 * h + 1) * HD] = part
    if base:
        for h in range(heads):
            d_ref[: 2 * width, 3 * h * HD : (3 * h + 1) * HD] = near_q_ref[
                :, h * HD : (h + 1) * HD
            ]
            d_ref[:, (3 * h + 1) * HD : (3 * h + 3) * HD] = low(
                sums[:, h * LANES : (h + 1) * LANES]
            )


def attend_back(qkv, d_heads, heads_out, log_total, image_id, bounds, heads, base, near):
    rows = qkv.shape[0]
    wide = heads * LANES
    width = rows // 4
    sums = far_shape(rows, wide, dtype=jnp.float32)
    near = list(near)
    if base == 0:
        outs = [far_shape(2 * width, heads * HD), sums]
    else:
        outs = [shape(rows, 3 * heads * HD)]
    padded = pltpu.VMEM((2, heads, width, LANES), jnp.bfloat16)
    result = pl.pallas_call(
        partial(attend_back_kernel, heads, base),
        grid_spec=pltpu.PrefetchScalarGridSpec(
            num_scalar_prefetch=1,
            grid=(1,),
            in_specs=[
                pl.BlockSpec((2 * width, wide), lambda i, _: (base // 2, 0)),
                pl.BlockSpec((rows, wide), lambda i, _: (0, 1)),
                pl.BlockSpec((rows, wide), lambda i, _: (0, 2)),
            ]
            + [whole(a) for a in (*d_heads, *heads_out, log_total)]
            + [
                pl.BlockSpec((1, 2 * width), lambda i, _: (0, base // 2)),
                pl.BlockSpec((rows, 1), lambda i, _: (0, 0)),
            ]
            + [whole(a) for a in near],
            out_specs=[whole(a) for a in outs],
            scratch_shapes=[
                pltpu.VMEM((heads, HD, rows), jnp.bfloat16),
                pltpu.VMEM((rows, LANES), jnp.int32),
                padded,
                padded,
                pltpu.VMEM((2, heads, 1, width), jnp.float32),
                pltpu.VMEM((2, heads, HD, width), jnp.float32),
            ]
            + ([pltpu.VMEM(sums.shape, jnp.float32)] if near else []),
        ),
        out_shape=outs,
        name="attend_back",
        **settings(36, 20 if base else 3),
    )(
        bounds,
        *[left(qkv)] * 3,
        *d_heads,
        *heads_out,
        log_total,
        image_id[None, :],
        image_id[:, None],
        *(left(a) for a in near),
    )
    return result[0] if near else result


def last_rows(refs, number):
    size = refs[number].shape[0]
    return refs[number][size - refs[0].shape[0] :, :]


def branch_kernel(*refs):
    parts = refs[0:4]
    weights = refs[4:8]
    tokens_ref, gain_ref, resid_ref, in_0_ref, in_1_ref = refs[8:]
    resid = tokens_ref[...].astype(jnp.float32)
    branch = product(parts[0][...], last_rows(weights, 0))
    for j in range(1, 4):
        branch = branch + product(parts[j][...], last_rows(weights, j))
    resid = resid + branch
    resid_ref[...] = resid
    normed = low(normalize(resid, gain_ref[...])[0])
    for half, in_ref in enumerate((in_0_ref, in_1_ref)):

        @pl.when(pl.program_id(0) == half)
        def _():
            in_ref[...] = normed


def branch(parts, weights, tokens, gain):
    rows, model = tokens.shape
    operands = (*parts, *weights, tokens, gain)
    half = far_shape(rows // 2, model)
    resid = far_shape(rows, model, dtype=jnp.float32)

    def halves(array):
        return pl.BlockSpec((rows // 2, array.shape[1]), lambda i: (i, 0))

    specs = [whole(a) for a in operands]
    specs[:4] = [halves(p) for p in parts]
    specs[8] = halves(tokens)
    return pl.pallas_call(
        branch_kernel,
        grid=(2,),
        in_specs=specs,
        out_specs=[halves(resid), whole(half), whole(half)],
        out_shape=[resid, half, half],
        name="branch",
        **settings(16),
    )(*operands)


def mlp_kernel(together, x_a_ref, x_b_ref, g_a_ref, g_b_ref, up_ref, down_ref, *refs):
    act_ref, d_pre_ref = refs[-2:]
    length = x_a_ref.shape[0]
    if together:
        m_a_ref, y_a_ref, both_ref = refs[-5:-2]
        m_b_ref, y_b_ref = both_ref.at[:length], both_ref.at[length:]
    else:
        m_a_ref, y_a_ref, m_b_ref, y_b_ref = refs[-6:-2]

    number = pl.program_id(0)
    mlp_in = chosen(number, (x_b_ref, x_a_ref))
    out_grads = chosen(number, (g_b_ref, g_a_ref))
    pre_act = product(mlp_in, up_ref[...])
    d_act = product(out_grads, down_ref[...], NT)
    below = 0.5 + 0.5 * lax.erf(pre_act * 0.7071067811865476)
    density = 0.3989422804014327 * jnp.exp(-0.5 * pre_act * pre_act)
    d_pre = low(d_act * (below + pre_act * density))
    act = low(pre_act * below)
    m = low(product(d_pre, up_ref[...], NT))
    y = low(product(act, down_ref[...]))
    act_ref[...] = act
    d_pre_ref[...] = d_pre
    for block, (m_ref, y_ref) in enumerate(((m_b_ref, y_b_ref), (m_a_ref, y_a_ref))):

        @pl.when(number == block)
        def _():
            m_ref[...] = m
            y_ref[...] = y


def mlp(x_a, x_b, g_a, g_b, half, place, w_up, w_down, earlier, near):
    length, model = x_a.shape
    hidden = w_up.shape[1]
    extra = [] if earlier is None else list(earlier)

    def grads():
        return pl.BlockSpec((length, model), lambda i: (half, 0))

    def kept(width):
        return pl.BlockSpec((length, width), lambda i: (2 * place + 1 - i, 0))

    one = far_shape(length, model)
    outs = [one, one, far_shape(2 * length, model)] if near else [one] * 4
    return pl.pallas_call(
        partial(mlp_kernel, near),
        grid=(2,),
        in_specs=[whole(x_a), whole(x_b), grads(), grads(), whole(w_up), whole(w_down)]
        + [pl.BlockSpec(memory_space=pl.ANY)] * len(extra),
        out_specs=[whole(a) for a in outs] + [kept(hidden)] * 2,
        out_shape=outs
        + [far_shape(4 * length, hidden)] * 2,
        input_output_aliases={6 + i: len(outs) + i for i in range(len(extra))},
        name="mlp",
        **settings(20),
    )(x_a, x_b, g_a, g_b, w_up, w_down, *extra)


def part_rows(count, bit, totals, kept_ref, sent_ref):
    share = totals[0].shape[0] // count
    for pair in range(count // 2):
        for side, ref in ((bit, kept_ref), (1 - bit, sent_ref)):
            at = pl.ds(pl.multiple_of((2 * pair + side) * share, 8), share)
            first = 0
            for total in totals:
                width = min(total.shape[1], ref.shape[2] - first)
                ref[pair, :, first : first + width] = total[at, :width].astype(ref.dtype)
                first += width


def row_sums(values):
    sums = jnp.sum(values, axis=1, keepdims=True)
    return jnp.broadcast_to(sums, (values.shape[0], LANES)).T[:1]


def mlp_grads_kernel(count, bit_ref, act_ref, d_pre_ref, *refs):
    number = pl.program_id(0)
    x_refs, g_refs = refs[0:4], refs[4:8]
    if count:
        up_ref, old_up_ref, old_down_ref, kept_ref, sent_ref, gain_ref, d_up, d_down = refs[8:]
    else:
        d_up, d_down = refs[8:]

    @pl.when(number == 0)
    def _():
        if count:
            d_up[...] = old_up_ref[...]
            d_down[...] = old_down_ref[...]
        else:
            d_up[...] = jnp.zeros_like(d_up)
            d_down[...] = jnp.zeros_like(d_down)

    x = jnp.concatenate([chosen(number, x_refs[j::2]) for j in range(2)], axis=0)
    d_up[...] += product(x, d_pre_ref[...], TN)
    grads = jnp.concatenate([chosen(number, g_refs[j::2]) for j in range(2)], axis=0)
    d_down[...] += product(grads, act_ref[...], TN)

    @pl.when(number == 1)
    def _():
        if count:
            part_rows(count, bit_ref[0], (d_up, d_down), kept_ref, sent_ref)
            gain_ref[...] = row_sums(d_up[...] * up_ref[...].astype(jnp.float32))


def mlp_grads(act, d_pre, blocks, grads, w_up, earlier):
    rows, hidden = act.shape
    model = blocks[0].shape[1]
    tile = rows // 4
    count = lax.axis_size("dp")
    bit = lax.axis_index("dp") % 2
    total = shape(model, hidden, dtype=jnp.float32)
    kept = far_shape(count // 2, model // count, 2 * hidden, dtype=jnp.float32)
    sent = far_shape(*kept.shape)
    gain = shape(1, model, dtype=jnp.float32)
    extra = [] if earlier is None else [w_up, *earlier]
    outs = [kept, sent, gain] if extra else [total, total]

    def half(rows, columns):
        return pl.BlockSpec((rows, columns), lambda i, _: (i, 0))

    return pl.pallas_call(
        partial(mlp_grads_kernel, count if extra else 0),
        grid_spec=pltpu.PrefetchScalarGridSpec(
            num_scalar_prefetch=1,
            grid=(2,),
            in_specs=[half(2 * tile, hidden)] * 2
            + [whole(a) for a in blocks]
            + [
                pl.BlockSpec((tile, model), lambda i, _, at=at: (at, 0)) for at, _ in grads
            ]
            + [whole(a) for a in extra],
            out_specs=[whole(a) for a in outs],
            scratch_shapes=[pltpu.VMEM((model, hidden), jnp.float32)] * 2 if extra else [],
        ),
        out_shape=outs,
        name="mlp_grads",
        **settings(40),
    )(bit[None], *(left(a) for a in (act, d_pre, *blocks, *(g for _, g in grads))), *extra)


def branch_back_kernel(*refs):
    cotangent_ref, resid_ref, gain_ref = refs[6:9]
    weights = refs[9:13]
    d_resid_ref, d_branch_ref = refs[13:15]
    out_refs = refs[15:19]
    own, pair, far = (chosen(pl.program_id(0), refs[j : j + 2]) for j in (0, 2, 4))
    d_mlp_in = add(own, pair) + far.astype(jnp.float32)
    _, unit, inverse = normalize(resid_ref[...], gain_ref[...])
    d_resid = cotangent_ref[...].astype(jnp.float32) + restore(
        d_mlp_in, unit, inverse, gain_ref[...]
    )
    d_resid_ref[...] = d_resid
    d_branch = low(d_resid)
    d_branch_ref[...] = d_branch
    for j in range(4):
        out_refs[j][...] = low(product(d_branch, last_rows(weights, j), NT))


def branch_back(own, pair, far, cotangent, resid, gain, weights):
    rows, model = resid.shape
    width = weights[0].shape[0]

    def at(columns):
        return pl.BlockSpec((rows // 2, columns), lambda i: (i, 0))

    operands = (*own, *pair, *far, cotangent, resid, gain, *weights)
    specs = [whole(a) for a in operands]
    specs[2] = specs[3] = pl.BlockSpec((rows // 2, model), lambda i: (0, 0))
    specs[6] = specs[7] = at(model)
    return pl.pallas_call(
        branch_back_kernel,
        grid=(2,),
        in_specs=specs,
        out_specs=[at(model), at(model)] + [at(width)] * 4,
        out_shape=[far_shape(rows, model, dtype=jnp.float32), shape(rows, model)]
        + [far_shape(rows, width)] * 4,
        name="branch_back",
        **settings(16),
    )(*(left(a) for a in operands))


def out_grads_kernel(d_ref, *refs):
    for j in range(4):
        refs[4 + j][...] = low(product(d_ref[...], refs[j][...], TN))


def out_weight_grads(d_branch, parts):
    model = d_branch.shape[1]
    out = far_shape(model, parts[0].shape[1])
    return pl.pallas_call(
        out_grads_kernel,
        in_specs=[whole(a) for a in (d_branch, *parts)],
        out_specs=[whole(out)] * 4,
        out_shape=[out] * 4,
        name="out_weight_grads",
        **settings(16),
    )(d_branch, *parts)


def qkv_grads_kernel(count, bit_ref, *refs):
    x_refs = refs[0:8]
    d_ref, w_ref, kept_ref, sent_ref, gain_ref, total = refs[8:]
    number = pl.program_id(0)
    block = jnp.concatenate([chosen(number, x_refs[j::4]) for j in range(4)], axis=0)
    part = product(block, d_ref[...], TN)

    @pl.when(number == 0)
    def _():
        total[...] = part

    @pl.when(number > 0)
    def _():
        total[...] += part

    @pl.when(number == 1)
    def _():
        part_rows(count, bit_ref[0], (total,), kept_ref, sent_ref)
        gain_ref[...] = row_sums(total[...] * w_ref[...].astype(jnp.float32).T)


def qkv_grads(attn_ins, d_qkv, w_qkv):
    rows, model = attn_ins[0].shape
    width = d_qkv.shape[1]
    count = lax.axis_size("dp")
    bit = lax.axis_index("dp") % 2
    kept = far_shape(count // 2, model // count, width, dtype=jnp.float32)
    sent = far_shape(*kept.shape)
    gain = shape(1, model, dtype=jnp.float32)
    return pl.pallas_call(
        partial(qkv_grads_kernel, count),
        grid_spec=pltpu.PrefetchScalarGridSpec(
            num_scalar_prefetch=1,
            grid=(2,),
            in_specs=[whole(x) for x in attn_ins]
            + [pl.BlockSpec((4 * rows, width), lambda i, _: (i, 0)), whole(w_qkv)],
            out_specs=[whole(kept), whole(sent), whole(gain)],
            scratch_shapes=[pltpu.VMEM((model, width), jnp.float32)],
        ),
        out_shape=[kept, sent, gain],
        name="qkv_grads",
        **settings(24),
    )(bit[None], *attn_ins, d_qkv, w_qkv)


def unproject_kernel(d_ref, w_ref, *out_refs):
    part = low(product(d_ref[...], w_ref[...]))
    for number in range(2):

        @pl.when(pl.program_id(0) == number)
        def _():
            out_refs[number][...] = part


def unproject(d_qkv, w_qkv, base):
    rows = d_qkv.shape[0] // 4
    out = far_shape(rows, w_qkv.shape[1])
    return pl.pallas_call(
        unproject_kernel,
        grid=(2,),
        in_specs=[
            pl.BlockSpec((rows, d_qkv.shape[1]), lambda i: (base + i, 0)),
            whole(w_qkv),
        ],
        out_specs=[whole(out), whole(out)],
        out_shape=[out, out],
        name="unproject",
        **settings(16),
    )(d_qkv, w_qkv)


def parted(total, distance):
    bit = (lax.axis_index("dp") // distance) % 2
    total = total.reshape(-1, 2, *total.shape[1:])
    return (
        lax.dynamic_index_in_dim(total, bit, 1, keepdims=False),
        low(lax.dynamic_index_in_dim(total, 1 - bit, 1, keepdims=False)),
    )


def halve(kept, got, distance):
    bit = (lax.axis_index("dp") // distance) % 2
    kept = kept.reshape(-1, 2, *kept.shape[1:])
    got = got.reshape(kept.shape)

    def side(number):
        return add(
            lax.dynamic_index_in_dim(kept, number, 1, keepdims=False),
            lax.dynamic_index_in_dim(got, number, 1, keepdims=False),
        )

    return side(bit), low(side(1 - bit))


def to_last(kept, sent, distance):
    while True:
        got = swap(sent, distance, "dp")
        distance *= 2
        if distance >= lax.axis_size("dp"):
            return kept[0], got[0]
        kept, sent = halve(kept, got, distance)


def sum_steps(value, axis, first=1):
    distance = first
    while distance < lax.axis_size(axis):
        value = value + swap(value, distance, axis)
        distance *= 2
    return value


def on_device(tokens, patch_side, gain_attn, w_qkv, w_out, gain_mlp, w_up, w_down, cotangent):
    rows, model = tokens.shape
    place = lax.axis_index("tp")
    group_rows = 4 * rows
    heads = w_out.shape[0] // HD

    own_0 = norm(tokens, gain_attn, 0)
    own_1 = norm(after(tokens, own_0), gain_attn, 1)
    across_0, across_1 = swap(own_0, 2), swap(own_1, 2)
    pair_0, pair_1 = swap(own_0, 1), swap(own_1, 1)

    cells = (IMAGE // patch_side[0]) ** 2
    full = group_rows // cells
    order = place ^ jnp.arange(4, dtype=jnp.int32)
    positions = (order[:, None] * rows + jnp.arange(rows, dtype=jnp.int32)).reshape(-1)
    image_id = jnp.minimum(positions // cells, full)
    first_id = jnp.minimum(order * rows // cells, full)
    last_id = jnp.minimum((order * rows + rows - 1) // cells, full)
    first_block = first_id * cells // rows
    stop = jnp.where(last_id == full, group_rows, (last_id + 1) * cells)
    last_block = (stop + rows - 1) // rows
    plan = plan_of(place, order, rows, cells)
    bounds = jnp.concatenate(
        [place[None], jnp.stack([first_block, last_block], axis=1).reshape(-1)]
    )

    turned_qkv = w_qkv.T
    by_head = turned_qkv.reshape(heads, 3, HD, model)
    by_head = by_head * jnp.array([0.125, 1.0, 1.0], jnp.bfloat16)[:, None, None]
    spread = jnp.pad(by_head.transpose(1, 0, 2, 3), ((0, 0), (0, 0), (0, LANES - HD), (0, 0)))
    spread = spread.reshape(3 * heads * LANES, model)
    qkv = project([own_0, own_1, pair_0, pair_1], spread, (0, 1, 2, 3), None)
    across_0, qkv = join(across_0, qkv)
    diagonal_0 = swap(across_0, 1)
    qkv = project([across_0, diagonal_0], spread, (4, 6), qkv)
    across_1, qkv = join(across_1, qkv)
    diagonal_1 = swap(across_1, 1)
    qkv = project([across_1], spread, (5,), qkv)
    diagonal_1, qkv = join(diagonal_1, qkv)
    qkv = project([diagonal_1], spread, (7,), qkv)
    attn_ins = [own_0, own_1, pair_0, pair_1, across_0, across_1, diagonal_0, diagonal_1]

    middle = rows // 2
    w_pair = swap(after(w_out, across_1), 1)
    grads_pair = swap(after(cotangent, across_1), 1)
    mixed_in = jnp.concatenate([cotangent[:middle], w_out], axis=0)
    in_across = swap(after(mixed_in, across_1), 2)
    far = attend(qkv, image_id, plan, heads, 2)
    *far, w_pair, grads_pair = join(*far, w_pair, grads_pair)
    out_2, out_3, logs_far = far
    got_2, got_3 = swap(out_2, 2), swap(out_3, 3)
    grads_1 = swap(after(cotangent[middle:], out_2), 2)
    near = attend(after(qkv, out_2), image_id, plan, heads, 0)
    *near, got_2, got_3, in_across = join(*near, got_2, got_3, in_across)
    in_diagonal = swap(in_across, 1)
    out_0, out_1, logs_near = near
    got_1 = swap(out_1, 1)
    mine = [out_0, got_1, got_2, got_3]
    w_outs = [w_out, w_pair, in_across, in_diagonal]
    resid, *mlp_in = branch(mine, w_outs, tokens, gain_mlp)

    pairs = [swap(m, 1) for m in mlp_in]
    pairs[0], grads_1 = join(pairs[0], grads_1)
    grads_1_diagonal = swap(grads_1, 1)
    across_0 = swap(mlp_in[0], 2)
    own_0, y_0, pair_0, *near = mlp(
        mlp_in[0], pairs[0], cotangent, grads_pair, 0, 0, w_up, w_down, None, True
    )
    own_1, y_1, pair_1, *near = mlp(
        mlp_in[1], pairs[1], cotangent, grads_pair, 1, 1, w_up, w_down, near, True
    )
    across_0, own_1, pair_0, pair_1, grads_1_diagonal = join(
        across_0, own_1, pair_0, pair_1, grads_1_diagonal
    )
    across_1 = swap(after(mlp_in[1], across_0), 2)
    diagonal_0, pair_0, pair_1 = join(swap(across_0, 1), swap(pair_0, 1), swap(pair_1, 1))
    m_2, y_20, m_3, y_30, *kept = mlp(
        across_0, diagonal_0, in_across, in_diagonal, 0, 0, w_up, w_down, None, False
    )
    across_1, m_2, y_30 = join(across_1, m_2, swap(y_30, 1))
    far_0 = low(add(m_2, swap(m_3, 1)))
    diagonal_1 = swap(across_1, 1)
    m_2, y_21, m_3, y_31, *kept = mlp(
        across_1, diagonal_1, grads_1, grads_1_diagonal, 0, 1, w_up, w_down, kept, False
    )
    sums = mlp_grads(
        after(near[0], m_2),
        near[1],
        (mlp_in[0], pairs[0], mlp_in[1], pairs[1]),
        ((0, cotangent), (0, grads_pair), (1, cotangent), (1, grads_pair)),
        w_up,
        None,
    )
    far_0, m_2, y_31, *sums = join(swap(far_0, 2), m_2, swap(y_31, 1), *sums)
    far_1 = low(add(m_2, swap(m_3, 1)))
    kept_mlp, sent_mlp, gain_mlp_part = mlp_grads(
        after(kept[0], far_1),
        kept[1],
        (across_0, diagonal_0, across_1, diagonal_1),
        ((0, in_across), (0, in_diagonal), (0, grads_1), (0, grads_1_diagonal)),
        w_up,
        sums,
    )
    mixed_far = [low(add(after(y_20, sent_mlp), y_30)), low(add(after(y_21, sent_mlp), y_31))]
    mixed_far, kept_mlp, sent_mlp, far_1 = join(
        jnp.concatenate(mixed_far, axis=0), kept_mlp, sent_mlp, swap(far_1, 2)
    )

    d_resid, d_branch, *d_pieces = branch_back(
        (own_0, own_1), (pair_0, pair_1), (far_0, far_1), cotangent, resid, gain_mlp, w_outs
    )
    d_1, d_2, d_3 = [swap(d_pieces[j], j) for j in range(1, 4)]
    d_outs = out_weight_grads(after(d_branch, d_pieces[0]), mine)
    out_far = low(add(d_outs[2], swap(d_outs[3], 1)))
    back = attend_back(
        after(qkv, out_far),
        (d_pieces[0], d_1),
        (out_0, out_1),
        logs_near,
        image_id,
        bounds,
        heads,
        0,
        (),
    )
    *back, got_mlp, d_2, d_3, out_far = join(
        *back, swap(sent_mlp, 1, "dp"), d_2, d_3, swap(out_far, 2)
    )
    count = lax.axis_size("dp")
    out_pair = swap(after(d_outs[1], back[0]), 1)
    kept_mlp, sent_mlp = halve(kept_mlp, got_mlp, 2)
    d_out = add(d_outs[0], out_pair) + out_far.astype(jnp.float32)
    kept_out, sent_out = parted(d_out.reshape(count, model // count, -1), 1)
    d_qkv = attend_back(
        after(qkv, sent_out, sent_mlp),
        (d_2, d_3),
        (out_2, out_3),
        logs_far,
        image_id,
        bounds,
        heads,
        2,
        back,
    )
    kept_mlp, got_mlp = to_last(kept_mlp, sent_mlp, 2)
    d_qkv, got_out, mixed_far = join(
        d_qkv, swap(sent_out, 1, "dp"), swap(after(mixed_far, sent_out), 2)
    )

    kept, sent, gain_attn_part = qkv_grads(attn_ins, d_qkv, turned_qkv)
    part_2, part_3, kept_mlp, got_mlp = join(
        *unproject(after(d_qkv, sent), turned_qkv, 2), kept_mlp, got_mlp
    )
    grad_mlp = low(add(kept_mlp, got_mlp))
    gains = jnp.concatenate(
        [gain_attn_part / gain_attn[None, :], gain_mlp_part / gain_mlp[None, :]], axis=0
    )
    gains, part_3, part_0, part_1 = join(
        gains + swap(gains, 1),
        swap(part_3, 1),
        *unproject(after(d_qkv, part_2, grad_mlp), turned_qkv, 0),
    )
    d_far = low(add(part_2, part_3))
    pair = swap(part_1, 1)
    kept_out, got_out = to_last(*halve(kept_out, got_out, 2), 2)
    gains = sum_steps(gains, "tp", 2)
    d_far = after(d_far, gains)
    got, gains, kept_out, got_out = join(swap(sent, 1, "dp"), gains, kept_out, got_out)

    kept, sent = halve(kept, got, 2)
    far = swap(d_far, 2)
    gains = sum_steps(gains, "grp")
    kept, got, gains, pair, got_mlp = join(
        *to_last(kept, sent, 2),
        gains + swap(gains, 1, "dp"),
        pair,
        swap(grad_mlp, 1, "grp"),
    )
    grad_rest = jnp.concatenate([low(add(kept, got)), low(add(kept_out, got_out))], axis=1)
    grad_mlp = add(grad_mlp, got_mlp)
    mixed_near = jnp.concatenate(
        [add(y_0, pair_0[middle:]), add(y_1, pair_1[middle:])], axis=0
    )
    mixed_rows = low(resid + (mixed_near + mixed_far.astype(jnp.float32)))
    input_grad = norm_back(tokens, gain_attn, part_0, pair, far, d_resid)
    got, gains, input_grad = join(
        swap(grad_rest, 1, "grp"), sum_steps(gains, "dp", 2), input_grad
    )
    grad_rest = add(grad_rest, got)
    width = w_qkv.shape[1]
    hidden = w_up.shape[1]
    return (
        mixed_rows,
        input_grad,
        gains[0],
        grad_rest[:, :width],
        grad_rest[:, width:].T,
        gains[1],
        grad_mlp[:, :hidden],
        grad_mlp[:, hidden:].T,
    )


def solution(mesh):
    in_specs = (
        P(("grp", "dp", "tp"), None),
        P(("grp", "dp")),
        P(),
        P(None, "tp"),
        P("tp", None),
        P(),
        P(None, "tp"),
        P("tp", None),
        P(("grp", "dp", "tp"), None),
    )
    out_specs = (
        P(("grp", "dp", "tp"), None),
        P(("grp", "dp", "tp"), None),
        P(),
        P("dp", "tp"),
        P("tp", "dp"),
        P(),
        P("dp", "tp"),
        P("tp", "dp"),
    )
    return jax.shard_map(
        on_device, mesh=mesh, in_specs=in_specs, out_specs=out_specs, check_vma=False
    )
```

```python
from functools import partial

import jax
import jax.numpy as jnp
from jax import lax
from jax.experimental import pallas as pl
from jax.experimental.pallas import tpu as pltpu
from jax.sharding import PartitionSpec as P

HD = 64
LANES = 128
IMAGE = 240
EXCLUDED = -1e30
MIB = 1024 * 1024
NT = (((1,), (1,)), ((), ()))
TN = (((0,), (0,)), ((), ()))

epsilon = 1e-06


def normalize(values, scaling):
    centred = values - jnp.mean(values, axis=1, keepdims=True)
    inverse = lax.rsqrt(jnp.mean(centred * centred, axis=1, keepdims=True) + epsilon)
    normed = centred * inverse
    return (normed * scaling, normed, inverse)


def restore(d_normed, normed, inverse, scaling):
    d_scaled = d_normed * scaling
    return inverse * (
        d_scaled
        - jnp.mean(d_scaled, axis=1, keepdims=True)
        - normed * jnp.mean(d_scaled * normed, axis=1, keepdims=True)
    )


def swap(value, distance, axis="tp"):
    size = lax.axis_size(axis)
    return lax.ppermute(value, axis, [(i, i ^ distance) for i in range(size)])


def after(value, *earlier):
    return lax.optimization_barrier((value, *earlier))[0]


def join(*values):
    return lax.optimization_barrier(values)


def add(left, right):
    return left.astype(jnp.float32) + right.astype(jnp.float32)


def product(left, right, dims=(((1,), (0,)), ((), ()))):
    return lax.dot_general(left, right, dims, preferred_element_type=jnp.float32)


def low(value):
    return value.astype(jnp.bfloat16)


def settings(limit, microseconds=0.1):
    return dict(
        compiler_params=pltpu.CompilerParams(vmem_limit_bytes=limit * MIB),
        cost_estimate=pl.CostEstimate(
            flops=int(microseconds * 1.1e9), bytes_accessed=MIB, transcendentals=0
        ),
    )


def whole(array):
    return pl.BlockSpec(array.shape, lambda *_: (0,) * len(array.shape))


def shape(*dims, dtype=jnp.bfloat16):
    return jax.ShapeDtypeStruct(dims, dtype)


def far_shape(*dims, dtype=jnp.bfloat16):
    return pltpu.HBM(dims, dtype)


def left(array):
    return pltpu.with_memory_space_constraint(array, pltpu.HBM)


def chosen(number, refs):
    value = refs[0][...]
    for other in range(1, len(refs)):
        value = jnp.where(number == other, refs[other][...], value)
    return value


def norm_kernel(x_ref, gain_ref, out_ref):
    out_ref[...] = low(normalize(x_ref[...].astype(jnp.float32), gain_ref[...])[0])


def norm(tokens, gain, half):
    rows, model = tokens.shape
    return pl.pallas_call(
        norm_kernel,
        grid=(1,),
        in_specs=[pl.BlockSpec((rows // 2, model), lambda i: (half, 0)), whole(gain)],
        out_specs=pl.BlockSpec((rows // 2, model), lambda i: (0, 0)),
        out_shape=far_shape(rows // 2, model),
        name="norm",
        **settings(8, 2),
    )(left(tokens), left(gain))


def norm_back_kernel(x_ref, gain_ref, own_ref, pair_ref, far_ref, d_ref, out_ref):
    d_normed = add(own_ref[...], pair_ref[...]) + far_ref[...].astype(jnp.float32)
    _, unit, inverse = normalize(x_ref[...].astype(jnp.float32), gain_ref[...])
    out_ref[...] = d_ref[...] + restore(d_normed, unit, inverse, gain_ref[...])


def norm_back(tokens, gain, own, pair, far, d_resid):
    rows, model = tokens.shape
    tile = pl.BlockSpec((rows // 2, model), lambda i: (i, 0))
    return pl.pallas_call(
        norm_back_kernel,
        grid=(2,),
        in_specs=[tile, whole(gain)] + [tile] * 4,
        out_specs=tile,
        out_shape=shape(rows, model, dtype=jnp.float32),
        name="norm_back",
        **settings(16, 2),
    )(tokens, gain, own, pair, far, d_resid)


def project_kernel(count, *refs):
    out_ref = refs[-1]
    out_ref[...] = low(product(chosen(pl.program_id(0), refs[:count]), refs[count][...], NT))


def project(blocks, weights, places, earlier):
    rows = blocks[0].shape[0]
    wide = weights.shape[0]
    count = len(blocks)
    group_rows = rows * 8 if earlier is None else earlier.shape[0]
    extra = [] if earlier is None else [earlier]
    return pl.pallas_call(
        partial(project_kernel, count),
        grid=(count,),
        in_specs=[whole(x) for x in blocks]
        + [whole(weights)]
        + [pl.BlockSpec(memory_space=pl.ANY)] * len(extra),
        out_specs=pl.BlockSpec(
            (rows, wide), lambda i: (places[0] + i * (places[-1] - places[0]) // max(count - 1, 1), 0)
        ),
        out_shape=shape(group_rows, wide),
        input_output_aliases={count + 1: 0} if extra else {},
        name="project",
        **settings(16),
    )(*blocks, weights, *extra)


def tiles_of(bounds_ref, base):
    where = 1 + 2 * base
    first, second = bounds_ref[where], bounds_ref[where + 2]
    count = bounds_ref[where + 1] - first
    total = count + bounds_ref[where + 3] - second

    def tile(number):
        late = (number >= count).astype(jnp.int32)
        key = jnp.where(late == 1, second + number - count, first + number)
        key = jnp.minimum(key, bounds_ref[where + 3] - 1 + (1 - late) * 4)
        return late, key ^ bounds_ref[0], number < total

    return tile, total


def block_at(number, width):
    return pl.ds(pl.multiple_of(number * width, width), width)


def mask_of(ids, id_q_ref, query, key, used, width):
    id_q = id_q_ref[:, block_at(query, width)] + jnp.where(used, 0, 1 << 20)
    return jnp.concatenate([ids[block_at(key, width), :]] * (width // LANES), axis=1) == id_q


TILE = 256
MOST = 40


def plan_of(place, order, rows, cells):
    group_rows = 4 * rows
    per = rows // TILE
    full = group_rows // cells
    inside = jnp.arange(per, dtype=jnp.int32) * TILE
    first = (order[:, None] * rows + inside).reshape(2, 1, 2 * per)
    first_id = jnp.minimum(first // cells, full)
    last_id = jnp.minimum((first + TILE - 1) // cells, full)
    low_key = first_id * cells // TILE
    stop = jnp.where(last_id == full, group_rows, (last_id + 1) * cells)
    turn = jnp.arange(4 * per, dtype=jnp.int32)[None, :, None]
    key = low_key + turn
    used = (key * TILE < stop).reshape(2, -1)
    key = ((key // per) ^ place) * per + key % per
    code = (key + 64 * jnp.arange(2 * per, dtype=jnp.int32)).reshape(2, -1)
    number = jnp.cumsum(used.astype(jnp.int32), axis=1)
    wanted = jnp.arange(1, MOST + 1, dtype=jnp.int32)[None, :, None]
    chosen = used[:, None, :] & (number[:, None, :] == wanted)
    listed = jnp.sum(jnp.where(chosen, code[:, None, :], 0), axis=2)
    return jnp.concatenate([number[:, -1:], listed], axis=1)


def tile_of(plan_ref, base, number):
    code = plan_ref[base // 2, 1 + number]
    return code // 64, code % 64, number < plan_ref[base // 2, 0]


def tile_at(number):
    return pl.ds(pl.multiple_of(number * TILE, TILE), TILE)


def tile_mask(ids, id_q_ref, query, key, used):
    id_q = id_q_ref[:, tile_at(query)] + jnp.where(used, 0, 1 << 20)
    return jnp.concatenate([ids[tile_at(key), :]] * (TILE // LANES), axis=1) == id_q


def in_turn(total, prepare, absorb):
    for number in range(2):
        prepare(number, 0, number)

    def step(number, carry):
        for side in range(2):
            for part in range(2):
                prepare(4 * number + 2 * side + 2 + part, 1 - side, part)
            for part in range(2):
                absorb(4 * number + 2 * side + part, side, part)
        return carry

    lax.fori_loop(0, (total + 3) // 4, step, 0)


def attend_kernel(heads, base, plan_ref, q_ref, k_ref, v_ref, id_q_ref, id_k_ref, *refs):
    out_refs = refs[:2]
    log_ref, turned, ids, scores_a, scores_b, tops, totals = refs[2:]
    scores_refs = (scores_a, scores_b)
    width = q_ref.shape[0] // 2
    for h in range(heads):
        value = v_ref[:, h * LANES : (h + 1) * LANES].astype(jnp.float32).T
        turned[h, :HD] = low(value[:HD])
        turned[h, HD:] = jnp.ones((turned.shape[1] - HD, v_ref.shape[0]), jnp.bfloat16)
    ids[...] = jnp.broadcast_to(id_k_ref[...], ids.shape)
    tops[...] = jnp.full(tops.shape, EXCLUDED, jnp.float32)
    totals[...] = jnp.zeros_like(totals)

    def prepare(number, side, part):
        query, key, _ = tile_of(plan_ref, base, number)
        for h in range(heads):
            columns = slice(h * LANES, (h + 1) * LANES)
            scores_refs[side][part, h] = product(
                k_ref[tile_at(key), columns], q_ref[tile_at(query), columns], NT
            )

    def absorb(number, side, part):
        query, key, used = tile_of(plan_ref, base, number)
        mask = tile_mask(ids, id_q_ref, query, key, used)
        for h in range(heads):
            scores = jnp.where(mask, scores_refs[side][part, h], EXCLUDED)
            largest = tops[query, h]
            top = jnp.maximum(largest, jnp.max(scores, axis=0, keepdims=True))
            exponent = low(jnp.exp(scores - top))
            tops[query, h] = top
            totals[query, h] = totals[query, h] * jnp.exp(largest - top) + product(
                turned[h, :, tile_at(key)], exponent
            )

    in_turn(plan_ref[base // 2, 0], prepare, absorb)
    for query in range(tops.shape[0]):
        block, at = divmod(query * TILE, width)
        for h in range(heads):
            sums = totals[query, h]
            denominator = sums[HD : HD + 1]
            out_refs[block][at : at + TILE, h * HD : (h + 1) * HD] = low(
                (sums[:HD] / denominator).T
            )
            log_ref[h : h + 1, query * TILE : (query + 1) * TILE] = tops[query, h] + jnp.log(
                denominator
            )


def attend(qkv, image_id, plan, heads, base):
    rows = qkv.shape[0]
    wide = heads * LANES
    width = rows // 4
    out = far_shape(width, heads * HD)
    log = far_shape(heads, 2 * width, dtype=jnp.float32)
    return pl.pallas_call(
        partial(attend_kernel, heads, base),
        grid_spec=pltpu.PrefetchScalarGridSpec(
            num_scalar_prefetch=1,
            grid=(1,),
            in_specs=[
                pl.BlockSpec((2 * width, wide), lambda i, _: (base // 2, 0)),
                pl.BlockSpec((rows, wide), lambda i, _: (0, 1)),
                pl.BlockSpec((rows, wide), lambda i, _: (0, 2)),
                pl.BlockSpec((1, 2 * width), lambda i, _: (0, base // 2)),
                pl.BlockSpec((rows, 1), lambda i, _: (0, 0)),
            ],
            out_specs=[whole(out), whole(out), whole(log)],
            scratch_shapes=[
                pltpu.VMEM((heads, HD + 16, rows), jnp.bfloat16),
                pltpu.VMEM((rows, LANES), jnp.int32),
                pltpu.VMEM((2, heads, TILE, TILE), jnp.float32),
                pltpu.VMEM((2, heads, TILE, TILE), jnp.float32),
                pltpu.VMEM((2 * width // TILE, heads, 1, TILE), jnp.float32),
                pltpu.VMEM((2 * width // TILE, heads, HD + 16, TILE), jnp.float32),
            ],
        ),
        out_shape=[out, out, log],
        name="attend",
        **settings(32, 14 if base else 0.1),
    )(plan, *[qkv] * 3, image_id[None, :], image_id[:, None])


def attend_back_kernel(heads, base, bounds_ref, q_ref, k_ref, v_ref, *refs):
    grad_refs = refs[0:2]
    out_refs = refs[2:4]
    log_ref, id_q_ref, id_k_ref = refs[4:7]
    if base == 0:
        d_q_ref, partial_ref = refs[7:9]
    else:
        near_q_ref, near_sums_ref, d_ref = refs[7:10]
    sums = refs[-1]
    first = 9 if base == 0 else 10
    turned, ids, grads, placed, inner, d_q = refs[first : first + 6]
    width = q_ref.shape[0] // 2
    tile, total = tiles_of(bounds_ref, base)
    for h in range(heads):
        key = k_ref[:, h * LANES : (h + 1) * LANES].astype(jnp.float32).T
        turned[h] = low(key[:HD])
    ids[...] = jnp.broadcast_to(id_k_ref[...], ids.shape)
    d_q[...] = jnp.zeros_like(d_q)
    if base == 0:
        sums[...] = jnp.zeros_like(sums)
    else:
        sums[...] = near_sums_ref[...].astype(jnp.float32)
    ones = jnp.ones((8, HD), jnp.float32)
    none = jnp.zeros((width, HD), jnp.bfloat16)
    for query in range(2):
        for h in range(heads):
            grad = grad_refs[query][:, h * HD : (h + 1) * HD]
            grads[query, h] = jnp.concatenate([grad, none], axis=1)
            placed[query, h] = jnp.concatenate([none, grad], axis=1)
            terms = grad.astype(jnp.float32) * out_refs[query][
                :, h * HD : (h + 1) * HD
            ].astype(jnp.float32)
            inner[query, h] = lax.dot_general(
                ones,
                terms,
                NT,
                precision=lax.Precision.HIGHEST,
                preferred_element_type=jnp.float32,
            )[:1]

    def absorb(number):
        query, key, used = tile(number)
        at = block_at(key, width)
        mask = mask_of(ids, id_q_ref, query, key, used, width)
        for h in range(heads):
            columns = slice(h * LANES, (h + 1) * LANES)
            logs = log_ref[h : h + 1, block_at(query, width)]
            queries = q_ref[block_at(query, width), columns]
            scores = product(k_ref[at, columns], queries, NT)
            d_probs = product(v_ref[at, columns], grads[query, h], NT)
            probs = jnp.where(mask, jnp.exp(scores - logs), 0.0)
            d_scores = low(probs * (d_probs - inner[query, h]))
            sums[at, columns] += product(low(probs), placed[query, h]) + product(d_scores, queries)
            d_q[query, h] += product(turned[h, :, at], d_scores)

    def step(number, carry):
        absorb(number)
        return carry

    lax.fori_loop(0, total, step, 0)
    for query in range(2):
        for h in range(heads):
            part = low((d_q[query, h] * 0.125).T)
            if base == 0:
                d_q_ref[query * width : (query + 1) * width, h * HD : (h + 1) * HD] = part
            else:
                here = slice((base + query) * width, (base + query + 1) * width)
                d_ref[here, 3 * h * HD : (3 * h + 1) * HD] = part
    if base == 0:
        partial_ref[...] = low(sums[...])
    else:
        for h in range(heads):
            d_ref[: 2 * width, 3 * h * HD : (3 * h + 1) * HD] = near_q_ref[
                :, h * HD : (h + 1) * HD
            ]
            d_ref[:, (3 * h + 1) * HD : (3 * h + 3) * HD] = low(
                sums[:, h * LANES : (h + 1) * LANES]
            )


def attend_back(qkv, d_heads, heads_out, log_total, image_id, bounds, heads, base, near):
    rows = qkv.shape[0]
    wide = heads * LANES
    width = rows // 4
    sums = far_shape(rows, wide)
    near = list(near)
    if base == 0:
        outs = [far_shape(2 * width, heads * HD), sums]
    else:
        outs = [shape(rows, 3 * heads * HD)]
    padded = pltpu.VMEM((2, heads, width, LANES), jnp.bfloat16)
    result = pl.pallas_call(
        partial(attend_back_kernel, heads, base),
        grid_spec=pltpu.PrefetchScalarGridSpec(
            num_scalar_prefetch=1,
            grid=(1,),
            in_specs=[
                pl.BlockSpec((2 * width, wide), lambda i, _: (base // 2, 0)),
                pl.BlockSpec((rows, wide), lambda i, _: (0, 1)),
                pl.BlockSpec((rows, wide), lambda i, _: (0, 2)),
            ]
            + [whole(a) for a in (*d_heads, *heads_out, log_total)]
            + [
                pl.BlockSpec((1, 2 * width), lambda i, _: (0, base // 2)),
                pl.BlockSpec((rows, 1), lambda i, _: (0, 0)),
            ]
            + [whole(a) for a in near],
            out_specs=[whole(a) for a in outs],
            scratch_shapes=[
                pltpu.VMEM((heads, HD, rows), jnp.bfloat16),
                pltpu.VMEM((rows, LANES), jnp.int32),
                padded,
                padded,
                pltpu.VMEM((2, heads, 1, width), jnp.float32),
                pltpu.VMEM((2, heads, HD, width), jnp.float32),
            ]
            + [pltpu.VMEM((rows, wide), jnp.float32)],
        ),
        out_shape=outs,
        name="attend_back",
        **settings(36, 20 if base else 3),
    )(
        bounds,
        *[left(qkv)] * 3,
        *d_heads,
        *heads_out,
        log_total,
        image_id[None, :],
        image_id[:, None],
        *(left(a) for a in near),
    )
    return result[0] if near else result


def last_rows(refs, number):
    size = refs[number].shape[0]
    return refs[number][size - refs[0].shape[0] :, :]


def branch_kernel(*refs):
    parts = refs[0:4]
    weights = refs[4:8]
    tokens_ref, gain_ref, resid_ref, in_0_ref, in_1_ref = refs[8:]
    resid = tokens_ref[...].astype(jnp.float32)
    branch = product(parts[0][...], last_rows(weights, 0))
    for j in range(1, 4):
        branch = branch + product(parts[j][...], last_rows(weights, j))
    resid = resid + branch
    resid_ref[...] = resid
    normed = low(normalize(resid, gain_ref[...])[0])
    for half, in_ref in enumerate((in_0_ref, in_1_ref)):

        @pl.when(pl.program_id(0) == half)
        def _():
            in_ref[...] = normed


def branch(parts, weights, tokens, gain):
    rows, model = tokens.shape
    operands = (*parts, *weights, tokens, gain)
    half = far_shape(rows // 2, model)
    resid = far_shape(rows, model, dtype=jnp.float32)

    def halves(array):
        return pl.BlockSpec((rows // 2, array.shape[1]), lambda i: (i, 0))

    specs = [whole(a) for a in operands]
    specs[:4] = [halves(p) for p in parts]
    specs[8] = halves(tokens)
    return pl.pallas_call(
        branch_kernel,
        grid=(2,),
        in_specs=specs,
        out_specs=[halves(resid), whole(half), whole(half)],
        out_shape=[resid, half, half],
        name="branch",
        **settings(16),
    )(*operands)


def mlp_kernel(together, x_a_ref, x_b_ref, g_a_ref, g_b_ref, up_ref, down_ref, *refs):
    act_ref, d_pre_ref = refs[-2:]
    length = x_a_ref.shape[0]
    if together:
        m_a_ref, y_a_ref, both_ref = refs[-5:-2]
        m_b_ref, y_b_ref = both_ref.at[:length], both_ref.at[length:]
    else:
        m_a_ref, y_a_ref, m_b_ref, y_b_ref = refs[-6:-2]

    number = pl.program_id(0)
    mlp_in = chosen(number, (x_b_ref, x_a_ref))
    out_grads = chosen(number, (g_b_ref, g_a_ref))
    pre_act = product(mlp_in, up_ref[...])
    d_act = product(out_grads, down_ref[...], NT)
    below = 0.5 + 0.5 * lax.erf(pre_act * 0.7071067811865476)
    density = 0.3989422804014327 * jnp.exp(-0.5 * pre_act * pre_act)
    d_pre = low(d_act * (below + pre_act * density))
    act = low(pre_act * below)
    m = low(product(d_pre, up_ref[...], NT))
    y = low(product(act, down_ref[...]))
    act_ref[...] = act
    d_pre_ref[...] = d_pre
    for block, (m_ref, y_ref) in enumerate(((m_b_ref, y_b_ref), (m_a_ref, y_a_ref))):

        @pl.when(number == block)
        def _():
            m_ref[...] = m
            y_ref[...] = y


def mlp(x_a, x_b, g_a, g_b, half, place, w_up, w_down, earlier, near):
    length, model = x_a.shape
    hidden = w_up.shape[1]
    extra = [] if earlier is None else list(earlier)

    def grads():
        return pl.BlockSpec((length, model), lambda i: (half, 0))

    def kept(width):
        return pl.BlockSpec((length, width), lambda i: (2 * place + 1 - i, 0))

    one = far_shape(length, model)
    outs = [one, one, far_shape(2 * length, model)] if near else [one] * 4
    return pl.pallas_call(
        partial(mlp_kernel, near),
        grid=(2,),
        in_specs=[whole(x_a), whole(x_b), grads(), grads(), whole(w_up), whole(w_down)]
        + [pl.BlockSpec(memory_space=pl.ANY)] * len(extra),
        out_specs=[whole(a) for a in outs] + [kept(hidden)] * 2,
        out_shape=outs
        + [far_shape(4 * length, hidden)] * 2,
        input_output_aliases={6 + i: len(outs) + i for i in range(len(extra))},
        name="mlp",
        **settings(20),
    )(x_a, x_b, g_a, g_b, w_up, w_down, *extra)


def part_rows(count, bit, totals, kept_ref, sent_ref):
    share = totals[0].shape[0] // count
    for pair in range(count // 2):
        for side, ref in ((bit, kept_ref), (1 - bit, sent_ref)):
            at = pl.ds(pl.multiple_of((2 * pair + side) * share, 8), share)
            first = 0
            for total in totals:
                width = min(total.shape[1], ref.shape[2] - first)
                ref[pair, :, first : first + width] = total[at, :width].astype(ref.dtype)
                first += width


def row_sums(values):
    sums = jnp.sum(values, axis=1, keepdims=True)
    return jnp.broadcast_to(sums, (values.shape[0], LANES)).T[:1]


def mlp_grads_kernel(count, bit_ref, act_ref, d_pre_ref, *refs):
    number = pl.program_id(0)
    x_refs, g_refs = refs[0:4], refs[4:8]
    if count:
        up_ref, old_up_ref, old_down_ref, kept_ref, sent_ref, gain_ref, d_up, d_down = refs[8:]
    else:
        d_up, d_down = refs[8:]

    @pl.when(number == 0)
    def _():
        if count:
            d_up[...] = old_up_ref[...]
            d_down[...] = old_down_ref[...]
        else:
            d_up[...] = jnp.zeros_like(d_up)
            d_down[...] = jnp.zeros_like(d_down)

    x = jnp.concatenate([chosen(number, x_refs[j::2]) for j in range(2)], axis=0)
    d_up[...] += product(x, d_pre_ref[...], TN)
    grads = jnp.concatenate([chosen(number, g_refs[j::2]) for j in range(2)], axis=0)
    d_down[...] += product(grads, act_ref[...], TN)

    @pl.when(number == 1)
    def _():
        if count:
            part_rows(count, bit_ref[0], (d_up, d_down), kept_ref, sent_ref)
            gain_ref[...] = row_sums(d_up[...] * up_ref[...].astype(jnp.float32))


def mlp_grads(act, d_pre, blocks, grads, w_up, earlier):
    rows, hidden = act.shape
    model = blocks[0].shape[1]
    tile = rows // 4
    count = lax.axis_size("dp")
    bit = lax.axis_index("dp") % 2
    total = shape(model, hidden, dtype=jnp.float32)
    kept = far_shape(count // 2, model // count, 2 * hidden, dtype=jnp.float32)
    sent = far_shape(*kept.shape)
    gain = shape(1, model, dtype=jnp.float32)
    extra = [] if earlier is None else [w_up, *earlier]
    outs = [kept, sent, gain] if extra else [total, total]

    def half(rows, columns):
        return pl.BlockSpec((rows, columns), lambda i, _: (i, 0))

    return pl.pallas_call(
        partial(mlp_grads_kernel, count if extra else 0),
        grid_spec=pltpu.PrefetchScalarGridSpec(
            num_scalar_prefetch=1,
            grid=(2,),
            in_specs=[half(2 * tile, hidden)] * 2
            + [whole(a) for a in blocks]
            + [
                pl.BlockSpec((tile, model), lambda i, _, at=at: (at, 0)) for at, _ in grads
            ]
            + [whole(a) for a in extra],
            out_specs=[whole(a) for a in outs],
            scratch_shapes=[pltpu.VMEM((model, hidden), jnp.float32)] * 2 if extra else [],
        ),
        out_shape=outs,
        name="mlp_grads",
        **settings(40),
    )(bit[None], *(left(a) for a in (act, d_pre, *blocks, *(g for _, g in grads))), *extra)


def branch_back_kernel(*refs):
    cotangent_ref, resid_ref, gain_ref = refs[6:9]
    weights = refs[9:13]
    d_resid_ref, d_branch_ref = refs[13:15]
    out_refs = refs[15:19]
    own, pair, far = (chosen(pl.program_id(0), refs[j : j + 2]) for j in (0, 2, 4))
    d_mlp_in = add(own, pair) + far.astype(jnp.float32)
    _, unit, inverse = normalize(resid_ref[...], gain_ref[...])
    d_resid = cotangent_ref[...].astype(jnp.float32) + restore(
        d_mlp_in, unit, inverse, gain_ref[...]
    )
    d_resid_ref[...] = d_resid
    d_branch = low(d_resid)
    d_branch_ref[...] = d_branch
    for j in range(4):
        out_refs[j][...] = low(product(d_branch, last_rows(weights, j), NT))


def branch_back(own, pair, far, cotangent, resid, gain, weights):
    rows, model = resid.shape
    width = weights[0].shape[0]

    def at(columns):
        return pl.BlockSpec((rows // 2, columns), lambda i: (i, 0))

    operands = (*own, *pair, *far, cotangent, resid, gain, *weights)
    specs = [whole(a) for a in operands]
    specs[2] = specs[3] = pl.BlockSpec((rows // 2, model), lambda i: (0, 0))
    specs[6] = specs[7] = at(model)
    return pl.pallas_call(
        branch_back_kernel,
        grid=(2,),
        in_specs=specs,
        out_specs=[at(model), at(model)] + [at(width)] * 4,
        out_shape=[far_shape(rows, model, dtype=jnp.float32), shape(rows, model)]
        + [far_shape(rows, width)] * 4,
        name="branch_back",
        **settings(16),
    )(*(left(a) for a in operands))


def out_grads_kernel(d_ref, *refs):
    for j in range(4):
        refs[4 + j][...] = low(product(d_ref[...], refs[j][...], TN))


def out_weight_grads(d_branch, parts):
    model = d_branch.shape[1]
    out = far_shape(model, parts[0].shape[1])
    return pl.pallas_call(
        out_grads_kernel,
        in_specs=[whole(a) for a in (d_branch, *parts)],
        out_specs=[whole(out)] * 4,
        out_shape=[out] * 4,
        name="out_weight_grads",
        **settings(16),
    )(d_branch, *parts)


def qkv_grads_kernel(count, bit_ref, *refs):
    x_refs = refs[0:8]
    d_ref, w_ref, kept_ref, sent_ref, gain_ref, total = refs[8:]
    number = pl.program_id(0)
    block = jnp.concatenate([chosen(number, x_refs[j::4]) for j in range(4)], axis=0)
    part = product(block, d_ref[...], TN)

    @pl.when(number == 0)
    def _():
        total[...] = part

    @pl.when(number > 0)
    def _():
        total[...] += part

    @pl.when(number == 1)
    def _():
        part_rows(count, bit_ref[0], (total,), kept_ref, sent_ref)
        gain_ref[...] = row_sums(total[...] * w_ref[...].astype(jnp.float32).T)


def qkv_grads(attn_ins, d_qkv, w_qkv):
    rows, model = attn_ins[0].shape
    width = d_qkv.shape[1]
    count = lax.axis_size("dp")
    bit = lax.axis_index("dp") % 2
    kept = far_shape(count // 2, model // count, width, dtype=jnp.float32)
    sent = far_shape(*kept.shape)
    gain = shape(1, model, dtype=jnp.float32)
    return pl.pallas_call(
        partial(qkv_grads_kernel, count),
        grid_spec=pltpu.PrefetchScalarGridSpec(
            num_scalar_prefetch=1,
            grid=(2,),
            in_specs=[whole(x) for x in attn_ins]
            + [pl.BlockSpec((4 * rows, width), lambda i, _: (i, 0)), whole(w_qkv)],
            out_specs=[whole(kept), whole(sent), whole(gain)],
            scratch_shapes=[pltpu.VMEM((model, width), jnp.float32)],
        ),
        out_shape=[kept, sent, gain],
        name="qkv_grads",
        **settings(24),
    )(bit[None], *attn_ins, d_qkv, w_qkv)


def unproject_kernel(d_ref, w_ref, *out_refs):
    part = low(product(d_ref[...], w_ref[...]))
    for number in range(2):

        @pl.when(pl.program_id(0) == number)
        def _():
            out_refs[number][...] = part


def unproject(d_qkv, w_qkv, base):
    rows = d_qkv.shape[0] // 4
    out = far_shape(rows, w_qkv.shape[1])
    return pl.pallas_call(
        unproject_kernel,
        grid=(2,),
        in_specs=[
            pl.BlockSpec((rows, d_qkv.shape[1]), lambda i: (base + i, 0)),
            whole(w_qkv),
        ],
        out_specs=[whole(out), whole(out)],
        out_shape=[out, out],
        name="unproject",
        **settings(16),
    )(d_qkv, w_qkv)


def parted(total, distance):
    bit = (lax.axis_index("dp") // distance) % 2
    total = total.reshape(-1, 2, *total.shape[1:])
    return (
        lax.dynamic_index_in_dim(total, bit, 1, keepdims=False),
        low(lax.dynamic_index_in_dim(total, 1 - bit, 1, keepdims=False)),
    )


def halve(kept, got, distance):
    bit = (lax.axis_index("dp") // distance) % 2
    kept = kept.reshape(-1, 2, *kept.shape[1:])
    got = got.reshape(kept.shape)

    def side(number):
        return add(
            lax.dynamic_index_in_dim(kept, number, 1, keepdims=False),
            lax.dynamic_index_in_dim(got, number, 1, keepdims=False),
        )

    return side(bit), low(side(1 - bit))


def to_last(kept, sent, distance):
    while True:
        got = swap(sent, distance, "dp")
        distance *= 2
        if distance >= lax.axis_size("dp"):
            return kept[0], got[0]
        kept, sent = halve(kept, got, distance)


def sum_steps(value, axis, first=1):
    distance = first
    while distance < lax.axis_size(axis):
        value = value + swap(value, distance, axis)
        distance *= 2
    return value


def on_device(tokens, patch_side, gain_attn, w_qkv, w_out, gain_mlp, w_up, w_down, cotangent):
    rows, model = tokens.shape
    place = lax.axis_index("tp")
    group_rows = 4 * rows
    heads = w_out.shape[0] // HD

    own_0 = norm(tokens, gain_attn, 0)
    own_1 = norm(after(tokens, own_0), gain_attn, 1)
    across_0, across_1 = swap(own_0, 2), swap(own_1, 2)
    pair_0, pair_1 = swap(own_0, 1), swap(own_1, 1)

    cells = (IMAGE // patch_side[0]) ** 2
    full = group_rows // cells
    order = place ^ jnp.arange(4, dtype=jnp.int32)
    positions = (order[:, None] * rows + jnp.arange(rows, dtype=jnp.int32)).reshape(-1)
    image_id = jnp.minimum(positions // cells, full)
    first_id = jnp.minimum(order * rows // cells, full)
    last_id = jnp.minimum((order * rows + rows - 1) // cells, full)
    first_block = first_id * cells // rows
    stop = jnp.where(last_id == full, group_rows, (last_id + 1) * cells)
    last_block = (stop + rows - 1) // rows
    plan = plan_of(place, order, rows, cells)
    bounds = jnp.concatenate(
        [place[None], jnp.stack([first_block, last_block], axis=1).reshape(-1)]
    )

    turned_qkv = w_qkv.T
    by_head = turned_qkv.reshape(heads, 3, HD, model)
    by_head = by_head * jnp.array([0.125, 1.0, 1.0], jnp.bfloat16)[:, None, None]
    spread = jnp.pad(by_head.transpose(1, 0, 2, 3), ((0, 0), (0, 0), (0, LANES - HD), (0, 0)))
    spread = spread.reshape(3 * heads * LANES, model)
    qkv = project([own_0, own_1, pair_0, pair_1], spread, (0, 1, 2, 3), None)
    across_0, qkv = join(across_0, qkv)
    diagonal_0 = swap(across_0, 1)
    qkv = project([across_0, diagonal_0], spread, (4, 6), qkv)
    across_1, qkv = join(across_1, qkv)
    diagonal_1 = swap(across_1, 1)
    qkv = project([across_1], spread, (5,), qkv)
    diagonal_1, qkv = join(diagonal_1, qkv)
    qkv = project([diagonal_1], spread, (7,), qkv)
    attn_ins = [own_0, own_1, pair_0, pair_1, across_0, across_1, diagonal_0, diagonal_1]

    middle = rows // 2
    w_pair = swap(after(w_out, across_1), 1)
    grads_pair = swap(after(cotangent, across_1), 1)
    mixed_in = jnp.concatenate([cotangent[:middle], w_out], axis=0)
    in_across = swap(after(mixed_in, across_1), 2)
    far = attend(qkv, image_id, plan, heads, 2)
    *far, w_pair, grads_pair = join(*far, w_pair, grads_pair)
    out_2, out_3, logs_far = far
    got_2, got_3 = swap(out_2, 2), swap(out_3, 3)
    grads_1 = swap(after(cotangent[middle:], out_2), 2)
    near = attend(after(qkv, out_2), image_id, plan, heads, 0)
    *near, got_2, got_3, in_across = join(*near, got_2, got_3, in_across)
    in_diagonal = swap(in_across, 1)
    out_0, out_1, logs_near = near
    got_1 = swap(out_1, 1)
    mine = [out_0, got_1, got_2, got_3]
    w_outs = [w_out, w_pair, in_across, in_diagonal]
    resid, *mlp_in = branch(mine, w_outs, tokens, gain_mlp)
    mlp_in[0], grads_1 = join(mlp_in[0], grads_1)
    grads_1_diagonal = swap(grads_1, 1)

    pairs = [swap(m, 1) for m in mlp_in]
    across_0 = swap(mlp_in[0], 2)
    own_0, y_0, pair_0, *near = mlp(
        mlp_in[0], pairs[0], cotangent, grads_pair, 0, 0, w_up, w_down, None, True
    )
    own_1, y_1, pair_1, *near = mlp(
        mlp_in[1], pairs[1], cotangent, grads_pair, 1, 1, w_up, w_down, near, True
    )
    across_0, own_1, pair_0, pair_1, grads_1_diagonal = join(
        across_0, own_1, pair_0, pair_1, grads_1_diagonal
    )
    across_1 = swap(after(mlp_in[1], across_0), 2)
    diagonal_0, pair_0, pair_1 = join(swap(across_0, 1), swap(pair_0, 1), swap(pair_1, 1))
    m_2, y_20, m_3, y_30, *kept = mlp(
        across_0, diagonal_0, in_across, in_diagonal, 0, 0, w_up, w_down, None, False
    )
    across_1, m_2, y_30 = join(across_1, m_2, swap(y_30, 1))
    far_0 = low(add(m_2, swap(m_3, 1)))
    diagonal_1 = swap(across_1, 1)
    m_2, y_21, m_3, y_31, *kept = mlp(
        across_1, diagonal_1, grads_1, grads_1_diagonal, 0, 1, w_up, w_down, kept, False
    )
    sums = mlp_grads(
        after(near[0], m_2),
        near[1],
        (mlp_in[0], pairs[0], mlp_in[1], pairs[1]),
        ((0, cotangent), (0, grads_pair), (1, cotangent), (1, grads_pair)),
        w_up,
        None,
    )
    far_0, m_2, y_31, *sums = join(swap(far_0, 2), m_2, swap(y_31, 1), *sums)
    far_1 = low(add(m_2, swap(m_3, 1)))
    kept_mlp, sent_mlp, gain_mlp_part = mlp_grads(
        after(kept[0], far_1),
        kept[1],
        (across_0, diagonal_0, across_1, diagonal_1),
        ((0, in_across), (0, in_diagonal), (0, grads_1), (0, grads_1_diagonal)),
        w_up,
        sums,
    )
    mixed_far = [low(add(after(y_20, sent_mlp), y_30)), low(add(after(y_21, sent_mlp), y_31))]
    mixed_far, kept_mlp, sent_mlp, far_1 = join(
        jnp.concatenate(mixed_far, axis=0), kept_mlp, sent_mlp, swap(far_1, 2)
    )

    d_resid, d_branch, *d_pieces = branch_back(
        (own_0, own_1), (pair_0, pair_1), (far_0, far_1), cotangent, resid, gain_mlp, w_outs
    )
    d_1, d_2, d_3 = [swap(d_pieces[j], j) for j in range(1, 4)]
    d_outs = out_weight_grads(after(d_branch, d_pieces[0]), mine)
    out_far = low(add(d_outs[2], swap(d_outs[3], 1)))
    back = attend_back(
        after(qkv, out_far),
        (d_pieces[0], d_1),
        (out_0, out_1),
        logs_near,
        image_id,
        bounds,
        heads,
        0,
        (),
    )
    *back, got_mlp, d_2, d_3, out_far = join(
        *back, swap(sent_mlp, 1, "dp"), d_2, d_3, swap(out_far, 2)
    )
    count = lax.axis_size("dp")
    out_pair = swap(after(d_outs[1], back[0]), 1)
    kept_mlp, sent_mlp = halve(kept_mlp, got_mlp, 2)
    d_out = add(d_outs[0], out_pair) + out_far.astype(jnp.float32)
    kept_out, sent_out = parted(d_out.reshape(count, model // count, -1), 1)
    d_qkv = attend_back(
        after(qkv, sent_out, sent_mlp),
        (d_2, d_3),
        (out_2, out_3),
        logs_far,
        image_id,
        bounds,
        heads,
        2,
        back,
    )
    kept_mlp, got_mlp = to_last(kept_mlp, sent_mlp, 2)
    d_qkv, got_out, mixed_far = join(
        d_qkv, swap(sent_out, 1, "dp"), swap(after(mixed_far, sent_out), 2)
    )

    kept, sent, gain_attn_part = qkv_grads(attn_ins, d_qkv, turned_qkv)
    part_2, part_3, kept_mlp, got_mlp = join(
        *unproject(after(d_qkv, sent), turned_qkv, 2), kept_mlp, got_mlp
    )
    grad_mlp = low(add(kept_mlp, got_mlp))
    gains = jnp.concatenate(
        [gain_attn_part / gain_attn[None, :], gain_mlp_part / gain_mlp[None, :]], axis=0
    )
    gains, part_3, part_0, part_1 = join(
        gains + swap(gains, 1),
        swap(part_3, 1),
        *unproject(after(d_qkv, part_2, grad_mlp), turned_qkv, 0),
    )
    d_far = low(add(part_2, part_3))
    pair = swap(part_1, 1)
    kept_out, got_out = to_last(*halve(kept_out, got_out, 2), 2)
    gains = sum_steps(gains, "tp", 2)
    d_far = after(d_far, gains)
    got, gains, kept_out, got_out = join(swap(sent, 1, "dp"), gains, kept_out, got_out)

    kept, sent = halve(kept, got, 2)
    far = swap(d_far, 2)
    gains = sum_steps(gains, "grp")
    kept, got, gains, pair, got_mlp = join(
        *to_last(kept, sent, 2),
        gains + swap(gains, 1, "dp"),
        pair,
        swap(grad_mlp, 1, "grp"),
    )
    grad_rest = jnp.concatenate([low(add(kept, got)), low(add(kept_out, got_out))], axis=1)
    grad_mlp = add(grad_mlp, got_mlp)
    mixed_near = jnp.concatenate(
        [add(y_0, pair_0[middle:]), add(y_1, pair_1[middle:])], axis=0
    )
    mixed_rows = low(resid + (mixed_near + mixed_far.astype(jnp.float32)))
    input_grad = norm_back(tokens, gain_attn, part_0, pair, far, d_resid)
    got, gains, input_grad = join(
        swap(grad_rest, 1, "grp"), sum_steps(gains, "dp", 2), input_grad
    )
    grad_rest = add(grad_rest, got)
    width = w_qkv.shape[1]
    hidden = w_up.shape[1]
    return (
        mixed_rows,
        input_grad,
        gains[0],
        grad_rest[:, :width],
        grad_rest[:, width:].T,
        gains[1],
        grad_mlp[:, :hidden],
        grad_mlp[:, hidden:].T,
    )


def solution(mesh):
    in_specs = (
        P(("grp", "dp", "tp"), None),
        P(("grp", "dp")),
        P(),
        P(None, "tp"),
        P("tp", None),
        P(),
        P(None, "tp"),
        P("tp", None),
        P(("grp", "dp", "tp"), None),
    )
    out_specs = (
        P(("grp", "dp", "tp"), None),
        P(("grp", "dp", "tp"), None),
        P(),
        P("dp", "tp"),
        P("tp", "dp"),
        P(),
        P("dp", "tp"),
        P("tp", "dp"),
    )
    return jax.shard_map(
        on_device, mesh=mesh, in_specs=in_specs, out_specs=out_specs, check_vma=False
    )
```

```python
from functools import partial

import jax
import jax.numpy as jnp
from jax import lax
from jax.experimental import pallas as pl
from jax.experimental.pallas import tpu as pltpu
from jax.sharding import PartitionSpec as P

HD = 64
LANES = 128
IMAGE = 240
EXCLUDED = -1e30
MIB = 1024 * 1024
NT = (((1,), (1,)), ((), ()))
TN = (((0,), (0,)), ((), ()))

epsilon = 1e-06


def normalize(values, scaling):
    centred = values - jnp.mean(values, axis=1, keepdims=True)
    inverse = lax.rsqrt(jnp.mean(centred * centred, axis=1, keepdims=True) + epsilon)
    normed = centred * inverse
    return (normed * scaling, normed, inverse)


def restore(d_normed, normed, inverse, scaling):
    d_scaled = d_normed * scaling
    return inverse * (
        d_scaled
        - jnp.mean(d_scaled, axis=1, keepdims=True)
        - normed * jnp.mean(d_scaled * normed, axis=1, keepdims=True)
    )


def swap(value, distance, axis="tp"):
    size = lax.axis_size(axis)
    return lax.ppermute(value, axis, [(i, i ^ distance) for i in range(size)])


def after(value, *earlier):
    return lax.optimization_barrier((value, *earlier))[0]


def join(*values):
    return lax.optimization_barrier(values)


def add(left, right):
    return left.astype(jnp.float32) + right.astype(jnp.float32)


def product(left, right, dims=(((1,), (0,)), ((), ()))):
    return lax.dot_general(left, right, dims, preferred_element_type=jnp.float32)


def low(value):
    return value.astype(jnp.bfloat16)


def settings(limit, microseconds=0.1):
    return dict(
        compiler_params=pltpu.CompilerParams(vmem_limit_bytes=limit * MIB),
        cost_estimate=pl.CostEstimate(
            flops=int(microseconds * 1.1e9), bytes_accessed=MIB, transcendentals=0
        ),
    )


def whole(array):
    return pl.BlockSpec(array.shape, lambda *_: (0,) * len(array.shape))


def shape(*dims, dtype=jnp.bfloat16):
    return jax.ShapeDtypeStruct(dims, dtype)


def far_shape(*dims, dtype=jnp.bfloat16):
    return pltpu.HBM(dims, dtype)


def left(array):
    return pltpu.with_memory_space_constraint(array, pltpu.HBM)


def chosen(number, refs):
    value = refs[0][...]
    for other in range(1, len(refs)):
        value = jnp.where(number == other, refs[other][...], value)
    return value


def norm_kernel(x_ref, gain_ref, out_ref):
    out_ref[...] = low(normalize(x_ref[...].astype(jnp.float32), gain_ref[...])[0])


def norm(tokens, gain, half):
    rows, model = tokens.shape
    return pl.pallas_call(
        norm_kernel,
        grid=(1,),
        in_specs=[pl.BlockSpec((rows // 2, model), lambda i: (half, 0)), whole(gain)],
        out_specs=pl.BlockSpec((rows // 2, model), lambda i: (0, 0)),
        out_shape=far_shape(rows // 2, model),
        name="norm",
        **settings(8, 2),
    )(left(tokens), left(gain))


def norm_back_kernel(x_ref, gain_ref, own_ref, pair_ref, far_ref, d_ref, out_ref):
    d_normed = add(own_ref[...], pair_ref[...]) + far_ref[...].astype(jnp.float32)
    _, unit, inverse = normalize(x_ref[...].astype(jnp.float32), gain_ref[...])
    out_ref[...] = d_ref[...] + restore(d_normed, unit, inverse, gain_ref[...])


def norm_back(tokens, gain, own, pair, far, d_resid):
    rows, model = tokens.shape
    tile = pl.BlockSpec((rows // 2, model), lambda i: (i, 0))
    return pl.pallas_call(
        norm_back_kernel,
        grid=(2,),
        in_specs=[tile, whole(gain)] + [tile] * 4,
        out_specs=tile,
        out_shape=shape(rows, model, dtype=jnp.float32),
        name="norm_back",
        **settings(16, 2),
    )(tokens, gain, own, pair, far, d_resid)


def project_kernel(count, *refs):
    out_ref = refs[-1]
    out_ref[...] = low(product(chosen(pl.program_id(0), refs[:count]), refs[count][...], NT))


def project(blocks, weights, places, earlier):
    rows = blocks[0].shape[0]
    wide = weights.shape[0]
    count = len(blocks)
    group_rows = rows * 8 if earlier is None else earlier.shape[0]
    extra = [] if earlier is None else [earlier]
    return pl.pallas_call(
        partial(project_kernel, count),
        grid=(count,),
        in_specs=[whole(x) for x in blocks]
        + [whole(weights)]
        + [pl.BlockSpec(memory_space=pl.ANY)] * len(extra),
        out_specs=pl.BlockSpec(
            (rows, wide), lambda i: (places[0] + i * (places[-1] - places[0]) // max(count - 1, 1), 0)
        ),
        out_shape=shape(group_rows, wide),
        input_output_aliases={count + 1: 0} if extra else {},
        name="project",
        **settings(16),
    )(*blocks, weights, *extra)


def tiles_of(bounds_ref, base):
    where = 1 + 2 * base
    first, second = bounds_ref[where], bounds_ref[where + 2]
    count = bounds_ref[where + 1] - first
    total = count + bounds_ref[where + 3] - second

    def tile(number):
        late = (number >= count).astype(jnp.int32)
        key = jnp.where(late == 1, second + number - count, first + number)
        key = jnp.minimum(key, bounds_ref[where + 3] - 1 + (1 - late) * 4)
        return late, key ^ bounds_ref[0], number < total

    return tile, total


def block_at(number, width):
    return pl.ds(pl.multiple_of(number * width, width), width)


def mask_of(ids, id_q_ref, query, key, used, width):
    id_q = id_q_ref[:, block_at(query, width)] + jnp.where(used, 0, 1 << 20)
    return jnp.concatenate([ids[block_at(key, width), :]] * (width // LANES), axis=1) == id_q


TILE = 256
MOST = 40


def plan_of(place, order, rows, cells):
    group_rows = 4 * rows
    per = rows // TILE
    full = group_rows // cells
    inside = jnp.arange(per, dtype=jnp.int32) * TILE
    first = (order[:, None] * rows + inside).reshape(2, 1, 2 * per)
    first_id = jnp.minimum(first // cells, full)
    last_id = jnp.minimum((first + TILE - 1) // cells, full)
    low_key = first_id * cells // TILE
    stop = jnp.where(last_id == full, group_rows, (last_id + 1) * cells)
    turn = jnp.arange(4 * per, dtype=jnp.int32)[None, :, None]
    key = low_key + turn
    used = (key * TILE < stop).reshape(2, -1)
    key = ((key // per) ^ place) * per + key % per
    code = (key + 64 * jnp.arange(2 * per, dtype=jnp.int32)).reshape(2, -1)
    number = jnp.cumsum(used.astype(jnp.int32), axis=1)
    wanted = jnp.arange(1, MOST + 1, dtype=jnp.int32)[None, :, None]
    chosen = used[:, None, :] & (number[:, None, :] == wanted)
    listed = jnp.sum(jnp.where(chosen, code[:, None, :], 0), axis=2)
    return jnp.concatenate([number[:, -1:], listed], axis=1)


def tile_of(plan_ref, base, number):
    code = plan_ref[base // 2, 1 + number]
    return code // 64, code % 64, number < plan_ref[base // 2, 0]


def tile_at(number):
    return pl.ds(pl.multiple_of(number * TILE, TILE), TILE)


def tile_mask(ids, id_q_ref, query, key, used):
    id_q = id_q_ref[:, tile_at(query)] + jnp.where(used, 0, 1 << 20)
    return jnp.concatenate([ids[tile_at(key), :]] * (TILE // LANES), axis=1) == id_q


def in_turn(total, prepare, absorb):
    for number in range(2):
        prepare(number, 0, number)

    def step(number, carry):
        for side in range(2):
            for part in range(2):
                prepare(4 * number + 2 * side + 2 + part, 1 - side, part)
            for part in range(2):
                absorb(4 * number + 2 * side + part, side, part)
        return carry

    lax.fori_loop(0, (total + 3) // 4, step, 0)


def attend_kernel(heads, base, plan_ref, q_ref, k_ref, v_ref, id_q_ref, id_k_ref, *refs):
    out_refs = refs[:2]
    log_ref, turned, ids, scores_a, scores_b, tops, totals = refs[2:]
    scores_refs = (scores_a, scores_b)
    width = q_ref.shape[0] // 2
    for h in range(heads):
        value = v_ref[:, h * LANES : (h + 1) * LANES].astype(jnp.float32).T
        turned[h, :HD] = low(value[:HD])
        turned[h, HD:] = jnp.ones((turned.shape[1] - HD, v_ref.shape[0]), jnp.bfloat16)
    ids[...] = jnp.broadcast_to(id_k_ref[...], ids.shape)
    tops[...] = jnp.full(tops.shape, EXCLUDED, jnp.float32)
    totals[...] = jnp.zeros_like(totals)

    def prepare(number, side, part):
        query, key, _ = tile_of(plan_ref, base, number)
        for h in range(heads):
            columns = slice(h * LANES, (h + 1) * LANES)
            scores_refs[side][part, h] = product(
                k_ref[tile_at(key), columns], q_ref[tile_at(query), columns], NT
            )

    def absorb(number, side, part):
        query, key, used = tile_of(plan_ref, base, number)
        mask = tile_mask(ids, id_q_ref, query, key, used)
        for h in range(heads):
            scores = jnp.where(mask, scores_refs[side][part, h], EXCLUDED)
            largest = tops[query, h]
            top = jnp.maximum(largest, jnp.max(scores, axis=0, keepdims=True))
            exponent = low(jnp.exp(scores - top))
            tops[query, h] = top
            totals[query, h] = totals[query, h] * jnp.exp(largest - top) + product(
                turned[h, :, tile_at(key)], exponent
            )

    in_turn(plan_ref[base // 2, 0], prepare, absorb)
    for query in range(tops.shape[0]):
        block, at = divmod(query * TILE, width)
        for h in range(heads):
            sums = totals[query, h]
            denominator = sums[HD : HD + 1]
            out_refs[block][at : at + TILE, h * HD : (h + 1) * HD] = low(
                (sums[:HD] / denominator).T
            )
            log_ref[h : h + 1, query * TILE : (query + 1) * TILE] = tops[query, h] + jnp.log(
                denominator
            )


def attend(qkv, image_id, plan, heads, base):
    rows = qkv.shape[0]
    wide = heads * LANES
    width = rows // 4
    out = far_shape(width, heads * HD)
    log = far_shape(heads, 2 * width, dtype=jnp.float32)
    return pl.pallas_call(
        partial(attend_kernel, heads, base),
        grid_spec=pltpu.PrefetchScalarGridSpec(
            num_scalar_prefetch=1,
            grid=(1,),
            in_specs=[
                pl.BlockSpec((2 * width, wide), lambda i, _: (base // 2, 0)),
                pl.BlockSpec((rows, wide), lambda i, _: (0, 1)),
                pl.BlockSpec((rows, wide), lambda i, _: (0, 2)),
                pl.BlockSpec((1, 2 * width), lambda i, _: (0, base // 2)),
                pl.BlockSpec((rows, 1), lambda i, _: (0, 0)),
            ],
            out_specs=[whole(out), whole(out), whole(log)],
            scratch_shapes=[
                pltpu.VMEM((heads, HD + 16, rows), jnp.bfloat16),
                pltpu.VMEM((rows, LANES), jnp.int32),
                pltpu.VMEM((2, heads, TILE, TILE), jnp.float32),
                pltpu.VMEM((2, heads, TILE, TILE), jnp.float32),
                pltpu.VMEM((2 * width // TILE, heads, 1, TILE), jnp.float32),
                pltpu.VMEM((2 * width // TILE, heads, HD + 16, TILE), jnp.float32),
            ],
        ),
        out_shape=[out, out, log],
        name="attend",
        **settings(32, 14 if base else 0.1),
    )(plan, *[qkv] * 3, image_id[None, :], image_id[:, None])


def attend_back_kernel(heads, base, bounds_ref, q_ref, k_ref, v_ref, *refs):
    grad_refs = refs[0:2]
    out_refs = refs[2:4]
    log_ref, id_q_ref, id_k_ref = refs[4:7]
    if base == 0:
        d_q_ref, partial_ref = refs[7:9]
    else:
        near_q_ref, near_sums_ref, d_ref = refs[7:10]
    sums = refs[-1]
    first = 9 if base == 0 else 10
    turned, ids, grads, placed, inner, d_q = refs[first : first + 6]
    width = q_ref.shape[0] // 2
    tile, total = tiles_of(bounds_ref, base)
    for h in range(heads):
        key = k_ref[:, h * LANES : (h + 1) * LANES].astype(jnp.float32).T
        turned[h] = low(key[:HD])
    ids[...] = jnp.broadcast_to(id_k_ref[...], ids.shape)
    d_q[...] = jnp.zeros_like(d_q)
    if base == 0:
        sums[...] = jnp.zeros_like(sums)
    else:
        sums[...] = near_sums_ref[...].astype(jnp.float32)
    ones = jnp.ones((8, HD), jnp.float32)
    none = jnp.zeros((width, HD), jnp.bfloat16)
    for query in range(2):
        for h in range(heads):
            grad = grad_refs[query][:, h * HD : (h + 1) * HD]
            grads[query, h] = jnp.concatenate([grad, none], axis=1)
            placed[query, h] = jnp.concatenate([none, grad], axis=1)
            terms = grad.astype(jnp.float32) * out_refs[query][
                :, h * HD : (h + 1) * HD
            ].astype(jnp.float32)
            inner[query, h] = lax.dot_general(
                ones,
                terms,
                NT,
                precision=lax.Precision.HIGHEST,
                preferred_element_type=jnp.float32,
            )[:1]

    def absorb(number):
        query, key, used = tile(number)
        at = block_at(key, width)
        mask = mask_of(ids, id_q_ref, query, key, used, width)
        for h in range(heads):
            columns = slice(h * LANES, (h + 1) * LANES)
            logs = log_ref[h : h + 1, block_at(query, width)]
            queries = q_ref[block_at(query, width), columns]
            scores = product(k_ref[at, columns], queries, NT)
            d_probs = product(v_ref[at, columns], grads[query, h], NT)
            probs = jnp.where(mask, jnp.exp(scores - logs), 0.0)
            d_scores = low(probs * (d_probs - inner[query, h]))
            sums[at, columns] += product(low(probs), placed[query, h]) + product(d_scores, queries)
            d_q[query, h] += product(turned[h, :, at], d_scores)

    def step(number, carry):
        absorb(number)
        return carry

    lax.fori_loop(0, total, step, 0)
    for query in range(2):
        for h in range(heads):
            part = low((d_q[query, h] * 0.125).T)
            if base == 0:
                d_q_ref[query * width : (query + 1) * width, h * HD : (h + 1) * HD] = part
            else:
                here = slice((base + query) * width, (base + query + 1) * width)
                d_ref[here, 3 * h * HD : (3 * h + 1) * HD] = part
    if base == 0:
        partial_ref[...] = low(sums[...])
    else:
        for h in range(heads):
            d_ref[: 2 * width, 3 * h * HD : (3 * h + 1) * HD] = near_q_ref[
                :, h * HD : (h + 1) * HD
            ]
            d_ref[:, (3 * h + 1) * HD : (3 * h + 3) * HD] = low(
                sums[:, h * LANES : (h + 1) * LANES]
            )


def attend_back(qkv, d_heads, heads_out, log_total, image_id, bounds, heads, base, near):
    rows = qkv.shape[0]
    wide = heads * LANES
    width = rows // 4
    sums = far_shape(rows, wide)
    near = list(near)
    if base == 0:
        outs = [far_shape(2 * width, heads * HD), sums]
    else:
        outs = [shape(rows, 3 * heads * HD)]
    padded = pltpu.VMEM((2, heads, width, LANES), jnp.bfloat16)
    result = pl.pallas_call(
        partial(attend_back_kernel, heads, base),
        grid_spec=pltpu.PrefetchScalarGridSpec(
            num_scalar_prefetch=1,
            grid=(1,),
            in_specs=[
                pl.BlockSpec((2 * width, wide), lambda i, _: (base // 2, 0)),
                pl.BlockSpec((rows, wide), lambda i, _: (0, 1)),
                pl.BlockSpec((rows, wide), lambda i, _: (0, 2)),
            ]
            + [whole(a) for a in (*d_heads, *heads_out, log_total)]
            + [
                pl.BlockSpec((1, 2 * width), lambda i, _: (0, base // 2)),
                pl.BlockSpec((rows, 1), lambda i, _: (0, 0)),
            ]
            + [whole(a) for a in near],
            out_specs=[whole(a) for a in outs],
            scratch_shapes=[
                pltpu.VMEM((heads, HD, rows), jnp.bfloat16),
                pltpu.VMEM((rows, LANES), jnp.int32),
                padded,
                padded,
                pltpu.VMEM((2, heads, 1, width), jnp.float32),
                pltpu.VMEM((2, heads, HD, width), jnp.float32),
            ]
            + [pltpu.VMEM((rows, wide), jnp.float32)],
        ),
        out_shape=outs,
        name="attend_back",
        **settings(36, 20 if base else 3),
    )(
        bounds,
        *[left(qkv)] * 3,
        *d_heads,
        *heads_out,
        log_total,
        image_id[None, :],
        image_id[:, None],
        *(left(a) for a in near),
    )
    return result[0] if near else result


def last_rows(refs, number):
    size = refs[number].shape[0]
    return refs[number][size - refs[0].shape[0] :, :]


def branch_kernel(*refs):
    parts = refs[0:4]
    weights = refs[4:8]
    tokens_ref, gain_ref, resid_ref, in_0_ref, in_1_ref = refs[8:]
    resid = tokens_ref[...].astype(jnp.float32)
    branch = product(parts[0][...], last_rows(weights, 0))
    for j in range(1, 4):
        branch = branch + product(parts[j][...], last_rows(weights, j))
    resid = resid + branch
    resid_ref[...] = resid
    normed = low(normalize(resid, gain_ref[...])[0])
    for half, in_ref in enumerate((in_0_ref, in_1_ref)):

        @pl.when(pl.program_id(0) == half)
        def _():
            in_ref[...] = normed


def branch(parts, weights, tokens, gain):
    rows, model = tokens.shape
    operands = (*parts, *weights, tokens, gain)
    half = far_shape(rows // 2, model)
    resid = far_shape(rows, model, dtype=jnp.float32)

    def halves(array):
        return pl.BlockSpec((rows // 2, array.shape[1]), lambda i: (i, 0))

    specs = [whole(a) for a in operands]
    specs[:4] = [halves(p) for p in parts]
    specs[8] = halves(tokens)
    return pl.pallas_call(
        branch_kernel,
        grid=(2,),
        in_specs=specs,
        out_specs=[halves(resid), whole(half), whole(half)],
        out_shape=[resid, half, half],
        name="branch",
        **settings(16),
    )(*operands)


def mlp_kernel(together, x_a_ref, x_b_ref, g_a_ref, g_b_ref, up_ref, down_ref, *refs):
    act_ref, d_pre_ref = refs[-2:]
    length = x_a_ref.shape[0]
    if together:
        m_a_ref, y_a_ref, both_ref = refs[-5:-2]
        m_b_ref, y_b_ref = both_ref.at[:length], both_ref.at[length:]
    else:
        m_a_ref, y_a_ref, m_b_ref, y_b_ref = refs[-6:-2]

    number = pl.program_id(0)
    mlp_in = chosen(number, (x_b_ref, x_a_ref))
    out_grads = chosen(number, (g_b_ref, g_a_ref))
    pre_act = product(mlp_in, up_ref[...])
    d_act = product(out_grads, down_ref[...], NT)
    below = 0.5 + 0.5 * lax.erf(pre_act * 0.7071067811865476)
    density = 0.3989422804014327 * jnp.exp(-0.5 * pre_act * pre_act)
    d_pre = low(d_act * (below + pre_act * density))
    act = low(pre_act * below)
    m = low(product(d_pre, up_ref[...], NT))
    y = low(product(act, down_ref[...]))
    act_ref[...] = act
    d_pre_ref[...] = d_pre
    for block, (m_ref, y_ref) in enumerate(((m_b_ref, y_b_ref), (m_a_ref, y_a_ref))):

        @pl.when(number == block)
        def _():
            m_ref[...] = m
            y_ref[...] = y


def mlp(x_a, x_b, g_a, g_b, half, place, w_up, w_down, earlier, near):
    length, model = x_a.shape
    hidden = w_up.shape[1]
    extra = [] if earlier is None else list(earlier)

    def grads():
        return pl.BlockSpec((length, model), lambda i: (half, 0))

    def kept(width):
        return pl.BlockSpec((length, width), lambda i: (2 * place + 1 - i, 0))

    one = far_shape(length, model)
    outs = [one, one, far_shape(2 * length, model)] if near else [one] * 4
    return pl.pallas_call(
        partial(mlp_kernel, near),
        grid=(2,),
        in_specs=[whole(x_a), whole(x_b), grads(), grads(), whole(w_up), whole(w_down)]
        + [pl.BlockSpec(memory_space=pl.ANY)] * len(extra),
        out_specs=[whole(a) for a in outs] + [kept(hidden)] * 2,
        out_shape=outs
        + [far_shape(4 * length, hidden)] * 2,
        input_output_aliases={6 + i: len(outs) + i for i in range(len(extra))},
        name="mlp",
        **settings(20),
    )(x_a, x_b, g_a, g_b, w_up, w_down, *extra)


def part_rows(count, bit, totals, kept_ref, sent_ref):
    share = totals[0].shape[0] // count
    for pair in range(count // 2):
        for side, ref in ((bit, kept_ref), (1 - bit, sent_ref)):
            at = pl.ds(pl.multiple_of((2 * pair + side) * share, 8), share)
            first = 0
            for total in totals:
                width = min(total.shape[1], ref.shape[2] - first)
                ref[pair, :, first : first + width] = total[at, :width].astype(ref.dtype)
                first += width


def row_sums(values):
    sums = jnp.sum(values, axis=1, keepdims=True)
    return jnp.broadcast_to(sums, (values.shape[0], LANES)).T[:1]


def mlp_grads_kernel(count, bit_ref, act_ref, d_pre_ref, *refs):
    number = pl.program_id(0)
    x_refs, g_refs = refs[0:4], refs[4:8]
    if count:
        up_ref, old_up_ref, old_down_ref, kept_ref, sent_ref, gain_ref, d_up, d_down = refs[8:]
    else:
        d_up, d_down = refs[8:]

    @pl.when(number == 0)
    def _():
        if count:
            d_up[...] = old_up_ref[...]
            d_down[...] = old_down_ref[...]
        else:
            d_up[...] = jnp.zeros_like(d_up)
            d_down[...] = jnp.zeros_like(d_down)

    x = jnp.concatenate([chosen(number, x_refs[j::2]) for j in range(2)], axis=0)
    d_up[...] += product(x, d_pre_ref[...], TN)
    grads = jnp.concatenate([chosen(number, g_refs[j::2]) for j in range(2)], axis=0)
    d_down[...] += product(grads, act_ref[...], TN)

    @pl.when(number == 1)
    def _():
        if count:
            part_rows(count, bit_ref[0], (d_up, d_down), kept_ref, sent_ref)
            gain_ref[...] = row_sums(d_up[...] * up_ref[...].astype(jnp.float32))


def mlp_grads(act, d_pre, blocks, grads, w_up, earlier):
    rows, hidden = act.shape
    model = blocks[0].shape[1]
    tile = rows // 4
    count = lax.axis_size("dp")
    bit = lax.axis_index("dp") % 2
    total = shape(model, hidden, dtype=jnp.float32)
    kept = far_shape(count // 2, model // count, 2 * hidden, dtype=jnp.float32)
    sent = far_shape(*kept.shape)
    gain = shape(1, model, dtype=jnp.float32)
    extra = [] if earlier is None else [w_up, *earlier]
    outs = [kept, sent, gain] if extra else [total, total]

    def half(rows, columns):
        return pl.BlockSpec((rows, columns), lambda i, _: (i, 0))

    return pl.pallas_call(
        partial(mlp_grads_kernel, count if extra else 0),
        grid_spec=pltpu.PrefetchScalarGridSpec(
            num_scalar_prefetch=1,
            grid=(2,),
            in_specs=[half(2 * tile, hidden)] * 2
            + [whole(a) for a in blocks]
            + [
                pl.BlockSpec((tile, model), lambda i, _, at=at: (at, 0)) for at, _ in grads
            ]
            + [whole(a) for a in extra],
            out_specs=[whole(a) for a in outs],
            scratch_shapes=[pltpu.VMEM((model, hidden), jnp.float32)] * 2 if extra else [],
        ),
        out_shape=outs,
        name="mlp_grads",
        **settings(40),
    )(bit[None], *(left(a) for a in (act, d_pre, *blocks, *(g for _, g in grads))), *extra)


def branch_back_kernel(*refs):
    cotangent_ref, resid_ref, gain_ref = refs[6:9]
    weights = refs[9:13]
    d_resid_ref, d_branch_ref = refs[13:15]
    out_refs = refs[15:19]
    own, pair, far = (chosen(pl.program_id(0), refs[j : j + 2]) for j in (0, 2, 4))
    d_mlp_in = add(own, pair) + far.astype(jnp.float32)
    _, unit, inverse = normalize(resid_ref[...], gain_ref[...])
    d_resid = cotangent_ref[...].astype(jnp.float32) + restore(
        d_mlp_in, unit, inverse, gain_ref[...]
    )
    d_resid_ref[...] = d_resid
    d_branch = low(d_resid)
    d_branch_ref[...] = d_branch
    for j in range(4):
        out_refs[j][...] = low(product(d_branch, last_rows(weights, j), NT))


def branch_back(own, pair, far, cotangent, resid, gain, weights):
    rows, model = resid.shape
    width = weights[0].shape[0]

    def at(columns):
        return pl.BlockSpec((rows // 2, columns), lambda i: (i, 0))

    operands = (*own, *pair, *far, cotangent, resid, gain, *weights)
    specs = [whole(a) for a in operands]
    specs[2] = specs[3] = pl.BlockSpec((rows // 2, model), lambda i: (0, 0))
    specs[6] = specs[7] = at(model)
    return pl.pallas_call(
        branch_back_kernel,
        grid=(2,),
        in_specs=specs,
        out_specs=[at(model), at(model)] + [at(width)] * 4,
        out_shape=[far_shape(rows, model, dtype=jnp.float32), shape(rows, model)]
        + [far_shape(rows, width)] * 4,
        name="branch_back",
        **settings(16),
    )(*(left(a) for a in operands))


def out_grads_kernel(d_ref, *refs):
    for j in range(4):
        refs[4 + j][...] = low(product(d_ref[...], refs[j][...], TN))


def out_weight_grads(d_branch, parts):
    model = d_branch.shape[1]
    out = far_shape(model, parts[0].shape[1])
    return pl.pallas_call(
        out_grads_kernel,
        in_specs=[whole(a) for a in (d_branch, *parts)],
        out_specs=[whole(out)] * 4,
        out_shape=[out] * 4,
        name="out_weight_grads",
        **settings(16),
    )(d_branch, *parts)


def qkv_grads_kernel(count, bit_ref, *refs):
    x_refs = refs[0:8]
    d_ref, w_ref, kept_ref, sent_ref, gain_ref, total = refs[8:]
    number = pl.program_id(0)
    block = jnp.concatenate([chosen(number, x_refs[j::4]) for j in range(4)], axis=0)
    part = product(block, d_ref[...], TN)

    @pl.when(number == 0)
    def _():
        total[...] = part

    @pl.when(number > 0)
    def _():
        total[...] += part

    @pl.when(number == 1)
    def _():
        part_rows(count, bit_ref[0], (total,), kept_ref, sent_ref)
        gain_ref[...] = row_sums(total[...] * w_ref[...].astype(jnp.float32).T)


def qkv_grads(attn_ins, d_qkv, w_qkv):
    rows, model = attn_ins[0].shape
    width = d_qkv.shape[1]
    count = lax.axis_size("dp")
    bit = lax.axis_index("dp") % 2
    kept = far_shape(count // 2, model // count, width, dtype=jnp.float32)
    sent = far_shape(*kept.shape)
    gain = shape(1, model, dtype=jnp.float32)
    return pl.pallas_call(
        partial(qkv_grads_kernel, count),
        grid_spec=pltpu.PrefetchScalarGridSpec(
            num_scalar_prefetch=1,
            grid=(2,),
            in_specs=[whole(x) for x in attn_ins]
            + [pl.BlockSpec((4 * rows, width), lambda i, _: (i, 0)), whole(w_qkv)],
            out_specs=[whole(kept), whole(sent), whole(gain)],
            scratch_shapes=[pltpu.VMEM((model, width), jnp.float32)],
        ),
        out_shape=[kept, sent, gain],
        name="qkv_grads",
        **settings(24),
    )(bit[None], *attn_ins, d_qkv, w_qkv)


def unproject_kernel(d_ref, w_ref, *out_refs):
    part = low(product(d_ref[...], w_ref[...]))
    for number in range(2):

        @pl.when(pl.program_id(0) == number)
        def _():
            out_refs[number][...] = part


def unproject(d_qkv, w_qkv, base):
    rows = d_qkv.shape[0] // 4
    out = far_shape(rows, w_qkv.shape[1])
    return pl.pallas_call(
        unproject_kernel,
        grid=(2,),
        in_specs=[
            pl.BlockSpec((rows, d_qkv.shape[1]), lambda i: (base + i, 0)),
            whole(w_qkv),
        ],
        out_specs=[whole(out), whole(out)],
        out_shape=[out, out],
        name="unproject",
        **settings(16),
    )(d_qkv, w_qkv)


def parted(total, distance):
    bit = (lax.axis_index("dp") // distance) % 2
    total = total.reshape(-1, 2, *total.shape[1:])
    return (
        lax.dynamic_index_in_dim(total, bit, 1, keepdims=False),
        low(lax.dynamic_index_in_dim(total, 1 - bit, 1, keepdims=False)),
    )


def halve(kept, got, distance):
    bit = (lax.axis_index("dp") // distance) % 2
    kept = kept.reshape(-1, 2, *kept.shape[1:])
    got = got.reshape(kept.shape)

    def side(number):
        return add(
            lax.dynamic_index_in_dim(kept, number, 1, keepdims=False),
            lax.dynamic_index_in_dim(got, number, 1, keepdims=False),
        )

    return side(bit), low(side(1 - bit))


def to_last(kept, sent, distance):
    while True:
        got = swap(sent, distance, "dp")
        distance *= 2
        if distance >= lax.axis_size("dp"):
            return kept[0], got[0]
        kept, sent = halve(kept, got, distance)


def sum_steps(value, axis, first=1):
    distance = first
    while distance < lax.axis_size(axis):
        value = value + swap(value, distance, axis)
        distance *= 2
    return value


def on_device(tokens, patch_side, gain_attn, w_qkv, w_out, gain_mlp, w_up, w_down, cotangent):
    rows, model = tokens.shape
    place = lax.axis_index("tp")
    group_rows = 4 * rows
    heads = w_out.shape[0] // HD

    own_0 = norm(tokens, gain_attn, 0)
    own_1 = norm(after(tokens, own_0), gain_attn, 1)
    across_0, across_1 = swap(own_0, 2), swap(own_1, 2)
    pair_0, pair_1 = swap(own_0, 1), swap(own_1, 1)

    cells = (IMAGE // patch_side[0]) ** 2
    full = group_rows // cells
    order = place ^ jnp.arange(4, dtype=jnp.int32)
    positions = (order[:, None] * rows + jnp.arange(rows, dtype=jnp.int32)).reshape(-1)
    image_id = jnp.minimum(positions // cells, full)
    first_id = jnp.minimum(order * rows // cells, full)
    last_id = jnp.minimum((order * rows + rows - 1) // cells, full)
    first_block = first_id * cells // rows
    stop = jnp.where(last_id == full, group_rows, (last_id + 1) * cells)
    last_block = (stop + rows - 1) // rows
    plan = plan_of(place, order, rows, cells)
    bounds = jnp.concatenate(
        [place[None], jnp.stack([first_block, last_block], axis=1).reshape(-1)]
    )

    turned_qkv = w_qkv.T
    by_head = turned_qkv.reshape(heads, 3, HD, model)
    by_head = by_head * jnp.array([0.125, 1.0, 1.0], jnp.bfloat16)[:, None, None]
    spread = jnp.pad(by_head.transpose(1, 0, 2, 3), ((0, 0), (0, 0), (0, LANES - HD), (0, 0)))
    spread = spread.reshape(3 * heads * LANES, model)
    qkv = project([own_0, own_1, pair_0, pair_1], spread, (0, 1, 2, 3), None)
    across_0, qkv = join(across_0, qkv)
    diagonal_0 = swap(across_0, 1)
    qkv = project([across_0, diagonal_0], spread, (4, 6), qkv)
    across_1, qkv = join(across_1, qkv)
    diagonal_1 = swap(across_1, 1)
    qkv = project([across_1], spread, (5,), qkv)
    diagonal_1, qkv = join(diagonal_1, qkv)
    qkv = project([diagonal_1], spread, (7,), qkv)
    attn_ins = [own_0, own_1, pair_0, pair_1, across_0, across_1, diagonal_0, diagonal_1]

    middle = rows // 2
    w_pair = swap(after(w_out, across_1), 1)
    grads_pair = swap(after(cotangent, across_1), 1)
    mixed_in = jnp.concatenate([cotangent[:middle], w_out], axis=0)
    in_across = swap(after(mixed_in, across_1), 2)
    far = attend(qkv, image_id, plan, heads, 2)
    *far, w_pair, grads_pair = join(*far, w_pair, grads_pair)
    out_2, out_3, logs_far = far
    got_2, got_3 = swap(out_2, 2), swap(out_3, 3)
    grads_1 = swap(after(cotangent[middle:], out_2), 2)
    near = attend(after(qkv, out_2), image_id, plan, heads, 0)
    *near, got_2, got_3, in_across = join(*near, got_2, got_3, in_across)
    in_diagonal = swap(in_across, 1)
    out_0, out_1, logs_near = near
    got_1 = swap(out_1, 1)
    mine = [out_0, got_1, got_2, got_3]
    w_outs = [w_out, w_pair, in_across, in_diagonal]
    resid, *mlp_in = branch(mine, w_outs, tokens, gain_mlp)

    pairs = [swap(m, 1) for m in mlp_in]
    pairs[0], grads_1 = join(pairs[0], grads_1)
    grads_1_diagonal = swap(grads_1, 1)
    across_0 = swap(mlp_in[0], 2)
    own_0, y_0, pair_0, *near = mlp(
        mlp_in[0], pairs[0], cotangent, grads_pair, 0, 0, w_up, w_down, None, True
    )
    own_1, y_1, pair_1, *near = mlp(
        mlp_in[1], pairs[1], cotangent, grads_pair, 1, 1, w_up, w_down, near, True
    )
    across_0, own_1, pair_0, pair_1, grads_1_diagonal = join(
        across_0, own_1, pair_0, pair_1, grads_1_diagonal
    )
    across_1 = swap(after(mlp_in[1], across_0), 2)
    diagonal_0, pair_0, pair_1 = join(swap(across_0, 1), swap(pair_0, 1), swap(pair_1, 1))
    m_2, y_20, m_3, y_30, *kept = mlp(
        across_0, diagonal_0, in_across, in_diagonal, 0, 0, w_up, w_down, None, False
    )
    across_1, m_2, y_30 = join(across_1, m_2, swap(y_30, 1))
    far_0 = low(add(m_2, swap(m_3, 1)))
    diagonal_1 = swap(across_1, 1)
    m_2, y_21, m_3, y_31, *kept = mlp(
        across_1, diagonal_1, grads_1, grads_1_diagonal, 0, 1, w_up, w_down, kept, False
    )
    sums = mlp_grads(
        after(near[0], m_2),
        near[1],
        (mlp_in[0], pairs[0], mlp_in[1], pairs[1]),
        ((0, cotangent), (0, grads_pair), (1, cotangent), (1, grads_pair)),
        w_up,
        None,
    )
    far_0, m_2, y_31, *sums = join(swap(far_0, 2), m_2, swap(y_31, 1), *sums)
    far_1 = low(add(m_2, swap(m_3, 1)))
    kept_mlp, sent_mlp, gain_mlp_part = mlp_grads(
        after(kept[0], far_1),
        kept[1],
        (across_0, diagonal_0, across_1, diagonal_1),
        ((0, in_across), (0, in_diagonal), (0, grads_1), (0, grads_1_diagonal)),
        w_up,
        sums,
    )
    mixed_far = [low(add(after(y_20, sent_mlp), y_30)), low(add(after(y_21, sent_mlp), y_31))]
    mixed_far, kept_mlp, sent_mlp, far_1 = join(
        jnp.concatenate(mixed_far, axis=0), kept_mlp, sent_mlp, swap(far_1, 2)
    )

    d_resid, d_branch, *d_pieces = branch_back(
        (own_0, own_1), (pair_0, pair_1), (far_0, far_1), cotangent, resid, gain_mlp, w_outs
    )
    d_1, d_2, d_3 = [swap(d_pieces[j], j) for j in range(1, 4)]
    d_outs = out_weight_grads(after(d_branch, d_pieces[0]), mine)
    out_far = low(add(d_outs[2], swap(d_outs[3], 1)))
    back = attend_back(
        after(qkv, out_far),
        (d_pieces[0], d_1),
        (out_0, out_1),
        logs_near,
        image_id,
        bounds,
        heads,
        0,
        (),
    )
    *back, got_mlp, d_2, d_3, out_far = join(
        *back, swap(sent_mlp, 1, "dp"), d_2, d_3, swap(out_far, 2)
    )
    count = lax.axis_size("dp")
    out_pair = swap(after(d_outs[1], back[0]), 1)
    kept_mlp, sent_mlp = halve(kept_mlp, got_mlp, 2)
    d_out = add(d_outs[0], out_pair) + out_far.astype(jnp.float32)
    kept_out, sent_out = parted(d_out.reshape(count, model // count, -1), 1)
    d_qkv = attend_back(
        after(qkv, sent_out, sent_mlp),
        (d_2, d_3),
        (out_2, out_3),
        logs_far,
        image_id,
        bounds,
        heads,
        2,
        back,
    )
    kept_mlp, got_mlp = to_last(kept_mlp, sent_mlp, 2)
    d_qkv, got_out, mixed_far = join(
        d_qkv, swap(sent_out, 1, "dp"), swap(after(mixed_far, sent_out), 2)
    )

    kept, sent, gain_attn_part = qkv_grads(attn_ins, d_qkv, turned_qkv)
    part_2, part_3, kept_mlp, got_mlp = join(
        *unproject(after(d_qkv, sent), turned_qkv, 2), kept_mlp, got_mlp
    )
    grad_mlp = low(add(kept_mlp, got_mlp))
    gains = jnp.concatenate(
        [gain_attn_part / gain_attn[None, :], gain_mlp_part / gain_mlp[None, :]], axis=0
    )
    gains, part_3, part_0, part_1 = join(
        gains + swap(gains, 1),
        swap(part_3, 1),
        *unproject(after(d_qkv, part_2, grad_mlp), turned_qkv, 0),
    )
    d_far = low(add(part_2, part_3))
    pair = swap(part_1, 1)
    kept_out, got_out = to_last(*halve(kept_out, got_out, 2), 2)
    gains = sum_steps(gains, "tp", 2)
    d_far = after(d_far, gains)
    got, gains, kept_out, got_out = join(swap(sent, 1, "dp"), gains, kept_out, got_out)

    kept, sent = halve(kept, got, 2)
    far = swap(d_far, 2)
    gains = sum_steps(gains, "grp")
    kept, got, gains, pair, got_mlp = join(
        *to_last(kept, sent, 2),
        gains + swap(gains, 1, "dp"),
        pair,
        swap(grad_mlp, 1, "grp"),
    )
    grad_rest = jnp.concatenate([low(add(kept, got)), low(add(kept_out, got_out))], axis=1)
    grad_mlp = add(grad_mlp, got_mlp)
    mixed_near = jnp.concatenate(
        [add(y_0, pair_0[middle:]), add(y_1, pair_1[middle:])], axis=0
    )
    mixed_rows = low(resid + (mixed_near + mixed_far.astype(jnp.float32)))
    input_grad = norm_back(tokens, gain_attn, part_0, pair, far, d_resid)
    got, gains, input_grad = join(
        swap(grad_rest, 1, "grp"), sum_steps(gains, "dp", 2), input_grad
    )
    grad_rest = add(grad_rest, got)
    width = w_qkv.shape[1]
    hidden = w_up.shape[1]
    return (
        mixed_rows,
        input_grad,
        gains[0],
        grad_rest[:, :width],
        grad_rest[:, width:].T,
        gains[1],
        grad_mlp[:, :hidden],
        grad_mlp[:, hidden:].T,
    )


def solution(mesh):
    in_specs = (
        P(("grp", "dp", "tp"), None),
        P(("grp", "dp")),
        P(),
        P(None, "tp"),
        P("tp", None),
        P(),
        P(None, "tp"),
        P("tp", None),
        P(("grp", "dp", "tp"), None),
    )
    out_specs = (
        P(("grp", "dp", "tp"), None),
        P(("grp", "dp", "tp"), None),
        P(),
        P("dp", "tp"),
        P("tp", "dp"),
        P(),
        P("dp", "tp"),
        P("tp", "dp"),
    )
    return jax.shard_map(
        on_device, mesh=mesh, in_specs=in_specs, out_specs=out_specs, check_vma=False
    )
```
